32 devices in a mesh: section: 4 (over x, core), dp: 8 (over z, y).
Axes of the slice: x: 2, y: 2, z: 4, core: 2. Of those that a mesh axis runs over, the one named last changes fastest.
Arguments:
- block_input: bfloat16 [2, 8, 1024, 768], P(None, 'dp'), may hold values from -6 to 6
- carried_state: float32 [4, 3, 2, 8, 768], P('section', None, None, 'dp'), may hold values from -21 to 21, as said below
- output_cotangent: bfloat16 [2, 8, 1024, 768], P(None, 'dp'), may hold values from -6 to 6
- in_weight: bfloat16 [4, 768, 3072], P('section'), may hold values from -0.21875 to 0.21875
- out_weight: bfloat16 [4, 3840, 768], P('section'), may hold values from -0.109375 to 0.109375
- norm_gain: float32 [4, 768], P('section'), may hold values from 0.5 to 1.5
- norm_bias: float32 [4, 768], P('section'), may hold values from -1.5 to 1.5
- mix_rates: float32 [4, 3, 768], P('section'), may hold values from 0.05 to 0.95
- wkv_params: float32 [4, 2, 768], P('section'), may hold values from -6 to 1, as said below
Outputs:
- section_outputs: bfloat16 [4, 2, 8, 1024, 768], P('section', None, 'dp')
- final_state: float32 [4, 2, 2, 8, 768], P('section', None, None, 'dp')
- last_normed: float32 [4, 2, 8, 768], P('section', None, 'dp')
- section_grads: bfloat16 [4, 2, 8, 1024, 768], P('section', None, 'dp')
- in_weight_grad: float32 [4, 768, 3072], P('section')
- out_weight_grad: float32 [4, 3840, 768], P('section')
- norm_gain_grad: float32 [4, 768], P('section')
- norm_bias_grad: float32 [4, 768], P('section')
- mix_rates_grad: float32 [4, 3, 768], P('section')
- wkv_params_grad: float32 [4, 2, 768], P('section')
The draws below stay inside these ranges and needn't reach their ends.
Inputs may be any that keep to these rules, and one draw needn't show every extreme that they name: `carried_state`: row 2 (the denominator) is positive and row 1 is at most row 2 in magnitude. `wkv_params`: row 0 holds log decay rates, between -6 and -2.3; row 1 holds bonuses, between -1 and 1.
All inputs are finite; a program needn't handle non-finite values.
Results may differ from the reference program's by a relative error of at most 0.014.
Values may be sent and summed in bfloat16 or wider, within the bound.
A program may use at most 256 MiB of HBM per device.

```python
import jax
import jax.numpy as jnp
from jax import lax

D = 768
FF = 3072
LENGTH = 1024
MICRO = 2
BATCH = 8
N_SECTION = 4


def draw_carried_state(key, part):
    key = jax.random.fold_in(key, 11)
    first_key, second_key, third_key = jax.random.split(key, 3)
    array_dimensions = (N_SECTION, 1, MICRO, BATCH, D)
    previous = jnp.clip(jax.random.normal(first_key, array_dimensions, jnp.float32), -4.0, 4.0)
    accruing_normalizer = jnp.exp(jax.random.uniform(second_key, array_dimensions, jnp.float32, 0.0, 3.0))
    accruing_upper_sum = accruing_normalizer * jax.random.uniform(third_key, array_dimensions, jnp.float32, -1.0, 1.0)
    return jnp.concatenate([previous, accruing_upper_sum, accruing_normalizer], axis=1)


def draw_wkv_params(key, part):
    key = jax.random.fold_in(key, 23)
    fading_sampler_seed, reward_added_to_address = jax.random.split(key, 2)
    array_dimensions = (N_SECTION, 1, D)
    logged_fading = jax.random.uniform(fading_sampler_seed, array_dimensions, jnp.float32, -6.0, -2.3)
    opening_item_reward = jax.random.uniform(reward_added_to_address, array_dimensions, jnp.float32, -1.0, 1.0)
    return jnp.concatenate([logged_fading, opening_item_reward], axis=1)


def shard_levels(rng, extent, shards, least, largest):
    factor_of, own = 1.0, jax.random.fold_in(rng, 6)
    for axis_at, parts in shards:
        heights = jnp.exp(jax.random.uniform(jax.random.fold_in(own, axis_at), (parts,), jnp.float32, least / len(shards), largest / len(shards)))
        factor_of = factor_of * jnp.repeat(heights, extent[axis_at] // parts).reshape([-1 if axis == axis_at else 1 for axis in range(len(extent))])
    return factor_of


def gaussian(rng, shape, deviation, most, cuts=(), dtype=jnp.bfloat16):
    level = shard_levels(rng, shape, cuts, -0.22, 0.18) if cuts else 1.0
    drawn = jax.random.normal(rng, shape, jnp.float32) * deviation * level
    return jnp.minimum(jnp.maximum(drawn, -most), most).astype(dtype)


def setup_inputs(seed: int = 0) -> dict:
    key_of = jax.random.split(jax.random.key(seed), 10)
    block_input = gaussian(key_of[0], (MICRO, BATCH, LENGTH, D), 1.0, 6.0, ((1, 8),))
    carried_state = draw_carried_state(jax.random.fold_in(key_of[9], 71), 0)
    output_cotangent = gaussian(key_of[2], (MICRO, BATCH, LENGTH, D), 1.0, 6.0, ((1, 8),))
    in_weight = gaussian(key_of[3], (N_SECTION, D, FF), D ** -0.5, 0.21875, ((0, 4),))
    out_weight = gaussian(key_of[4], (N_SECTION, FF + D, D), FF ** -0.5, 0.109375, ((0, 4),))
    norm_gain = jnp.clip(1.0 + 0.1 * jax.random.normal(key_of[5], (N_SECTION, D), jnp.float32), 0.5, 1.5)
    norm_bias = gaussian(key_of[6], (N_SECTION, D), 0.3, 1.5, ((0, 4),), jnp.float32)
    mix_rates = jnp.clip(0.05 + 0.9 * jax.random.uniform(key_of[7], (N_SECTION, 3, D), jnp.float32) ** shard_levels(key_of[7], (N_SECTION, 3, D), ((0, 4),), -0.2, 0.2), 0.05, 0.95)
    wkv_params = draw_wkv_params(jax.random.fold_in(key_of[9], 71), 0)
    return {"block_input": block_input, "carried_state": carried_state, "output_cotangent": output_cotangent, "in_weight": in_weight, "out_weight": out_weight, "norm_gain": norm_gain, "norm_bias": norm_bias, "mix_rates": mix_rates, "wkv_params": wkv_params}


precise = lax.Precision.HIGHEST

@jax.custom_vjp
def low(v):
    return lax.optimization_barrier(v.astype(jnp.bfloat16)).astype(jnp.float32)

@jax.custom_vjp
def low_back(v):
    return v

def low_keep(v):
    return (low(v), None)

def low_pass(kept, grad):
    return (grad,)

def back_keep(v):
    return (v, None)

def back_low(kept, grad):
    return (low(grad),)
low.defvjp(low_keep, low_pass)
low_back.defvjp(back_keep, back_low)

def layer_norm(tokens, norm_gain, norm_bias):
    center = tokens - lax.optimization_barrier(jnp.mean(tokens, axis=-1, keepdims=True))
    spread = lax.optimization_barrier(jnp.mean(center * center, axis=-1, keepdims=True))
    return center * lax.rsqrt(spread + 1e-05) * norm_gain + norm_bias

def premix(tokens, norm_gain, norm_bias, mix_rates, previous):
    normed = layer_norm(tokens, norm_gain, norm_bias)
    shifted = jnp.concatenate([previous[:, None, :], normed[:, :-1, :]], axis=1)
    rate_rows = mix_rates[:, None, None, :]
    mixture = normed[None] * rate_rows + shifted[None] * (1.0 - rate_rows)
    return (mixture, normed[:, -1, :])

def matmul(left_operand, weight_matrix):
    return jnp.einsum('gld,de->gle', left_operand, weight_matrix, precision=precise)

def scaled_content_sweep(address_linear_map, content_linear_map, feature_fading_speed, opening_item_reward, accruing_upper_sum, accruing_normalizer):

    def advance(running, inputs):
        present_upper_sum, present_normalizer = running
        present_address, present_content = inputs
        exponentiated_reward = jnp.exp(opening_item_reward + present_address)
        returned_content = (present_upper_sum + exponentiated_reward * present_content) / (present_normalizer + exponentiated_reward)
        exp_key = jnp.exp(present_address)
        present_upper_sum = jnp.exp(-feature_fading_speed) * present_upper_sum + exp_key * present_content
        present_normalizer = jnp.exp(-feature_fading_speed) * present_normalizer + exp_key
        return ((present_upper_sum, present_normalizer), returned_content)
    (accruing_upper_sum, accruing_normalizer), results = lax.scan(advance, (accruing_upper_sum, accruing_normalizer), (address_linear_map.transpose(1, 0, 2), content_linear_map.transpose(1, 0, 2)))
    return (results.transpose(1, 0, 2), accruing_upper_sum, accruing_normalizer)

def time_mix(tokens, weight_in, weight_out, gain_row, bias_row, rate_rows, wkv_rows, carried):
    mixture, last_row = premix(tokens, gain_row, bias_row, rate_rows, carried[0])
    channels = tokens.shape[-1]
    address_linear_map = low_back(matmul(low(mixture[0]), weight_in[:, :channels]))
    content_linear_map = low_back(matmul(low(mixture[2]), weight_in[:, channels:2 * channels]))
    recept = low_back(matmul(low(mixture[1]), weight_in[:, 2 * channels:3 * channels]))
    weighted_avg, accruing_upper_sum, accruing_normalizer = scaled_content_sweep(address_linear_map, content_linear_map, jnp.exp(wkv_rows[0]), wkv_rows[1], carried[1], carried[2])
    gated_mix = jax.nn.sigmoid(recept) * weighted_avg
    branch = low_back(matmul(low(gated_mix), weight_in[:, 3 * channels:]))
    return (tokens + branch, jnp.stack([last_row, accruing_upper_sum, accruing_normalizer]))

def channel_mix(tokens, weight_in, weight_out, gain_row, bias_row, rate_rows, wkv_rows, carried):
    mixture, last_row = premix(tokens, gain_row, bias_row, rate_rows, carried[0])
    hidden_width = weight_in.shape[1]
    pre_act = low_back(matmul(low(mixture[0]), weight_in))
    hidden = low(jnp.square(jnp.maximum(pre_act, 0.0)))
    key_value = low_back(matmul(hidden, weight_out[:hidden_width]))
    recept = low_back(matmul(low(mixture[1]), weight_out[hidden_width:]))
    zero_rows = jnp.zeros_like(last_row)
    return (tokens + jax.nn.sigmoid(recept) * key_value, jnp.stack([last_row, zero_rows, zero_rows]))

def forward(weights, probes, tokens, carried):
    weight_in, weight_out, gains, biases, rates, wkv_all = weights
    current = tokens
    outputs = []
    finals = []
    for section_pos in range(N_SECTION):
        entry = low_back(current) + probes[section_pos]
        if section_pos % 2 == 0:
            sublayer = time_mix
        else:
            sublayer = channel_mix
        returned_content, final_rows = sublayer(entry, weight_in[section_pos], weight_out[section_pos], gains[section_pos], biases[section_pos], rates[section_pos], wkv_all[section_pos], carried[section_pos])
        current = low(returned_content)
        outputs.append(current)
        finals.append(final_rows)
    return (current, (jnp.stack(outputs), jnp.stack(finals)))

def reference(block_input, carried_state, output_cotangent, in_weight, out_weight, norm_gain, norm_bias, mix_rates, wkv_params):
    group_size = 2
    seq_total = MICRO * BATCH
    group_count = seq_total // group_size
    inputs_all = block_input.astype(jnp.float32).reshape(group_count, group_size, LENGTH, D)
    cotangents = output_cotangent.astype(jnp.float32).reshape(group_count, group_size, LENGTH, D)
    states_all = carried_state.astype(jnp.float32).reshape(N_SECTION, 3, group_count, group_size, D).transpose(2, 0, 1, 3, 4)
    weights = (in_weight.astype(jnp.float32), out_weight.astype(jnp.float32), norm_gain.astype(jnp.float32), norm_bias.astype(jnp.float32), mix_rates.astype(jnp.float32), wkv_params.astype(jnp.float32))

    def one_group(totals, inputs):
        tokens, cotangent, carried = inputs
        probes = jnp.zeros((N_SECTION,) + tokens.shape, jnp.float32)

        def local_forward(weight_set, probe_set):
            return forward(weight_set, probe_set, tokens, carried)
        final_out, pullback, aux_out = jax.vjp(local_forward, weights, probes, has_aux=True)
        grad_weights, grad_probes = pullback(cotangent)
        totals = jax.tree.map(jnp.add, totals, grad_weights)
        return (totals, (aux_out[0], aux_out[1], grad_probes))
    zero_totals = jax.tree.map(jnp.zeros_like, weights)
    totals, (outputs, finals, grad_probes) = lax.scan(one_group, zero_totals, (inputs_all, cotangents, states_all))
    section_outputs = outputs.transpose(1, 0, 2, 3, 4).reshape(N_SECTION, MICRO, BATCH, LENGTH, D).astype(jnp.bfloat16)
    all_states = finals.transpose(1, 2, 0, 3, 4).reshape(N_SECTION, 3, MICRO, BATCH, D)
    final_state = all_states[:, 1:]
    last_normed = all_states[:, 0]
    section_grads = grad_probes.transpose(1, 0, 2, 3, 4).reshape(N_SECTION, MICRO, BATCH, LENGTH, D).astype(jnp.bfloat16)
    return (section_outputs, final_state, last_normed, section_grads, totals[0], totals[1], totals[2], totals[3], totals[4], totals[5])
```

```python
import functools

import jax
import jax.numpy as jnp
from jax import lax
from jax.experimental import pallas as pl
from jax.experimental.pallas import tpu as pltpu
from jax.sharding import PartitionSpec as P

MESH = pl.DeviceIdType.MESH
F32 = jnp.float32
BF16 = jnp.bfloat16
CHUNK = 256
ROWS = 32
UNROLL = 4
VMEM_BYTES = 63 << 20

T_MIX0, T_MIX2, T_MIX1, T_GATED, C_MIX0, C_MIX1 = 0, 1, 2, 3, 4, 5
EARLY = 6
T_DK, T_DV, T_DQ, T_G, C_DKV, C_DQ, C_HID, C_DPRE = 0, 1, 2, 3, 4, 5, 6, 10
LATE = 14
KEPT = EARLY + LATE
GAIN, BIAS, RATES, DECAY, BONUS = 0, 1, 2, 5, 6


def nn(left, right):
    return jnp.dot(left, right, preferred_element_type=F32)


def nt(left, right):
    return lax.dot_general(left, right, (((1,), (1,)), ((), ())), preferred_element_type=F32)


def tn(left, right):
    return lax.dot_general(left, right, (((0,), (0,)), ((), ())), preferred_element_type=F32)


def folded(rows):
    total = rows[0:8]
    for start in range(8, rows.shape[0], 8):
        total = total + rows[start : start + 8]
    return total


def chain_kernel(
    sections,
    length,
    channels,
    hidden_blocks,
    x_hbm,
    cot_hbm,
    w_in_hbm,
    w_out_hbm,
    gain_hbm,
    bias_hbm,
    rates_hbm,
    wkv_hbm,
    state_hbm,
    outs_hbm,
    grads_hbm,
    fin_hbm,
    sums_hbm,
    kept_hbm,
    weights,
    early,
    kept,
    entry,
    hs,
    states,
    upstream,
    wide,
    pairs,
    tables,
    triangles,
    gains,
    biases,
    rates,
    wkvs,
    starts,
    previous,
    carry,
    carry_next,
    fin,
    sums,
    totals,
    weight_sem,
    weight_send,
    small_sem,
    small_send,
    entry_sem,
    entry_send,
    up_sem,
    up_send,
    out_sem,
    out_send,
    out_recv,
    early_sem,
    kept_sem,
):
    section = lax.axis_index("section")
    core = section % 2
    stage = section // 2
    stages = sections // 2
    partner = {"section": section + 1 - 2 * core}
    chunks = length // CHUNK
    blocks = CHUNK // ROWS
    time_blocks = 4
    last_stage = stage == stages - 1

    barrier = pltpu.get_barrier_semaphore()
    pl.semaphore_signal(barrier, inc=1, device_id=partner, device_id_type=MESH)

    @pl.when(stage > 0)
    def _():
        pl.semaphore_signal(
            barrier, inc=1, device_id={"section": section - 2}, device_id_type=MESH
        )

    @pl.when(stage < stages - 1)
    def _():
        pl.semaphore_signal(
            barrier, inc=1, device_id={"section": section + 2}, device_id_type=MESH
        )

    def entry_copy(chunk):
        rows = pl.ds(chunk * CHUNK, CHUNK)
        return pltpu.make_async_copy(
            x_hbm.at[core, 0, rows], entry.at[rows], entry_sem.at[chunk]
        )

    def up_copy(chunk):
        rows = pl.ds(chunk * CHUNK, CHUNK)
        return pltpu.make_async_copy(
            cot_hbm.at[core, 0, rows], upstream.at[rows], up_sem.at[chunk]
        )

    @pl.when(stage == 0)
    def _():
        for chunk in range(chunks):
            entry_copy(chunk).start()

    @pl.when(last_stage)
    def _():
        for chunk in range(chunks):
            up_copy(chunk).start()

    small_pairs = (
        (gain_hbm, gains.at[core]),
        (bias_hbm, biases.at[core]),
        (rates_hbm, rates.at[core]),
        (wkv_hbm.at[0], wkvs.at[core]),
        (state_hbm.at[0], starts.at[core]),
    )
    small_copies = [
        pltpu.make_async_copy(source, target, small_sem.at[0, at])
        for at, (source, target) in enumerate(small_pairs)
    ]
    for copy in small_copies:
        copy.start()

    def in_block(index):
        return w_in_hbm.at[0, :, pl.ds(index * channels, channels)]

    def out_block(index):
        return w_out_hbm.at[0, pl.ds(index * channels, channels), :]

    for index in range(4):
        slot = core * time_blocks + index
        pltpu.make_async_copy(in_block(index), weights.at[slot], weight_sem.at[slot]).start()

    @pl.when(core == 1)
    def _():
        for index in range(hidden_blocks + 1):
            slot = 8 + index
            pltpu.make_async_copy(
                out_block(index), weights.at[slot], weight_sem.at[slot]
            ).start()

    has_previous = jnp.where(stage > 0, 1, 0)
    has_next = jnp.where(stage < stages - 1, 1, 0)
    pl.semaphore_wait(barrier, 1 + has_previous + has_next)

    small_remotes = [
        pltpu.make_async_remote_copy(
            src_ref=source,
            dst_ref=target,
            send_sem=small_send.at[at],
            recv_sem=small_sem.at[1, at],
            device_id=partner,
            device_id_type=MESH,
        )
        for at, (source, target) in enumerate(small_pairs)
    ]

    def in_remote(index):
        slot = core * time_blocks + index
        return pltpu.make_async_remote_copy(
            src_ref=in_block(index),
            dst_ref=weights.at[slot],
            send_sem=weight_send.at[slot],
            recv_sem=weight_sem.at[slot],
            device_id=partner,
            device_id_type=MESH,
        )

    def out_remote(index):
        slot = 8 + index
        return pltpu.make_async_remote_copy(
            src_ref=out_block(index),
            dst_ref=weights.at[slot],
            send_sem=weight_send.at[slot],
            recv_sem=weight_sem.at[slot],
            device_id=partner,
            device_id_type=MESH,
        )

    for copy in small_remotes:
        copy.start()
    for index in range(4):
        in_remote(index).start()

    @pl.when(core == 1)
    def _():
        for index in (hidden_blocks, *range(hidden_blocks)):
            out_remote(index).start()

    row_at = lax.broadcasted_iota(jnp.int32, (CHUNK, 2 * CHUNK), 0)
    column_at = lax.broadcasted_iota(jnp.int32, (CHUNK, 2 * CHUNK), 1)
    column_at = jnp.where(column_at >= CHUNK, column_at - CHUNK, column_at)
    triangles[0] = jnp.where(row_at > column_at, 1.0, 0.0).astype(BF16)
    triangles[1] = jnp.where(row_at < column_at, 1.0, 0.0).astype(BF16)
    sums[...] = jnp.zeros_like(sums)
    fin[...] = jnp.zeros_like(fin)

    for copy in small_copies:
        copy.wait()
    for copy in small_remotes:
        copy.wait_recv()

    rate = jnp.exp(wkvs[0, 0:1, :])
    step = jnp.exp(-rate)
    lift = jnp.exp(wkvs[0, 1:2, :])

    def table_rows(index, _):
        start = pl.multiple_of(index * ROWS, ROWS)
        place = (lax.broadcasted_iota(jnp.int32, (ROWS, channels), 0) + start).astype(F32)
        tables[0, pl.ds(start, ROWS), :] = jnp.exp(-(CHUNK - 1.0 - place) * rate)
        tables[1, pl.ds(start, ROWS), :] = jnp.exp(-place * rate)
        return 0

    lax.fori_loop(0, blocks, table_rows, 0)

    for row in range(3):
        carry[row : row + 1] = starts[0, row, core]
    carry[3:4] = starts[1, 0, core]

    def weight_wait(slot):
        pltpu.make_async_copy(weights.at[slot], weights.at[slot], weight_sem.at[slot]).wait()

    def stats(tokens):
        center = tokens - jnp.mean(tokens, axis=-1, keepdims=True)
        spread = jnp.mean(center * center, axis=-1, keepdims=True)
        root = lax.rsqrt(spread + 1e-05)
        return center * root, root

    row_index = lax.broadcasted_iota(jnp.int32, (ROWS, channels), 0)

    def token_mix(kind, source, base, side, slots, carry_row):
        gain, bias = gains[kind], biases[kind]

        def body(index, before):
            start = pl.multiple_of(base + index * ROWS, ROWS)
            rows = pl.ds(start, ROWS)
            unit, _ = stats(source[rows, :].astype(F32))
            normed = unit * gain + bias
            previous[kind, pl.ds(start // ROWS, 1), :] = before
            shifted = jnp.where(
                row_index == 0, jnp.broadcast_to(before, normed.shape), pltpu.roll(normed, 1, 0)
            )
            gap = normed - shifted
            for rate_row, slot in slots:
                early[side, slot, pl.ds(pl.multiple_of(index * ROWS, ROWS), ROWS), :] = (
                    shifted + gap * rates[kind, rate_row]
                ).astype(BF16)
            return normed[ROWS - 1 : ROWS, :]

        carry[carry_row : carry_row + 1] = lax.fori_loop(
            0, blocks, body, carry[carry_row : carry_row + 1], unroll=UNROLL
        )

    def early_copy(chunk):
        rows = pl.ds(pl.multiple_of(chunk * CHUNK, CHUNK), CHUNK)
        side = chunk % 2
        return pltpu.make_async_copy(
            early.at[side], kept_hbm.at[pl.ds(0, EARLY), rows], early_sem.at[side]
        )

    def forward_chunk(chunk, _):
        base = pl.multiple_of(chunk * CHUNK, CHUNK)
        rows = pl.ds(base, CHUNK)
        side = chunk % 2

        @pl.when(chunk >= 2)
        def _():
            early_copy(chunk - 2).wait()

        pltpu.make_async_copy(entry.at[rows], entry.at[rows], entry_sem.at[chunk]).wait()

        token_mix(0, entry, base, side, ((0, T_MIX0), (2, T_MIX2), (1, T_MIX1)), 0)

        for slot in range(3):

            @pl.when(chunk == 0)
            def _():
                weight_wait(slot)

            wide[slot] = nn(early[side, slot], weights[slot])

        def weighted(index, _):
            start = pl.multiple_of(index * ROWS, ROWS)
            local = pl.ds(start, ROWS)
            whole = pl.ds(pl.multiple_of(base + start, ROWS), ROWS)
            value = wide[1, local, :]
            power = jnp.exp(wide[0, local, :])
            wide[0, local, :] = power
            scaled = power * tables[0, local, :]
            pairs[local, pl.ds(0, channels)] = (scaled * value).astype(BF16)
            pairs[local, pl.ds(channels, channels)] = scaled.astype(BF16)
            kept[T_DK, whole, :] = power.astype(BF16)
            kept[T_DV, whole, :] = value.astype(BF16)
            return 0

        lax.fori_loop(0, blocks, weighted, 0)
        wide[3] = nn(triangles[0, :, pl.ds(0, CHUNK)], pairs[pl.ds(0, CHUNK), pl.ds(0, channels)])
        wide[4] = nn(
            triangles[0, :, pl.ds(0, CHUNK)], pairs[pl.ds(0, CHUNK), pl.ds(channels, channels)]
        )
        upper, lower = carry[1:2], carry[2:3]

        def averaged(index, _):
            start = pl.multiple_of(index * ROWS, ROWS)
            local = pl.ds(start, ROWS)
            whole = pl.ds(pl.multiple_of(base + start, ROWS), ROWS)
            place = (row_index + start).astype(F32)
            grown = jnp.exp((CHUNK - place) * rate)
            faded = tables[1, local, :]
            power, value = wide[0, local, :], wide[1, local, :]
            before_upper = grown * wide[3, local, :] + faded * upper
            before_lower = grown * wide[4, local, :] + faded * lower
            now = power * lift
            average = (before_upper + now * value) / (before_lower + now)
            gate = jax.nn.sigmoid(wide[2, local, :])
            states[0, whole, :] = before_upper
            states[1, whole, :] = before_lower
            kept[T_DQ, whole, :] = gate.astype(BF16)
            early[side, T_GATED, local, :] = (gate * average).astype(BF16)
            tail = slice(ROWS - 8, ROWS)
            after_upper = step * before_upper[tail] + power[tail] * value[tail]
            after_lower = step * before_lower[tail] + power[tail]
            carry_next[0:1] = after_upper[7:8]
            carry_next[1:2] = after_lower[7:8]
            return 0

        lax.fori_loop(0, blocks, averaged, 0)
        carry[1:3] = carry_next[0:2]

        @pl.when(chunk == 0)
        def _():
            weight_wait(3)

        hs[0, rows, :] = (
            entry[rows, :].astype(F32) + nn(early[side, T_GATED], weights[3])
        ).astype(BF16)

        token_mix(1, hs.at[0], base, side, ((0, C_MIX0), (1, C_MIX1)), 3)

        for index in range(hidden_blocks):

            @pl.when(chunk == 0)
            def _():
                weight_wait(4 + index)

            pre = nn(early[side, C_MIX0], weights[4 + index])
            kept[C_HID + index, rows, :] = jnp.square(jnp.maximum(pre, 0.0)).astype(BF16)

        @pl.when(chunk == 0)
        def _():
            weight_wait(8 + hidden_blocks)

        early_copy(chunk).start()
        wide[1] = nn(early[side, C_MIX1], weights[8 + hidden_blocks])

        @pl.when(chunk == 0)
        def _():
            for index in range(hidden_blocks):
                weight_wait(8 + index)

        total = nn(kept[C_HID, rows, :], weights[8])
        for index in range(1, hidden_blocks):
            total = total + nn(kept[C_HID + index, rows, :], weights[8 + index])
        wide[0] = total

        def joined(index, _):
            start = pl.multiple_of(index * ROWS, ROWS)
            local = pl.ds(start, ROWS)
            whole = pl.ds(pl.multiple_of(base + start, ROWS), ROWS)
            gate = jax.nn.sigmoid(wide[1, local, :])
            value = wide[0, local, :]
            kept[C_DKV, whole, :] = gate.astype(BF16)
            kept[C_DQ, whole, :] = value.astype(BF16)
            hs[1, whole, :] = (hs[0, whole, :].astype(F32) + gate * value).astype(BF16)
            return 0

        lax.fori_loop(0, blocks, joined, 0)

        @pl.when(stage < stages - 1)
        def _():
            entry_remote(chunk).start()

        return 0

    def entry_remote(chunk):
        rows = pl.ds(pl.multiple_of(chunk * CHUNK, CHUNK), CHUNK)
        return pltpu.make_async_remote_copy(
            src_ref=hs.at[1, rows],
            dst_ref=entry.at[rows],
            send_sem=entry_send.at[chunk],
            recv_sem=entry_sem.at[chunk],
            device_id={"section": section + 2},
            device_id_type=MESH,
        )

    def up_remote(chunk):
        rows = pl.ds(pl.multiple_of(chunk * CHUNK, CHUNK), CHUNK)
        return pltpu.make_async_remote_copy(
            src_ref=upstream.at[rows],
            dst_ref=upstream.at[rows],
            send_sem=up_send.at[chunk],
            recv_sem=up_sem.at[chunk],
            device_id={"section": section - 2},
            device_id_type=MESH,
        )

    lax.fori_loop(0, chunks, forward_chunk, 0)
    early_copy(chunks - 2).wait()
    early_copy(chunks - 1).wait()
    fin[0, 0:1] = carry[0:1]
    fin[0, 1:3] = carry[1:3]
    fin[1, 0:1] = carry[3:4]

    def to_owner(index, own_src, other_src, dst):
        own = pltpu.make_async_copy(own_src, dst, out_sem.at[index])
        other = pltpu.make_async_remote_copy(
            src_ref=other_src,
            dst_ref=dst,
            send_sem=out_send.at[index],
            recv_sem=out_recv.at[index],
            device_id=partner,
            device_id_type=MESH,
        )
        return own, other

    outs_copies = to_owner(0, hs.at[core], hs.at[1 - core], outs_hbm.at[core])
    fin_copies = to_owner(1, fin.at[core], fin.at[1 - core], fin_hbm.at[core])
    for copy in outs_copies + fin_copies:
        copy.start()

    carry[0:4] = jnp.zeros((4, channels), F32)

    def norm_back(kind, source, base, mixes, above, target, carry_row):
        gain, bias = gains[kind], biases[kind]

        def body(index, after):
            back = blocks - 1 - index
            local = pl.ds(pl.multiple_of(back * ROWS, ROWS), ROWS)
            start = pl.multiple_of(base + back * ROWS, ROWS)
            rows = pl.ds(start, ROWS)
            unit, root = stats(source[rows, :].astype(F32))
            normed = unit * gain + bias
            before = previous[kind, pl.ds(start // ROWS, 1), :]
            shifted = jnp.where(
                row_index == 0, jnp.broadcast_to(before, normed.shape), pltpu.roll(normed, 1, 0)
            )
            gap = normed - shifted
            straight = jnp.zeros_like(normed)
            total = jnp.zeros_like(normed)
            for rate_row, slot in mixes:
                mix = wide[slot, local, :]
                straight = straight + mix * rates[kind, rate_row]
                total = total + mix
                sums[kind, RATES + rate_row] += folded(mix * gap)
            late = total - straight
            moved = jnp.where(
                row_index == ROWS - 1,
                jnp.broadcast_to(after, late.shape),
                pltpu.roll(late, ROWS - 1, 0),
            )
            d_normed = straight + moved
            sums[kind, GAIN] += folded(d_normed * unit)
            sums[kind, BIAS] += folded(d_normed)
            d_unit = d_normed * gain
            d_tokens = (
                d_unit
                - jnp.mean(d_unit, axis=-1, keepdims=True)
                - unit * jnp.mean(d_unit * unit, axis=-1, keepdims=True)
            ) * root
            target[rows, :] = (above[rows, :].astype(F32) + d_tokens).astype(BF16)
            return late[0:1, :]

        carry[carry_row : carry_row + 1] = lax.fori_loop(
            0, blocks, body, carry[carry_row : carry_row + 1], unroll=UNROLL
        )

    def late_copy(chunk, part):
        rows = pl.ds(pl.multiple_of(chunk * CHUNK, CHUNK), CHUNK)
        begin, count = ((C_DKV, LATE - C_DKV), (T_DK, C_DKV))[part]
        return pltpu.make_async_copy(
            kept.at[pl.ds(begin, count), rows],
            kept_hbm.at[pl.ds(EARLY + begin, count), rows],
            kept_sem.at[part, chunk],
        )

    def grad_copies(chunk, kind):
        rows = pl.ds(pl.multiple_of(chunk * CHUNK, CHUNK), CHUNK)
        sources = (upstream.at[rows], kept.at[T_G, rows])
        return to_owner(
            2 + chunk, sources[kind], sources[1 - kind], grads_hbm.at[core, rows]
        )

    def backward_chunk(turn, _):
        chunk = chunks - 1 - turn
        base = pl.multiple_of(chunk * CHUNK, CHUNK)
        rows = pl.ds(base, CHUNK)
        pltpu.make_async_copy(upstream.at[rows], upstream.at[rows], up_sem.at[chunk]).wait()

        def split(index, _):
            whole = pl.ds(pl.multiple_of(base + index * ROWS, ROWS), ROWS)
            above = upstream[whole, :].astype(F32)
            gate = kept[C_DKV, whole, :].astype(F32)
            value = kept[C_DQ, whole, :].astype(F32)
            d_value = above * gate
            kept[C_DKV, whole, :] = d_value.astype(BF16)
            kept[C_DQ, whole, :] = (d_value * value * (1.0 - gate)).astype(BF16)
            return 0

        lax.fori_loop(0, blocks, split, 0)

        for index in range(hidden_blocks):
            d_hidden = nt(kept[C_DKV, rows, :], weights[8 + index])
            slope = jnp.sqrt(kept[C_HID + index, rows, :].astype(F32))
            kept[C_DPRE + index, rows, :] = (d_hidden * (2.0 * slope)).astype(BF16)
        total = nt(kept[C_DPRE, rows, :], weights[4])
        for index in range(1, hidden_blocks):
            total = total + nt(kept[C_DPRE + index, rows, :], weights[4 + index])
        wide[0] = total
        wide[1] = nt(kept[C_DQ, rows, :], weights[8 + hidden_blocks])
        late_copy(chunk, 0).start()
        norm_back(1, hs.at[0], base, ((0, 0), (1, 1)), upstream, kept.at[T_G], 3)

        wide[0] = nt(kept[T_G, rows, :], weights[3])

        def inputs(index, _):
            start = pl.multiple_of(index * ROWS, ROWS)
            local = pl.ds(start, ROWS)
            whole = pl.ds(pl.multiple_of(base + start, ROWS), ROWS)
            power = kept[T_DK, whole, :].astype(F32)
            value = kept[T_DV, whole, :].astype(F32)
            gate = kept[T_DQ, whole, :].astype(F32)
            now = power * lift
            inverse = 1.0 / (states[1, whole, :] + now)
            average = (states[0, whole, :] + now * value) * inverse
            d_average = wide[0, local, :] * gate
            kept[T_DQ, whole, :] = (d_average * average * (1.0 - gate)).astype(BF16)
            unit = d_average * inverse
            wide[1, local, :] = unit
            wide[2, local, :] = average
            scaled = unit * tables[1, local, :]
            for column, term in ((0, scaled), (channels, -scaled * average)):
                high = term.astype(BF16)
                pairs[local, pl.ds(column, channels)] = high
                pairs[pl.ds(pl.multiple_of(CHUNK + start, ROWS), ROWS), pl.ds(column, channels)] = (
                    term - high.astype(F32)
                ).astype(BF16)
            return 0

        lax.fori_loop(0, blocks, inputs, 0)
        wide[3] = nn(triangles[1], pairs[:, pl.ds(0, channels)])
        wide[4] = nn(triangles[1], pairs[:, pl.ds(channels, channels)])
        alpha_after, beta_after = carry[1:2], carry[2:3]

        def outputs(index, _):
            start = pl.multiple_of((blocks - 1 - index) * ROWS, ROWS)
            local = pl.ds(start, ROWS)
            whole = pl.ds(pl.multiple_of(base + start, ROWS), ROWS)
            place = (row_index + start).astype(F32)
            grown = jnp.exp((place + 1.0) * rate)
            faded = tables[0, local, :]
            alpha = grown * wide[3, local, :] + faded * alpha_after
            beta = grown * wide[4, local, :] + faded * beta_after
            unit, average = wide[1, local, :], wide[2, local, :]
            power = kept[T_DK, whole, :].astype(F32)
            value = kept[T_DV, whole, :].astype(F32)
            weighed = unit * (power * lift)
            own = weighed * (value - average)
            kept[T_DK, whole, :] = (own + power * (alpha * value + beta)).astype(BF16)
            kept[T_DV, whole, :] = (weighed + power * alpha).astype(BF16)
            sums[0, BONUS] += folded(own)
            sums[0, DECAY] += folded(
                alpha * states[0, whole, :] + beta * states[1, whole, :]
            )
            carry_next[0:1] = unit[0:1] + step * alpha[0:1]
            carry_next[1:2] = step * beta[0:1] - unit[0:1] * average[0:1]
            return 0

        lax.fori_loop(0, blocks, outputs, 0)
        carry[1:3] = carry_next[0:2]
        wide[0] = nt(kept[T_DK, rows, :], weights[0])
        wide[1] = nt(kept[T_DQ, rows, :], weights[2])
        wide[2] = nt(kept[T_DV, rows, :], weights[1])
        norm_back(
            0, entry, base, ((0, 0), (1, 1), (2, 2)), kept.at[T_G], upstream, 0
        )

        @pl.when(stage > 0)
        def _():
            up_remote(chunk).start()

        late_copy(chunk, 1).start()
        for kind in range(2):

            @pl.when(core == kind)
            def _():
                for copy in grad_copies(chunk, kind):
                    copy.start()

        return 0

    lax.fori_loop(0, chunks, backward_chunk, 0)

    sums[0, DECAY] = sums[0, DECAY] * (-rate * step)
    for kind in range(2):
        for row in range(7):
            totals[kind, row : row + 1] = jnp.sum(sums[kind, row], axis=0, keepdims=True)
        totals[kind, 7:8] = jnp.zeros((1, channels), F32)
    sums_copy = pltpu.make_async_copy(totals, sums_hbm, kept_sem.at[0, chunks])
    sums_copy.start()
    for copy in (sums_copy,) + outs_copies + fin_copies:
        copy.wait()
    for chunk in range(chunks):
        for part in range(2):
            late_copy(chunk, part).wait()
        for copy in grad_copies(chunk, 0):
            copy.wait()
    for copy in small_remotes:
        copy.wait_send()
    for index in range(4):
        in_remote(index).wait_send()

    @pl.when(core == 1)
    def _():
        for index in range(hidden_blocks + 1):
            out_remote(index).wait_send()

    @pl.when(stage < stages - 1)
    def _():
        for chunk in range(chunks):
            entry_remote(chunk).wait_send()

    @pl.when(stage > 0)
    def _():
        for chunk in range(chunks):
            up_remote(chunk).wait_send()


def chain(sections, x, cotangent, w_in, w_out, gain, bias, rates, wkv, state):
    length, channels = x.shape[2:]
    hidden_blocks = w_in.shape[2] // channels
    chunks = length // CHUNK
    anywhere = pl.BlockSpec(memory_space=pl.ANY)
    dma = pltpu.SemaphoreType.DMA
    slots = 9 + hidden_blocks
    return pl.pallas_call(
        functools.partial(chain_kernel, sections, length, channels, hidden_blocks),
        out_shape=(
            jax.ShapeDtypeStruct((2, length, channels), BF16),
            jax.ShapeDtypeStruct((2, length, channels), BF16),
            jax.ShapeDtypeStruct((2, 8, channels), F32),
            jax.ShapeDtypeStruct((2, 8, channels), F32),
            jax.ShapeDtypeStruct((KEPT, length, channels), BF16),
        ),
        in_specs=[anywhere] * 9,
        out_specs=(anywhere,) * 5,
        scratch_shapes=[
            pltpu.VMEM((slots, channels, channels), BF16),
            pltpu.VMEM((2, EARLY, CHUNK, channels), BF16),
            pltpu.VMEM((LATE, length, channels), BF16),
            pltpu.VMEM((length, channels), BF16),
            pltpu.VMEM((2, length, channels), BF16),
            pltpu.VMEM((2, length, channels), F32),
            pltpu.VMEM((length, channels), BF16),
            pltpu.VMEM((5, CHUNK, channels), F32),
            pltpu.VMEM((2 * CHUNK, 2 * channels), BF16),
            pltpu.VMEM((2, CHUNK, channels), F32),
            pltpu.VMEM((2, CHUNK, 2 * CHUNK), BF16),
            pltpu.VMEM((2, 1, channels), F32),
            pltpu.VMEM((2, 1, channels), F32),
            pltpu.VMEM((2, 3, 1, channels), F32),
            pltpu.VMEM((2, 2, channels), F32),
            pltpu.VMEM((2, 3, 2, 1, channels), F32),
            pltpu.VMEM((2, length // ROWS, channels), F32),
            pltpu.VMEM((8, channels), F32),
            pltpu.VMEM((8, channels), F32),
            pltpu.VMEM((2, 8, channels), F32),
            pltpu.VMEM((2, 8, 8, channels), F32),
            pltpu.VMEM((2, 8, channels), F32),
            dma((slots,)),
            dma((slots,)),
            dma((2, 5)),
            dma((5,)),
            dma((chunks,)),
            dma((chunks,)),
            dma((chunks,)),
            dma((chunks,)),
            dma((2 + chunks,)),
            dma((2 + chunks,)),
            dma((2 + chunks,)),
            dma((2,)),
            dma((2, chunks + 1)),
        ],
        compiler_params=pltpu.CompilerParams(
            collective_id=0, has_side_effects=True, vmem_limit_bytes=VMEM_BYTES
        ),
    )(x, cotangent, w_in, w_out, gain, bias, rates, wkv, state)


C_BLOCKS = 9
T_BLOCKS = 4
BLOCKS = C_BLOCKS + T_BLOCKS
PLACES = (8, 9, 0, 1, 2, 3, 10, 4, 5, 6, 11, 12, 7)
PAIRED = 8


def lookup(index, table):
    value = jnp.int32(table[0])
    for at, entry in enumerate(table[1:], 1):
        value = jnp.where(index == at, entry, value)
    return value


def reduce_plan(line, half):
    pieces = (max(16, half // (2 * line)), max(16, half // line))
    sizes = (2 * line * pieces[0], line * pieces[1])
    counts = (-(-PAIRED * half // sizes[0]), -(-(BLOCKS - PAIRED) * half // sizes[1]))
    return pieces, sizes, counts


def ready_times(first, size, count, half):
    made = {place: time for time, place in enumerate(PLACES)}
    times = []
    for group in range(count):
        begin, end = first + group * size, first + (group + 1) * size
        times.append(
            max(made[place] for place in range(BLOCKS) if place * half < end and begin < (place + 1) * half)
        )
    return tuple(times)


COMPUTE = 2
FETCHED_AHEAD = 3
ORDER_OF_FOUR = (
    2000, 1000, 2010, 2020, 1001, 1010, 2030, 2040, 1002, 2050, 30, 1011, 2060, 1020, 2070, 1003,
    2080, 1012, 31, 1021, 2090, 0, 2100, 1004, 1013, 2110, 1022, 2120, 32, 1, 1005, 50,
    1014, 1023, 1006, 2, 33, 1040, 1015, 1007, 51, 3, 60, 1016, 1041, 52, 34, 1017,
    61, 70, 1042, 53, 35, 62, 20, 1024, 71, 1043, 4, 36, 1030, 63, 1025, 21,
    40, 5, 72, 37, 1044, 1026, 1031, 6, 22, 64, 41, 73, 1027, 1045, 7, 1032,
    10, 23, 65, 42, 1046, 1033, 11, 24, 66, 43, 1047, 12, 25, 67, 44, 13,
    26, 45, 14, 27, 46, 15, 47, 16, 54, 74, 17, 55, 75, 1034, 56, 76,
    1035, 77, 57, 1036, 1037,
)


def event_order(line, half):
    _, sizes, counts = reduce_plan(line, half)
    if line == 4 and counts == (8, 5):
        return [(code // 1000, code // 10 % 100, code % 10) for code in ORDER_OF_FOUR]
    firsts = (0, counts[0] * sizes[0])
    steps = [(block, 0, (COMPUTE, block, 0)) for block in range(BLOCKS)]
    for kind in range(2):
        times = ready_times(firsts[kind], sizes[kind], counts[kind], half)
        for group, time in enumerate(times):
            steps += [(time + turn, 1 + kind, (kind, group, turn)) for turn in range(2 * line)]
    return [step for _, _, step in sorted(steps)]


def reduce_kernel(
    count,
    length,
    channels,
    kept_hbm,
    sums_hbm,
    in_hbm,
    out_hbm,
    total_hbm,
    kept,
    mine,
    theirs,
    pair_landing,
    cross_landing,
    right0,
    left0,
    right1,
    left1,
    small,
    kept_sem,
    pair_sem,
    pair_send,
    y_sem,
    y_send,
    sum_sem0,
    sum_send0,
    sum_sem1,
    sum_send1,
    spread_sem0,
    spread_send0,
    spread_sem1,
    spread_send1,
    give_sem,
    give_send,
    give_recv,
    small_sem,
    small_send,
):
    section = lax.axis_index("section")
    dp_index = lax.axis_index("dp")
    core = section % 2
    line = count // 2
    z, y = dp_index // 2, dp_index % 2
    half = channels // 2
    pieces, sizes, counts = reduce_plan(line, half)
    firsts = (0, counts[0] * sizes[0])
    partner = {"section": section + 1 - 2 * core}
    across = {"dp": dp_index + 1 - 2 * y}

    def peer(offset):
        return {"dp": lax.rem(dp_index + offset, count)}

    late = EARLY

    def operands(block):
        turn = block - C_BLOCKS
        left = jnp.where(block < 8, late + C_HID + block - 4, jnp.where(block == 8, C_MIX1, T_MIX0 + turn))
        left = jnp.where(block < 4, C_MIX0, left)
        right = jnp.where(block == 8, late + C_DQ, late + T_DK + turn)
        right = jnp.where(block < 8, late + C_DKV, right)
        right = jnp.where(block < 4, late + C_DPRE + block, right)
        return (left, (block == 0) | (block >= 4)), (right, (block <= 4) | (block >= 8))

    def kept_copy(slot):
        return pltpu.make_async_copy(kept_hbm.at[slot], kept.at[slot], kept_sem.at[slot])

    def fetch(block):
        for slot, first in operands(block):
            pl.when(first & (block < BLOCKS))(lambda: kept_copy(slot).start())

    for block in range(FETCHED_AHEAD):
        fetch(jnp.int32(block))
    own_small = pltpu.make_async_copy(sums_hbm.at[core], small.at[0], small_sem.at[0])
    own_small.start()

    barrier = pltpu.get_barrier_semaphore()
    diagonal = {"section": section + 1 - 2 * core, "dp": dp_index + 1 - 2 * y}
    for device in (partner, diagonal):
        pl.semaphore_signal(barrier, inc=1, device_id=device, device_id_type=MESH)

    def greet(offset, _):
        pl.semaphore_signal(barrier, inc=1, device_id=peer(offset), device_id_type=MESH)
        return 0

    lax.fori_loop(1, count, greet, 0)

    small_pair = pltpu.make_async_remote_copy(
        src_ref=sums_hbm.at[1 - core],
        dst_ref=small.at[1],
        send_sem=small_send.at[0],
        recv_sem=small_sem.at[1],
        device_id=partner,
        device_id_type=MESH,
    )

    def small_copy(offset):
        return pltpu.make_async_remote_copy(
            src_ref=small.at[0],
            dst_ref=small.at[1 + offset],
            send_sem=small_send.at[offset],
            recv_sem=small_sem.at[1 + offset],
            device_id=peer(offset),
            device_id_type=MESH,
        )

    def small_start(offset, _):
        small_copy(offset).start()
        return 0

    def small_add(offset, total):
        small_copy(offset).wait()
        return total + small[1 + offset]

    def product(block, which):
        (left, _), (right, _) = operands(block)
        columns = pl.ds(pl.multiple_of(which * half, 128), half)
        return tn(kept[left, :, columns], kept[right])

    def block_rows(block):
        return pl.ds(pl.multiple_of(lookup(block, PLACES) * half, half), half)

    def sent_rows(block):
        return pl.ds(pl.multiple_of(block * half, half), half)

    def pair_copy(block):
        return pltpu.make_async_remote_copy(
            src_ref=theirs.at[sent_rows(block)],
            dst_ref=mine.at[block_rows(block)],
            send_sem=pair_send.at[block],
            recv_sem=pair_sem.at[block],
            device_id=partner,
            device_id_type=MESH,
        )

    def for_partner(block):
        for slot, first in operands(block):
            pl.when(first)(lambda: kept_copy(slot).wait())
        fetch(block + FETCHED_AHEAD)
        theirs[sent_rows(block), :] = product(block, 1 - core).astype(BF16)

        @pl.when(block == 0)
        def _():
            pl.semaphore_wait(barrier, count + 1)
            small_pair.start()

        pair_copy(block).start()

    def for_me(block):
        rows = block_rows(block)
        own = product(block, core)
        pair_copy(block).wait_recv()
        mine[rows, :] = (own + mine[rows, :].astype(F32)).astype(BF16)

    blocks_at = tuple(PLACES.index(place) for place in range(BLOCKS))

    def give(kind, group, start):
        size = pieces[kind]
        rows = pl.ds(pl.multiple_of(start, size), size)
        place = start // half if half % sizes[kind] else firsts[kind] // half + group * sizes[kind] // half
        block = lookup(place, blocks_at)
        row = core * half + start - place * half

        def copies(owner, target):
            @pl.when(owner == core)
            def _():
                pltpu.make_async_copy(mine.at[rows], target, give_sem.at[0]).start()

            def remote(device):
                return pltpu.make_async_remote_copy(
                    src_ref=mine.at[rows],
                    dst_ref=target,
                    send_sem=give_send.at[0],
                    recv_sem=give_recv.at[0],
                    device_id=device,
                    device_id_type=MESH,
                )

            @pl.when(owner != core)
            def _():
                remote(partner).start()

            if kind == 0:
                remote({"section": section - core + owner, "dp": dp_index + 1 - 2 * y}).start()

        def to_in(owner, column):
            columns = pl.ds(pl.multiple_of(column * channels, channels), channels)
            copies(owner, in_hbm.at[pl.ds(pl.multiple_of(row, size), size), columns])

        def to_out():
            within = (block - 4) * channels + row
            copies(1, out_hbm.at[pl.ds(pl.multiple_of(within, size), size)])

        of_time = block >= C_BLOCKS
        pl.when((block < 4) | (of_time & (place < BLOCKS)))(
            lambda: to_in(jnp.where(of_time, 0, 1), jnp.where(of_time, block - C_BLOCKS, block))
        )
        pl.when((block >= 4) & ~of_time)(to_out)

    right_peer, left_peer = {"dp": dp_index + 2}, {"dp": dp_index - 2}
    landings = ((right0, left0), (right1, left1))
    sum_sems = ((sum_sem0, sum_send0), (sum_sem1, sum_send1))
    spread_sems = ((spread_sem0, spread_send0), (spread_sem1, spread_send1))

    def piece_rows(kind, group, index):
        start = firsts[kind] + group * sizes[kind] + index * pieces[kind]
        if kind == 0:
            start = start + y * (sizes[0] // 2)
        return start, pl.ds(pl.multiple_of(start, pieces[kind]), pieces[kind])

    def sum_copy(kind, group, direction, step):
        place = landings[kind][direction].at[group, step]
        receive, send = sum_sems[kind]
        return pltpu.make_async_remote_copy(
            src_ref=place,
            dst_ref=place,
            send_sem=send.at[group, direction, step],
            recv_sem=receive.at[group, direction, step],
            device_id=(right_peer, left_peer)[direction],
            device_id_type=MESH,
        )

    def spread_copy(kind, group, direction, step, index):
        _, rows = piece_rows(kind, group, index)
        receive, send = spread_sems[kind]
        return pltpu.make_async_remote_copy(
            src_ref=mine.at[rows],
            dst_ref=mine.at[rows],
            send_sem=send.at[group, direction, step],
            recv_sem=receive.at[group, direction, step],
            device_id=(right_peer, left_peer)[direction],
            device_id_type=MESH,
        )

    def passing(kind, group, turn):
        for direction in range(2):
            behind = z if direction == 0 else line - 1 - z
            step = turn - behind
            index = line - 1 - step if direction == 0 else step
            place = landings[kind][direction].at[group, step]
            _, rows = piece_rows(kind, group, index)

            @pl.when((step >= 0) & (behind == 0) & (step < line - 1))
            def _():
                place[...] = mine[rows, :]
                sum_copy(kind, group, direction, step).start()

            @pl.when((step >= 0) & (behind > 0))
            def _():
                sum_copy(kind, group, direction, step).wait_recv()

                @pl.when(turn < line - 1)
                def _():
                    place[...] = (place[...].astype(F32) + mine[rows, :].astype(F32)).astype(BF16)
                    sum_copy(kind, group, direction, step).start()

    def arrived(kind, group):
        _, rows = piece_rows(kind, group, z)
        total = mine[rows, :].astype(F32)
        from_left = landings[kind][0].at[group, jnp.minimum(line - 1 - z, line - 2)]
        from_right = landings[kind][1].at[group, jnp.minimum(z, line - 2)]
        mine[rows, :] = total.astype(BF16)

        @pl.when(z == 0)
        def _():
            mine[rows, :] = (total + from_right[...].astype(F32)).astype(BF16)

        @pl.when(z == line - 1)
        def _():
            mine[rows, :] = (total + from_left[...].astype(F32)).astype(BF16)

        @pl.when((z > 0) & (z < line - 1))
        def _():
            mine[rows, :] = (
                total + from_left[...].astype(F32) + from_right[...].astype(F32)
            ).astype(BF16)

    def finished(kind, group, index):
        start, _ = piece_rows(kind, group, index)
        give(kind, group, start)

    def spread_own(kind, group):
        @pl.when(z < line - 1)
        def _():
            spread_copy(kind, group, 0, 0, z).start()

        @pl.when(z > 0)
        def _():
            spread_copy(kind, group, 1, 0, z).start()

        finished(kind, group, z)

    def spreading(kind, group, hop):
        for direction in range(2):
            index = z - hop if direction == 0 else z + hop
            onward = z < line - 1 if direction == 0 else z > 0
            exists = index >= 0 if direction == 0 else index < line

            @pl.when(exists)
            def _():
                spread_copy(kind, group, direction, hop - 1, index).wait_recv()

                @pl.when(onward)
                def _():
                    spread_copy(kind, group, direction, hop, index).start()

                finished(kind, group, index)

    def over(group):
        start = group * sizes[0] + (1 - y) * (sizes[0] // 2)
        return pltpu.make_async_remote_copy(
            src_ref=mine.at[pl.ds(pl.multiple_of(start, pieces[0]), sizes[0] // 2)],
            dst_ref=pair_landing.at[group],
            send_sem=y_send.at[group],
            recv_sem=y_sem.at[group],
            device_id=across,
            device_id_type=MESH,
        )

    def swap(group):
        _, rows = piece_rows(1, group, z)
        return pltpu.make_async_remote_copy(
            src_ref=mine.at[rows],
            dst_ref=cross_landing.at[group],
            send_sem=y_send.at[counts[0] + group],
            recv_sem=y_sem.at[counts[0] + group],
            device_id=across,
            device_id_type=MESH,
        )

    def event0(group, turn):
        @pl.when(turn == 0)
        def _():
            over(group).start()

        @pl.when(turn == 1)
        def _():
            over(group).wait_recv()

            def add(index, _):
                _, rows = piece_rows(0, group, index)
                local = pl.ds(pl.multiple_of(index * pieces[0], pieces[0]), pieces[0])
                mine[rows, :] = (
                    mine[rows, :].astype(F32) + pair_landing[group, local, :].astype(F32)
                ).astype(BF16)
                return 0

            lax.fori_loop(0, line, add, 0)

        @pl.when((turn >= 1) & (turn <= line))
        def _():
            passing(0, group, turn - 1)

        @pl.when(turn == line)
        def _():
            arrived(0, group)
            spread_own(0, group)

        @pl.when(turn > line)
        def _():
            spreading(0, group, turn - line)

    def event1(group, turn):
        @pl.when(turn < line)
        def _():
            passing(1, group, turn)

        @pl.when(turn == line - 1)
        def _():
            arrived(1, group)
            swap(group).start()

        @pl.when(turn == line)
        def _():
            swap(group).wait()
            _, rows = piece_rows(1, group, z)
            mine[rows, :] = (
                mine[rows, :].astype(F32) + cross_landing[group].astype(F32)
            ).astype(BF16)
            spread_own(1, group)

        @pl.when(turn > line)
        def _():
            spreading(1, group, turn - line)

    spare = firsts[1] + counts[1] * sizes[1] - BLOCKS * half
    if spare:
        mine[pl.ds(BLOCKS * half, spare), :] = jnp.zeros((spare, channels), BF16)
    order = [(COMPUTE, 0, 0)]
    for kind, group, turn in event_order(line, half):
        if kind == COMPUTE:
            order += [(COMPUTE, group + 1, 0)] * (group + 1 < BLOCKS) + [(COMPUTE, group, 1)]
        else:
            order.append((kind, group, turn))
    codes = [kind * 1024 + group * 64 + turn for kind, group, turn in order]
    steps = len(codes)
    words = tuple(a + 4096 * b for a, b in zip(codes[::2], (codes + [0])[1::2], strict=True))

    def take(index, _):
        word = lookup(index // 2, words)
        code = jnp.where(index % 2 == 0, word % 4096, word // 4096)
        kind, group, turn = code // 1024, code // 64 % 16, code % 64

        @pl.when(kind == COMPUTE)
        def _():
            pl.when(turn == 0)(lambda: for_partner(group))
            pl.when(turn == 1)(lambda: for_me(group))

            @pl.when((turn == 1) & (group == BLOCKS // 2))
            def _():
                own_small.wait()
                small_pair.wait()
                small[0] = small[0] + small[1]
                lax.fori_loop(1, count, small_start, 0)

        pl.when(kind == 0)(lambda: event0(group, turn))
        pl.when(kind == 1)(lambda: event1(group, turn))
        return 0

    lax.fori_loop(0, steps, take, 0)
    small[0] = lax.fori_loop(1, count, small_add, small[0])
    total_copy = pltpu.make_async_copy(small.at[0], total_hbm, small_sem.at[0])
    total_copy.start()

    def pair_done(block, _):
        pair_copy(block).wait_send()
        return 0

    def over_done(group, _):
        over(group).wait_send()
        return 0

    lax.fori_loop(0, BLOCKS, pair_done, 0)
    lax.fori_loop(0, counts[0], over_done, 0)
    for kind in range(2):

        def group_done(group, _):
            def step_done(step, _):
                for direction in range(2):
                    behind = z if direction == 0 else line - 1 - z

                    @pl.when(step < line - 1 - behind)
                    def _():
                        sum_copy(kind, group, direction, step).wait_send()

                    @pl.when((step <= behind) & (behind < line - 1))
                    def _():
                        spread_copy(kind, group, direction, step, 0).wait_send()

                return 0

            return lax.fori_loop(0, line - 1, step_done, 0)

        lax.fori_loop(0, counts[kind], group_done, 0)

    def taken(rows, sem):
        if rows:
            ref = mine.at[pl.ds(0, rows)]
            pltpu.make_async_copy(ref, ref, sem.at[0]).wait()

    paired = [PLACES[block] < PAIRED for block in range(BLOCKS)]
    whole = [half // 2 if pair else half for pair in paired]
    by_kind = (range(C_BLOCKS, BLOCKS), range(C_BLOCKS))
    for own in range(2):

        @pl.when(core == own)
        def _():
            local = sum(whole[block] for block in by_kind[own])
            crossed = sum(half // 2 for block in range(BLOCKS) if paired[block])
            other = sum(whole[block] for block in by_kind[1 - own])
            taken(local, give_sem)
            taken(other + crossed, give_send)
            taken(len(by_kind[own]) * channels - local, give_recv)

    total_copy.wait()


def reduced(count, kept, sums):
    length, channels = kept.shape[1:]
    half = channels // 2
    line = count // 2
    pieces, sizes, counts = reduce_plan(line, half)
    anywhere = pl.BlockSpec(memory_space=pl.ANY)
    dma = pltpu.SemaphoreType.DMA
    hops = [dma((counts[kind], 2, line - 1)) for kind in range(2)]
    landings = [pltpu.VMEM((counts[kind], line - 1, pieces[kind], channels), BF16) for kind in range(2)]
    return pl.pallas_call(
        functools.partial(reduce_kernel, count, length, channels),
        out_shape=(
            jax.ShapeDtypeStruct((channels, 4 * channels), BF16),
            jax.ShapeDtypeStruct(((C_BLOCKS - 4) * channels, channels), BF16),
            jax.ShapeDtypeStruct((8, channels), F32),
        ),
        in_specs=[anywhere] * 2,
        out_specs=(anywhere,) * 3,
        scratch_shapes=[
            pltpu.VMEM((KEPT, length, channels), BF16),
            pltpu.VMEM((counts[0] * sizes[0] + counts[1] * sizes[1], channels), BF16),
            pltpu.VMEM((BLOCKS * half, channels), BF16),
            pltpu.VMEM((counts[0], sizes[0] // 2, channels), BF16),
            pltpu.VMEM((counts[1], pieces[1], channels), BF16),
            landings[0],
            landings[0],
            landings[1],
            landings[1],
            pltpu.VMEM((count + 1, 8, channels), F32),
            dma((KEPT,)),
            dma((BLOCKS,)),
            dma((BLOCKS,)),
            dma((sum(counts),)),
            dma((sum(counts),)),
            hops[0],
            hops[0],
            hops[1],
            hops[1],
            hops[0],
            hops[0],
            hops[1],
            hops[1],
            dma((1,)),
            dma((1,)),
            dma((1,)),
            dma((count + 1,)),
            dma((count + 1,)),
        ],
        compiler_params=pltpu.CompilerParams(
            collective_id=1, has_side_effects=True, vmem_limit_bytes=VMEM_BYTES
        ),
    )(kept, sums)


def finish_kernel(
    steps,
    in_short,
    out_short,
    outs_in,
    grads_in,
    fin,
    total,
    in_wide,
    out_wide,
    outs,
    grads,
    states,
    normed,
    gain,
    bias,
    rates,
    wkv,
):
    holds_channel_mix = lax.axis_index("section") % 2 == 1
    step = pl.program_id(0)

    @pl.when(step == 0)
    def _():
        for micro in range(2):
            normed[0, micro] = fin[micro, 0:1]
            for row in range(2):
                states[0, row, micro] = fin[micro, 1 + row : 2 + row]
        gain[...] = total[GAIN : GAIN + 1]
        bias[...] = total[BIAS : BIAS + 1]
        for row in range(3):
            rates[row] = total[RATES + row : RATES + row + 1]
        wkv[0] = total[DECAY : DECAY + 2]

    in_wide[...] = in_short[...].astype(F32)
    out_wide[...] = jnp.where(holds_channel_mix, out_short[...].astype(F32), 0.0)
    outs[0, :, 0] = outs_in[...]
    grads[0, :, 0] = grads_in[...]


def finished_outputs(in_short, out_short, outs, grads, fin, total):
    steps = 8
    length, channels = outs.shape[1:]
    whole = pl.BlockSpec(memory_space=pltpu.VMEM)
    kept = pl.BlockSpec((2, length // steps, channels), lambda i: (0, i, 0))
    placed = pl.BlockSpec((1, 2, 1, length // steps, channels), lambda i: (0, 0, 0, i, 0))

    def spec(array):
        rows, columns = array.shape
        return pl.BlockSpec((rows // steps, columns), lambda i: (i, 0))

    def shape(*sizes, dtype=F32):
        return jax.ShapeDtypeStruct(sizes, dtype)

    in_wide, out_wide, *rest = pl.pallas_call(
        functools.partial(finish_kernel, steps),
        grid=(steps,),
        out_shape=(
            shape(*in_short.shape),
            shape(*out_short.shape),
            shape(1, 2, 1, length, channels, dtype=BF16),
            shape(1, 2, 1, length, channels, dtype=BF16),
            shape(1, 2, 2, 1, channels),
            shape(1, 2, 1, channels),
            shape(1, channels),
            shape(1, channels),
            shape(3, 1, channels),
            shape(1, 2, channels),
        ),
        in_specs=[spec(in_short), spec(out_short), kept, kept, whole, whole],
        out_specs=(spec(in_short), spec(out_short), placed, placed) + (whole,) * 6,
        compiler_params=pltpu.CompilerParams(vmem_limit_bytes=VMEM_BYTES),
    )(in_short, out_short, outs, grads, fin, total)
    *rest, rates, wkv = rest
    return in_wide, out_wide, *rest, jnp.swapaxes(rates, 0, 1), wkv


def shards(
    block_input,
    carried_state,
    output_cotangent,
    in_weight,
    out_weight,
    norm_gain,
    norm_bias,
    mix_rates,
    wkv_params,
):
    sections = lax.axis_size("section")
    outs, grads, fin, sums, kept = chain(
        sections,
        block_input,
        output_cotangent,
        in_weight,
        out_weight,
        norm_gain,
        norm_bias,
        jnp.swapaxes(mix_rates, 0, 1),
        wkv_params,
        carried_state,
    )
    in_short, out_short, total = reduced(lax.axis_size("dp"), kept, sums)
    in_grad, out_grad, outs, grads, states, normed, gain, bias, rates, wkv = finished_outputs(
        in_short, out_short, outs, grads, fin, total
    )
    return outs, states, normed, grads, in_grad[None], out_grad[None], gain, bias, rates, wkv


def solution(mesh):
    return jax.shard_map(
        shards,
        mesh=mesh,
        in_specs=(
            P(None, "dp", None, None),
            P("section", None, None, "dp", None),
            P(None, "dp", None, None),
            P("section", None, None),
            P("section", None, None),
            P("section", None),
            P("section", None),
            P("section", None, None),
            P("section", None, None),
        ),
        out_specs=(
            P("section", None, "dp", None, None),
            P("section", None, None, "dp", None),
            P("section", None, "dp", None),
            P("section", None, "dp", None, None),
            P("section", None, None),
            P("section", None, None),
            P("section", None),
            P("section", None),
            P("section", None, None),
            P("section", None, None),
        ),
        check_vma=False,
    )
```

```python
import functools

import jax
import jax.numpy as jnp
from jax import lax
from jax.experimental import pallas as pl
from jax.experimental.pallas import tpu as pltpu
from jax.sharding import PartitionSpec as P

MESH = pl.DeviceIdType.MESH
F32 = jnp.float32
BF16 = jnp.bfloat16
CHUNK = 256
ROWS = 32
UNROLL = 4
VMEM_BYTES = (64 << 20) - (128 << 10)

T_MIX0, T_MIX2, T_MIX1, T_GATED, C_MIX0, C_MIX1 = 0, 1, 2, 3, 4, 5
EARLY = 6
T_DK, T_DV, T_DQ, T_G, C_DKV, C_DQ, C_HID, C_DPRE = 0, 1, 2, 3, 4, 5, 6, 10
LATE = 14
GAIN, BIAS, RATES, DECAY, BONUS = 0, 1, 2, 5, 6


def nn(left, right):
    return jnp.dot(left, right, preferred_element_type=F32)


def nt(left, right):
    return lax.dot_general(left, right, (((1,), (1,)), ((), ())), preferred_element_type=F32)


def tn(left, right):
    return lax.dot_general(left, right, (((0,), (0,)), ((), ())), preferred_element_type=F32)


class Stack:
    def __init__(self, buffer, start, *heights):
        self.buffer, self.start, self.heights = buffer, start, heights

    @property
    def at(self):
        return Places(self)

    def __getitem__(self, index):
        return self.at[index][...]


class Places:
    def __init__(self, stack):
        self.stack = stack

    def __getitem__(self, index):
        index = index if isinstance(index, tuple) else (index,)
        start, height = self.stack.start, self.stack.heights[-1]
        for place, tall in zip(index, self.stack.heights, strict=True):
            start = start + place * tall
        if not isinstance(start, int):
            start = pl.multiple_of(start, 16)
        return self.stack.buffer.at[pl.ds(start, height)]


def folded(rows):
    total = rows[0:8]
    for start in range(8, rows.shape[0], 8):
        total = total + rows[start : start + 8]
    return total


def chain_kernel(
    sections,
    length,
    channels,
    hidden_blocks,
    count,
    x_hbm,
    cot_hbm,
    w_in_hbm,
    w_out_hbm,
    gain_hbm,
    bias_hbm,
    rates_hbm,
    wkv_hbm,
    state_hbm,
    outs_hbm,
    grads_hbm,
    fin_hbm,
    early_hbm,
    in_hbm,
    out_hbm,
    total_hbm,
    pool,
    early,
    kept,
    states,
    upstream,
    wide,
    pairs,
    tables,
    triangles,
    gains,
    biases,
    rates,
    wkvs,
    starts,
    previous,
    carry,
    carry_next,
    fin,
    sums,
    totals,
    weight_sem,
    weight_send,
    small_sem,
    small_send,
    entry_sem,
    entry_send,
    up_sem,
    up_send,
    out_sem,
    out_send,
    out_recv,
    early_sem,
    *reducing,
):
    section = lax.axis_index("section")
    dp_index = lax.axis_index("dp")
    core = section % 2
    stage = section // 2
    stages = sections // 2
    partner = {"section": section + 1 - 2 * core}
    chunks = length // CHUNK
    blocks = CHUNK // ROWS
    time_blocks = 4
    last_stage = stage == stages - 1
    weights = Stack(pool, 0, channels)
    after_weights = (9 + hidden_blocks) * channels
    entry = pool.at[pl.ds(after_weights, length)]
    hs = Stack(pool, after_weights + length, length)
    mid, top = hs.at[0], hs.at[1]

    barrier = pltpu.get_barrier_semaphore()
    across = {"dp": dp_index + 1 - 2 * (dp_index % 2)}
    for device in (partner, partner | across):
        pl.semaphore_signal(barrier, inc=1, device_id=device, device_id_type=MESH)

    def greet(offset, _):
        peer = {"dp": lax.rem(dp_index + offset, count)}
        pl.semaphore_signal(barrier, inc=1, device_id=peer, device_id_type=MESH)
        return 0

    lax.fori_loop(1, count, greet, 0)

    @pl.when(stage > 0)
    def _():
        pl.semaphore_signal(
            barrier, inc=1, device_id={"section": section - 2}, device_id_type=MESH
        )

    @pl.when(stage < stages - 1)
    def _():
        pl.semaphore_signal(
            barrier, inc=1, device_id={"section": section + 2}, device_id_type=MESH
        )

    def entry_copy(chunk):
        rows = pl.ds(chunk * CHUNK, CHUNK)
        return pltpu.make_async_copy(
            x_hbm.at[core, 0, rows], entry.at[rows], entry_sem.at[chunk]
        )

    def up_copy(chunk):
        rows = pl.ds(chunk * CHUNK, CHUNK)
        return pltpu.make_async_copy(
            cot_hbm.at[core, 0, rows], upstream.at[rows], up_sem.at[chunk]
        )

    @pl.when(stage == 0)
    def _():
        for chunk in range(chunks):
            entry_copy(chunk).start()

    @pl.when(last_stage)
    def _():
        for chunk in range(chunks):
            up_copy(chunk).start()

    small_pairs = (
        (gain_hbm, gains.at[core]),
        (bias_hbm, biases.at[core]),
        (rates_hbm, rates.at[core]),
        (wkv_hbm.at[0], wkvs.at[core]),
        (state_hbm.at[0], starts.at[core]),
    )
    small_copies = [
        pltpu.make_async_copy(source, target, small_sem.at[0, at])
        for at, (source, target) in enumerate(small_pairs)
    ]
    for copy in small_copies:
        copy.start()

    def in_block(index):
        return w_in_hbm.at[0, :, pl.ds(index * channels, channels)]

    def out_block(index):
        return w_out_hbm.at[0, pl.ds(index * channels, channels), :]

    for index in range(4):
        slot = core * time_blocks + index
        pltpu.make_async_copy(in_block(index), weights.at[slot], weight_sem.at[slot]).start()

    @pl.when(core == 1)
    def _():
        for index in range(hidden_blocks + 1):
            slot = 8 + index
            pltpu.make_async_copy(
                out_block(index), weights.at[slot], weight_sem.at[slot]
            ).start()

    has_previous = jnp.where(stage > 0, 1, 0)
    has_next = jnp.where(stage < stages - 1, 1, 0)
    pl.semaphore_wait(barrier, 1 + count + has_previous + has_next)

    small_remotes = [
        pltpu.make_async_remote_copy(
            src_ref=source,
            dst_ref=target,
            send_sem=small_send.at[at],
            recv_sem=small_sem.at[1, at],
            device_id=partner,
            device_id_type=MESH,
        )
        for at, (source, target) in enumerate(small_pairs)
    ]

    def in_remote(index):
        slot = core * time_blocks + index
        return pltpu.make_async_remote_copy(
            src_ref=in_block(index),
            dst_ref=weights.at[slot],
            send_sem=weight_send.at[slot],
            recv_sem=weight_sem.at[slot],
            device_id=partner,
            device_id_type=MESH,
        )

    def out_remote(index):
        slot = 8 + index
        return pltpu.make_async_remote_copy(
            src_ref=out_block(index),
            dst_ref=weights.at[slot],
            send_sem=weight_send.at[slot],
            recv_sem=weight_sem.at[slot],
            device_id=partner,
            device_id_type=MESH,
        )

    for copy in small_remotes:
        copy.start()
    for index in range(4):
        in_remote(index).start()

    @pl.when(core == 1)
    def _():
        for index in (hidden_blocks, *range(hidden_blocks)):
            out_remote(index).start()

    row_at = lax.broadcasted_iota(jnp.int32, (CHUNK, 2 * CHUNK), 0)
    column_at = lax.broadcasted_iota(jnp.int32, (CHUNK, 2 * CHUNK), 1)
    column_at = jnp.where(column_at >= CHUNK, column_at - CHUNK, column_at)
    triangles[0] = jnp.where(row_at > column_at, 1.0, 0.0).astype(BF16)
    triangles[1] = jnp.where(row_at < column_at, 1.0, 0.0).astype(BF16)
    sums[...] = jnp.zeros_like(sums)
    fin[...] = jnp.zeros_like(fin)

    for copy in small_copies:
        copy.wait()
    for copy in small_remotes:
        copy.wait_recv()

    rate = jnp.exp(wkvs[0, 0:1, :])
    step = jnp.exp(-rate)
    lift = jnp.exp(wkvs[0, 1:2, :])

    def table_rows(index, _):
        start = pl.multiple_of(index * ROWS, ROWS)
        place = (lax.broadcasted_iota(jnp.int32, (ROWS, channels), 0) + start).astype(F32)
        tables[0, pl.ds(start, ROWS), :] = jnp.exp(-(CHUNK - 1.0 - place) * rate)
        tables[1, pl.ds(start, ROWS), :] = jnp.exp(-place * rate)
        return 0

    lax.fori_loop(0, blocks, table_rows, 0)

    for row in range(3):
        carry[row : row + 1] = starts[0, row, core]
    carry[3:4] = starts[1, 0, core]

    def weight_wait(slot):
        pltpu.make_async_copy(weights.at[slot], weights.at[slot], weight_sem.at[slot]).wait()

    def stats(tokens):
        center = tokens - jnp.mean(tokens, axis=-1, keepdims=True)
        spread = jnp.mean(center * center, axis=-1, keepdims=True)
        root = lax.rsqrt(spread + 1e-05)
        return center * root, root

    row_index = lax.broadcasted_iota(jnp.int32, (ROWS, channels), 0)

    def token_mix(kind, source, base, side, slots, carry_row):
        gain, bias = gains[kind], biases[kind]

        def body(index, before):
            start = pl.multiple_of(base + index * ROWS, ROWS)
            rows = pl.ds(start, ROWS)
            unit, _ = stats(source[rows, :].astype(F32))
            normed = unit * gain + bias
            previous[kind, pl.ds(start // ROWS, 1), :] = before
            shifted = jnp.where(
                row_index == 0, jnp.broadcast_to(before, normed.shape), pltpu.roll(normed, 1, 0)
            )
            gap = normed - shifted
            for rate_row, slot in slots:
                early[side, slot, pl.ds(pl.multiple_of(index * ROWS, ROWS), ROWS), :] = (
                    shifted + gap * rates[kind, rate_row]
                ).astype(BF16)
            return normed[ROWS - 1 : ROWS, :]

        carry[carry_row : carry_row + 1] = lax.fori_loop(
            0, blocks, body, carry[carry_row : carry_row + 1], unroll=UNROLL
        )

    def early_copy(chunk):
        rows = pl.ds(pl.multiple_of(chunk * CHUNK, CHUNK), CHUNK)
        side = chunk % 2
        return pltpu.make_async_copy(
            early.at[side], early_hbm.at[:, rows], early_sem.at[side]
        )

    def forward_chunk(chunk, _):
        base = pl.multiple_of(chunk * CHUNK, CHUNK)
        rows = pl.ds(base, CHUNK)
        side = chunk % 2

        @pl.when(chunk >= 2)
        def _():
            early_copy(chunk - 2).wait()

        pltpu.make_async_copy(entry.at[rows], entry.at[rows], entry_sem.at[chunk]).wait()

        token_mix(0, entry, base, side, ((0, T_MIX0), (2, T_MIX2), (1, T_MIX1)), 0)

        for slot in range(3):

            @pl.when(chunk == 0)
            def _():
                weight_wait(slot)

            wide[slot] = nn(early[side, slot], weights[slot])

        def weighted(index, _):
            start = pl.multiple_of(index * ROWS, ROWS)
            local = pl.ds(start, ROWS)
            whole = pl.ds(pl.multiple_of(base + start, ROWS), ROWS)
            value = wide[1, local, :]
            power = jnp.exp(wide[0, local, :])
            wide[0, local, :] = power
            scaled = power * tables[0, local, :]
            pairs[local, pl.ds(0, channels)] = (scaled * value).astype(BF16)
            pairs[local, pl.ds(channels, channels)] = scaled.astype(BF16)
            kept[T_DK, whole, :] = power.astype(BF16)
            kept[T_DV, whole, :] = value.astype(BF16)
            return 0

        lax.fori_loop(0, blocks, weighted, 0)
        wide[3] = nn(triangles[0, :, pl.ds(0, CHUNK)], pairs[pl.ds(0, CHUNK), pl.ds(0, channels)])
        wide[4] = nn(
            triangles[0, :, pl.ds(0, CHUNK)], pairs[pl.ds(0, CHUNK), pl.ds(channels, channels)]
        )
        upper, lower = carry[1:2], carry[2:3]

        def averaged(index, _):
            start = pl.multiple_of(index * ROWS, ROWS)
            local = pl.ds(start, ROWS)
            whole = pl.ds(pl.multiple_of(base + start, ROWS), ROWS)
            place = (row_index + start).astype(F32)
            grown = jnp.exp((CHUNK - place) * rate)
            faded = tables[1, local, :]
            power, value = wide[0, local, :], wide[1, local, :]
            before_upper = grown * wide[3, local, :] + faded * upper
            before_lower = grown * wide[4, local, :] + faded * lower
            now = power * lift
            average = (before_upper + now * value) / (before_lower + now)
            gate = jax.nn.sigmoid(wide[2, local, :])
            states[0, whole, :] = before_upper
            states[1, whole, :] = before_lower
            kept[T_DQ, whole, :] = gate.astype(BF16)
            early[side, T_GATED, local, :] = (gate * average).astype(BF16)
            tail = slice(ROWS - 8, ROWS)
            after_upper = step * before_upper[tail] + power[tail] * value[tail]
            after_lower = step * before_lower[tail] + power[tail]
            carry_next[0:1] = after_upper[7:8]
            carry_next[1:2] = after_lower[7:8]
            return 0

        lax.fori_loop(0, blocks, averaged, 0)
        carry[1:3] = carry_next[0:2]

        @pl.when(chunk == 0)
        def _():
            weight_wait(3)

        mid[rows, :] = (
            entry[rows, :].astype(F32) + nn(early[side, T_GATED], weights[3])
        ).astype(BF16)

        token_mix(1, mid, base, side, ((0, C_MIX0), (1, C_MIX1)), 3)

        for index in range(hidden_blocks):

            @pl.when(chunk == 0)
            def _():
                weight_wait(4 + index)

            pre = nn(early[side, C_MIX0], weights[4 + index])
            kept[C_HID + index, rows, :] = jnp.square(jnp.maximum(pre, 0.0)).astype(BF16)

        @pl.when(chunk == 0)
        def _():
            weight_wait(8 + hidden_blocks)

        early_copy(chunk).start()
        wide[1] = nn(early[side, C_MIX1], weights[8 + hidden_blocks])

        @pl.when(chunk == 0)
        def _():
            for index in range(hidden_blocks):
                weight_wait(8 + index)

        total = nn(kept[C_HID, rows, :], weights[8])
        for index in range(1, hidden_blocks):
            total = total + nn(kept[C_HID + index, rows, :], weights[8 + index])
        wide[0] = total

        def joined(index, _):
            start = pl.multiple_of(index * ROWS, ROWS)
            local = pl.ds(start, ROWS)
            whole = pl.ds(pl.multiple_of(base + start, ROWS), ROWS)
            gate = jax.nn.sigmoid(wide[1, local, :])
            value = wide[0, local, :]
            kept[C_DKV, whole, :] = gate.astype(BF16)
            kept[C_DQ, whole, :] = value.astype(BF16)
            top[whole, :] = (mid[whole, :].astype(F32) + gate * value).astype(BF16)
            return 0

        lax.fori_loop(0, blocks, joined, 0)

        @pl.when(stage < stages - 1)
        def _():
            entry_remote(chunk).start()

        return 0

    def entry_remote(chunk):
        rows = pl.ds(pl.multiple_of(chunk * CHUNK, CHUNK), CHUNK)
        return pltpu.make_async_remote_copy(
            src_ref=top.at[rows],
            dst_ref=entry.at[rows],
            send_sem=entry_send.at[chunk],
            recv_sem=entry_sem.at[chunk],
            device_id={"section": section + 2},
            device_id_type=MESH,
        )

    def up_remote(chunk):
        rows = pl.ds(pl.multiple_of(chunk * CHUNK, CHUNK), CHUNK)
        return pltpu.make_async_remote_copy(
            src_ref=upstream.at[rows],
            dst_ref=upstream.at[rows],
            send_sem=up_send.at[chunk],
            recv_sem=up_sem.at[chunk],
            device_id={"section": section - 2},
            device_id_type=MESH,
        )

    lax.fori_loop(0, chunks, forward_chunk, 0)
    early_copy(chunks - 2).wait()
    early_copy(chunks - 1).wait()

    def mix_back(side, chunk):
        return pltpu.make_async_copy(
            early_hbm.at[C_MIX0 + side, pl.ds(chunk * CHUNK, CHUNK)],
            early.at[side, chunk],
            back_sem.at[side, chunk],
        )

    back_sem, reducing = reducing[0], reducing[1:]
    for side in range(2):
        for chunk in range(chunks):
            mix_back(side, chunk).start()

    fin[0, 0:1] = carry[0:1]
    fin[0, 1:3] = carry[1:3]
    fin[1, 0:1] = carry[3:4]

    def to_owner(index, own_src, other_src, dst):
        own = pltpu.make_async_copy(own_src, dst, out_sem.at[index])
        other = pltpu.make_async_remote_copy(
            src_ref=other_src,
            dst_ref=dst,
            send_sem=out_send.at[index],
            recv_sem=out_recv.at[index],
            device_id=partner,
            device_id_type=MESH,
        )
        return own, other

    outs_copies = to_owner(0, hs.at[core], hs.at[1 - core], outs_hbm.at[core])
    fin_copies = to_owner(1, fin.at[core], fin.at[1 - core], fin_hbm.at[core])
    for copy in outs_copies + fin_copies:
        copy.start()

    carry[0:4] = jnp.zeros((4, channels), F32)

    def norm_back(kind, source, base, mixes, above, target, carry_row):
        gain, bias = gains[kind], biases[kind]

        def body(index, after):
            back = blocks - 1 - index
            local = pl.ds(pl.multiple_of(back * ROWS, ROWS), ROWS)
            start = pl.multiple_of(base + back * ROWS, ROWS)
            rows = pl.ds(start, ROWS)
            unit, root = stats(source[rows, :].astype(F32))
            normed = unit * gain + bias
            before = previous[kind, pl.ds(start // ROWS, 1), :]
            shifted = jnp.where(
                row_index == 0, jnp.broadcast_to(before, normed.shape), pltpu.roll(normed, 1, 0)
            )
            gap = normed - shifted
            straight = jnp.zeros_like(normed)
            total = jnp.zeros_like(normed)
            for rate_row, slot in mixes:
                mix = wide[slot, local, :]
                straight = straight + mix * rates[kind, rate_row]
                total = total + mix
                sums[kind, RATES + rate_row] += folded(mix * gap)
            late = total - straight
            moved = jnp.where(
                row_index == ROWS - 1,
                jnp.broadcast_to(after, late.shape),
                pltpu.roll(late, ROWS - 1, 0),
            )
            d_normed = straight + moved
            sums[kind, GAIN] += folded(d_normed * unit)
            sums[kind, BIAS] += folded(d_normed)
            d_unit = d_normed * gain
            d_tokens = (
                d_unit
                - jnp.mean(d_unit, axis=-1, keepdims=True)
                - unit * jnp.mean(d_unit * unit, axis=-1, keepdims=True)
            ) * root
            target[rows, :] = (above[rows, :].astype(F32) + d_tokens).astype(BF16)
            return late[0:1, :]

        carry[carry_row : carry_row + 1] = lax.fori_loop(
            0, blocks, body, carry[carry_row : carry_row + 1], unroll=UNROLL
        )

    def grad_copies(chunk, kind):
        rows = pl.ds(pl.multiple_of(chunk * CHUNK, CHUNK), CHUNK)
        sources = (upstream.at[rows], kept.at[T_G, rows])
        return to_owner(
            2 + chunk, sources[kind], sources[1 - kind], grads_hbm.at[core, rows]
        )

    def backward_chunk(turn, _):
        chunk = chunks - 1 - turn
        base = pl.multiple_of(chunk * CHUNK, CHUNK)
        rows = pl.ds(base, CHUNK)
        pltpu.make_async_copy(upstream.at[rows], upstream.at[rows], up_sem.at[chunk]).wait()

        def split(index, _):
            whole = pl.ds(pl.multiple_of(base + index * ROWS, ROWS), ROWS)
            above = upstream[whole, :].astype(F32)
            gate = kept[C_DKV, whole, :].astype(F32)
            value = kept[C_DQ, whole, :].astype(F32)
            d_value = above * gate
            kept[C_DKV, whole, :] = d_value.astype(BF16)
            kept[C_DQ, whole, :] = (d_value * value * (1.0 - gate)).astype(BF16)
            return 0

        lax.fori_loop(0, blocks, split, 0)

        for index in range(hidden_blocks):
            d_hidden = nt(kept[C_DKV, rows, :], weights[8 + index])
            slope = jnp.sqrt(kept[C_HID + index, rows, :].astype(F32))
            kept[C_DPRE + index, rows, :] = (d_hidden * (2.0 * slope)).astype(BF16)
        total = nt(kept[C_DPRE, rows, :], weights[4])
        for index in range(1, hidden_blocks):
            total = total + nt(kept[C_DPRE + index, rows, :], weights[4 + index])
        wide[0] = total
        wide[1] = nt(kept[C_DQ, rows, :], weights[8 + hidden_blocks])
        norm_back(1, mid, base, ((0, 0), (1, 1)), upstream, kept.at[T_G], 3)

        wide[0] = nt(kept[T_G, rows, :], weights[3])

        def inputs(index, _):
            start = pl.multiple_of(index * ROWS, ROWS)
            local = pl.ds(start, ROWS)
            whole = pl.ds(pl.multiple_of(base + start, ROWS), ROWS)
            power = kept[T_DK, whole, :].astype(F32)
            value = kept[T_DV, whole, :].astype(F32)
            gate = kept[T_DQ, whole, :].astype(F32)
            now = power * lift
            inverse = 1.0 / (states[1, whole, :] + now)
            average = (states[0, whole, :] + now * value) * inverse
            d_average = wide[0, local, :] * gate
            kept[T_DQ, whole, :] = (d_average * average * (1.0 - gate)).astype(BF16)
            unit = d_average * inverse
            wide[1, local, :] = unit
            wide[2, local, :] = average
            scaled = unit * tables[1, local, :]
            for column, term in ((0, scaled), (channels, -scaled * average)):
                high = term.astype(BF16)
                pairs[local, pl.ds(column, channels)] = high
                pairs[pl.ds(pl.multiple_of(CHUNK + start, ROWS), ROWS), pl.ds(column, channels)] = (
                    term - high.astype(F32)
                ).astype(BF16)
            return 0

        lax.fori_loop(0, blocks, inputs, 0)
        wide[3] = nn(triangles[1], pairs[:, pl.ds(0, channels)])
        wide[4] = nn(triangles[1], pairs[:, pl.ds(channels, channels)])
        alpha_after, beta_after = carry[1:2], carry[2:3]

        def outputs(index, _):
            start = pl.multiple_of((blocks - 1 - index) * ROWS, ROWS)
            local = pl.ds(start, ROWS)
            whole = pl.ds(pl.multiple_of(base + start, ROWS), ROWS)
            place = (row_index + start).astype(F32)
            grown = jnp.exp((place + 1.0) * rate)
            faded = tables[0, local, :]
            alpha = grown * wide[3, local, :] + faded * alpha_after
            beta = grown * wide[4, local, :] + faded * beta_after
            unit, average = wide[1, local, :], wide[2, local, :]
            power = kept[T_DK, whole, :].astype(F32)
            value = kept[T_DV, whole, :].astype(F32)
            weighed = unit * (power * lift)
            own = weighed * (value - average)
            kept[T_DK, whole, :] = (own + power * (alpha * value + beta)).astype(BF16)
            kept[T_DV, whole, :] = (weighed + power * alpha).astype(BF16)
            sums[0, BONUS] += folded(own)
            sums[0, DECAY] += folded(
                alpha * states[0, whole, :] + beta * states[1, whole, :]
            )
            carry_next[0:1] = unit[0:1] + step * alpha[0:1]
            carry_next[1:2] = step * beta[0:1] - unit[0:1] * average[0:1]
            return 0

        lax.fori_loop(0, blocks, outputs, 0)
        carry[1:3] = carry_next[0:2]
        wide[0] = nt(kept[T_DK, rows, :], weights[0])
        wide[1] = nt(kept[T_DQ, rows, :], weights[2])
        wide[2] = nt(kept[T_DV, rows, :], weights[1])
        norm_back(
            0, entry, base, ((0, 0), (1, 1), (2, 2)), kept.at[T_G], upstream, 0
        )

        @pl.when(stage > 0)
        def _():
            up_remote(chunk).start()

        for kind in range(2):

            @pl.when(core == kind)
            def _():
                for copy in grad_copies(chunk, kind):
                    copy.start()

        return 0

    lax.fori_loop(0, chunks, backward_chunk, 0)

    sums[0, DECAY] = sums[0, DECAY] * (-rate * step)
    for kind in range(2):
        for row in range(7):
            totals[kind, row : row + 1] = jnp.sum(sums[kind, row], axis=0, keepdims=True)
        totals[kind, 7:8] = jnp.zeros((1, channels), F32)

    for copy in outs_copies:
        copy.wait()

    @pl.when(stage < stages - 1)
    def _():
        for chunk in range(chunks):
            entry_remote(chunk).wait_send()

    reduce_phase(
        count, channels, pool, early, kept, early_hbm, totals, mix_back, in_hbm, out_hbm, total_hbm, *reducing
    )

    for copy in fin_copies:
        copy.wait()
    for chunk in range(chunks):
        for copy in grad_copies(chunk, 0):
            copy.wait()
    for copy in small_remotes:
        copy.wait_send()
    for index in range(4):
        in_remote(index).wait_send()

    @pl.when(core == 1)
    def _():
        for index in range(hidden_blocks + 1):
            out_remote(index).wait_send()

    @pl.when(stage > 0)
    def _():
        for chunk in range(chunks):
            up_remote(chunk).wait_send()


C_BLOCKS = 9
T_BLOCKS = 4
BLOCKS = C_BLOCKS + T_BLOCKS
PLACES = (8, 9, 0, 1, 2, 10, 3, 11, 4, 5, 6, 12, 7)
PAIRED = 8


def lookup(index, table):
    value = jnp.int32(table[0])
    for at, entry in enumerate(table[1:], 1):
        value = jnp.where(index == at, entry, value)
    return value


def reduce_plan(line, half):
    pieces = (max(16, half // (2 * line)), max(16, half // line))
    sizes = (2 * line * pieces[0], line * pieces[1])
    counts = (-(-PAIRED * half // sizes[0]), -(-(BLOCKS - PAIRED) * half // sizes[1]))
    return pieces, sizes, counts


def ready_times(first, size, count, half):
    made = {place: time for time, place in enumerate(PLACES)}
    times = []
    for group in range(count):
        begin, end = first + group * size, first + (group + 1) * size
        times.append(
            max(made[place] for place in range(BLOCKS) if place * half < end and begin < (place + 1) * half)
        )
    return tuple(times)


COMPUTE = 2
ORDER_OF_FOUR = (
    2000, 1000, 2010, 1010, 2020, 1001, 2030, 2040, 20, 1011, 1002, 2050, 1020, 2060, 2070, 1003,
    21, 1012, 2080, 40, 1021, 2090, 2100, 1004, 22, 1013, 2110, 1022, 41, 10, 2120, 1005,
    1014, 23, 1023, 42, 1006, 11, 1040, 1015, 24, 1024, 43, 1007, 50, 1041, 0, 12,
    1016, 1025, 25, 51, 1042, 1, 30, 1017, 52, 1026, 13, 26, 1043, 2, 53, 1027,
    31, 27, 3, 60, 14, 32, 1044, 4, 1030, 15, 61, 33, 70, 1045, 5, 54,
    1031, 16, 62, 1046, 71, 6, 55, 1047, 1032, 72, 17, 56, 63, 7, 57, 73,
    1033, 34, 44, 64, 35, 74, 45, 65, 75, 36, 46, 1034, 76, 66, 37, 47,
    1035, 77, 67, 1036, 1037,
)


def event_order(line, half):
    _, sizes, counts = reduce_plan(line, half)
    if line == 4 and counts == (8, 5):
        return [(code // 1000, code // 10 % 100, code % 10) for code in ORDER_OF_FOUR]
    firsts = (0, counts[0] * sizes[0])
    steps = [(block, 0, (COMPUTE, block, 0)) for block in range(BLOCKS)]
    for kind in range(2):
        times = ready_times(firsts[kind], sizes[kind], counts[kind], half)
        for group, time in enumerate(times):
            steps += [(time + turn, 1 + kind, (kind, group, turn)) for turn in range(2 * line)]
    return [step for _, _, step in sorted(steps)]


def reduce_phase(
    count,
    channels,
    pool,
    early,
    kept,
    early_hbm,
    totals,
    mix_back,
    in_hbm,
    out_hbm,
    total_hbm,
    small,
    ready_sem,
    back_sem,
    pair_sem,
    pair_send,
    y_sem,
    y_send,
    sum_sem0,
    sum_send0,
    sum_sem1,
    sum_send1,
    spread_sem0,
    spread_send0,
    spread_sem1,
    spread_send1,
    give_sem,
    give_send,
    give_recv,
    small_sem,
    small_send,
):
    section = lax.axis_index("section")
    dp_index = lax.axis_index("dp")
    core = section % 2
    line = count // 2
    z, y = dp_index // 2, dp_index % 2
    half = channels // 2
    pieces, sizes, counts = reduce_plan(line, half)
    firsts = (0, counts[0] * sizes[0])
    partner = {"section": section + 1 - 2 * core}
    across = {"dp": dp_index + 1 - 2 * y}

    def peer(offset):
        return {"dp": lax.rem(dp_index + offset, count)}

    length, chunks = kept.shape[1], early.shape[1] - 2
    starts, _ = pool_plan(count, channels, length, 0)
    mine = pool.at[pl.ds(starts[0], starts[1] - starts[0])]
    theirs = Stack(pool, starts[1], half)
    pair_landing = Stack(pool, starts[2], sizes[0] // 2)
    cross_landing = Stack(pool, starts[3], pieces[1])
    passed = [Stack(pool, starts[4 + kind], (line + 1) * pieces[kind], pieces[kind]) for kind in range(2)]

    def landing(kind, direction, group, step):
        return passed[kind].at[group, step if direction == 0 else line - step]

    right_peer, left_peer = {"dp": dp_index + 2}, {"dp": dp_index - 2}

    def ready(device):
        pl.semaphore_signal(ready_sem, inc=1, device_id=device, device_id_type=MESH)

    ready(partner)
    ready(across)
    pl.when(z < line - 1)(lambda: ready(right_peer))
    pl.when(z > 0)(lambda: ready(left_peer))
    neighbours = 2 + jnp.where(z < line - 1, 1, 0) + jnp.where(z > 0, 1, 0)

    small_pair = pltpu.make_async_remote_copy(
        src_ref=totals.at[1 - core],
        dst_ref=small.at[1],
        send_sem=small_send.at[0],
        recv_sem=small_sem.at[1],
        device_id=partner,
        device_id_type=MESH,
    )

    def small_copy(offset):
        return pltpu.make_async_remote_copy(
            src_ref=small.at[0],
            dst_ref=small.at[1 + offset],
            send_sem=small_send.at[offset],
            recv_sem=small_sem.at[1 + offset],
            device_id=peer(offset),
            device_id_type=MESH,
        )

    def small_start(offset, _):
        small_copy(offset).start()
        return 0

    def small_add(offset, total):
        small_copy(offset).wait()
        return total + small[1 + offset]

    def product(block, which, use):
        columns = pl.ds(pl.multiple_of(which * half, 128), half)
        turn = block - C_BLOCKS
        mixed = (block < 4) | (block == 8)

        @pl.when(mixed)
        def _():
            side = jnp.where(block == 8, 1, 0)
            left = early[side, pl.ds(0, chunks), :, columns].reshape(length, half)
            use(tn(left, kept[jnp.where(block == 8, C_DQ, C_DPRE + block)]))

        @pl.when(~mixed)
        def _():
            left = jnp.where(block < 8, C_HID + block - 4, C_DPRE + turn)
            use(tn(kept[left, :, columns], kept[jnp.where(block < 8, C_DKV, T_DK + turn)]))

    def time_mix_back(turn):
        return pltpu.make_async_copy(
            early_hbm.at[T_MIX0 + turn], kept.at[C_DPRE + turn], back_sem.at[turn]
        )

    def block_rows(block):
        return pl.ds(pl.multiple_of(lookup(block, PLACES) * half, half), half)

    def pair_copy(block):
        return pltpu.make_async_remote_copy(
            src_ref=theirs.at[block % 2],
            dst_ref=mine.at[block_rows(block)],
            send_sem=pair_send.at[block],
            recv_sem=pair_sem.at[block],
            device_id=partner,
            device_id_type=MESH,
        )

    def for_partner(block):
        for side, first in ((0, 0), (1, 8)):

            @pl.when(block == first)
            def _():
                for chunk in range(chunks):
                    mix_back(side, chunk).wait()

        pl.when(block >= C_BLOCKS)(lambda: time_mix_back(block - C_BLOCKS).wait())
        pl.when(block >= 2)(lambda: pair_copy(block - 2).wait_send())

        def store(gradient):
            theirs.at[block % 2][...] = gradient.astype(BF16)

        product(block, 1 - core, store)

        @pl.when(block == 0)
        def _():
            pl.semaphore_wait(ready_sem, neighbours)
            small_pair.start()

        pair_copy(block).start()

    def for_me(block):
        rows = block_rows(block)

        def add(gradient):
            pair_copy(block).wait_recv()
            mine[rows, :] = (gradient + mine[rows, :].astype(F32)).astype(BF16)

        product(block, core, add)
        pl.when(block < 4)(lambda: time_mix_back(block).start())

    blocks_at = tuple(PLACES.index(place) for place in range(BLOCKS))

    def give(kind, group, start):
        size = pieces[kind]
        rows = pl.ds(pl.multiple_of(start, size), size)
        place = start // half if half % sizes[kind] else firsts[kind] // half + group * sizes[kind] // half
        block = lookup(place, blocks_at)
        row = core * half + start - place * half

        def copies(owner, target):
            @pl.when(owner == core)
            def _():
                pltpu.make_async_copy(mine.at[rows], target, give_sem.at[0]).start()

            def remote(device):
                return pltpu.make_async_remote_copy(
                    src_ref=mine.at[rows],
                    dst_ref=target,
                    send_sem=give_send.at[0],
                    recv_sem=give_recv.at[0],
                    device_id=device,
                    device_id_type=MESH,
                )

            @pl.when(owner != core)
            def _():
                remote(partner).start()

            if kind == 0:
                remote({"section": section - core + owner, "dp": dp_index + 1 - 2 * y}).start()

        def to_in(owner, column):
            columns = pl.ds(pl.multiple_of(column * channels, channels), channels)
            copies(owner, in_hbm.at[pl.ds(pl.multiple_of(row, size), size), columns])

        def to_out():
            within = (block - 4) * channels + row
            copies(1, out_hbm.at[pl.ds(pl.multiple_of(within, size), size)])

        of_time = block >= C_BLOCKS
        pl.when((block < 4) | (of_time & (place < BLOCKS)))(
            lambda: to_in(jnp.where(of_time, 0, 1), jnp.where(of_time, block - C_BLOCKS, block))
        )
        pl.when((block >= 4) & ~of_time)(to_out)

    sum_sems = ((sum_sem0, sum_send0), (sum_sem1, sum_send1))
    spread_sems = ((spread_sem0, spread_send0), (spread_sem1, spread_send1))

    def piece_rows(kind, group, index):
        start = firsts[kind] + group * sizes[kind] + index * pieces[kind]
        if kind == 0:
            start = start + y * (sizes[0] // 2)
        return start, pl.ds(pl.multiple_of(start, pieces[kind]), pieces[kind])

    def sum_copy(kind, group, direction, step):
        place = landing(kind, direction, group, step)
        receive, send = sum_sems[kind]
        return pltpu.make_async_remote_copy(
            src_ref=place,
            dst_ref=place,
            send_sem=send.at[group, direction, step],
            recv_sem=receive.at[group, direction, step],
            device_id=(right_peer, left_peer)[direction],
            device_id_type=MESH,
        )

    def spread_copy(kind, group, direction, step, index):
        _, rows = piece_rows(kind, group, index)
        receive, send = spread_sems[kind]
        return pltpu.make_async_remote_copy(
            src_ref=mine.at[rows],
            dst_ref=mine.at[rows],
            send_sem=send.at[group, direction, step],
            recv_sem=receive.at[group, direction, step],
            device_id=(right_peer, left_peer)[direction],
            device_id_type=MESH,
        )

    def passing(kind, group, turn):
        for direction in range(2):
            behind = z if direction == 0 else line - 1 - z
            step = turn - behind
            index = line - 1 - step if direction == 0 else step
            place = landing(kind, direction, group, step)
            _, rows = piece_rows(kind, group, index)

            @pl.when((step >= 0) & (behind == 0) & (step < line - 1))
            def _():
                place[...] = mine[rows, :]
                sum_copy(kind, group, direction, step).start()

            @pl.when((step >= 0) & (behind > 0))
            def _():
                sum_copy(kind, group, direction, step).wait_recv()

                @pl.when(turn < line - 1)
                def _():
                    place[...] = (place[...].astype(F32) + mine[rows, :].astype(F32)).astype(BF16)
                    sum_copy(kind, group, direction, step).start()

    def arrived(kind, group):
        _, rows = piece_rows(kind, group, z)
        total = mine[rows, :].astype(F32)
        from_left = landing(kind, 0, group, jnp.minimum(line - 1 - z, line - 2))
        from_right = landing(kind, 1, group, jnp.minimum(z, line - 2))
        mine[rows, :] = total.astype(BF16)

        @pl.when(z == 0)
        def _():
            mine[rows, :] = (total + from_right[...].astype(F32)).astype(BF16)

        @pl.when(z == line - 1)
        def _():
            mine[rows, :] = (total + from_left[...].astype(F32)).astype(BF16)

        @pl.when((z > 0) & (z < line - 1))
        def _():
            mine[rows, :] = (
                total + from_left[...].astype(F32) + from_right[...].astype(F32)
            ).astype(BF16)

    def finished(kind, group, index):
        start, _ = piece_rows(kind, group, index)
        give(kind, group, start)

    def spread_own(kind, group):
        @pl.when(z < line - 1)
        def _():
            spread_copy(kind, group, 0, 0, z).start()

        @pl.when(z > 0)
        def _():
            spread_copy(kind, group, 1, 0, z).start()

        finished(kind, group, z)

    def spreading(kind, group, hop):
        for direction in range(2):
            index = z - hop if direction == 0 else z + hop
            onward = z < line - 1 if direction == 0 else z > 0
            exists = index >= 0 if direction == 0 else index < line

            @pl.when(exists)
            def _():
                spread_copy(kind, group, direction, hop - 1, index).wait_recv()

                @pl.when(onward)
                def _():
                    spread_copy(kind, group, direction, hop, index).start()

                finished(kind, group, index)

    def over(group):
        start = group * sizes[0] + (1 - y) * (sizes[0] // 2)
        return pltpu.make_async_remote_copy(
            src_ref=mine.at[pl.ds(pl.multiple_of(start, pieces[0]), sizes[0] // 2)],
            dst_ref=pair_landing.at[group],
            send_sem=y_send.at[group],
            recv_sem=y_sem.at[group],
            device_id=across,
            device_id_type=MESH,
        )

    def swap(group):
        _, rows = piece_rows(1, group, z)
        return pltpu.make_async_remote_copy(
            src_ref=mine.at[rows],
            dst_ref=cross_landing.at[group],
            send_sem=y_send.at[counts[0] + group],
            recv_sem=y_sem.at[counts[0] + group],
            device_id=across,
            device_id_type=MESH,
        )

    def event0(group, turn):
        @pl.when(turn == 0)
        def _():
            over(group).start()

        @pl.when(turn == 1)
        def _():
            over(group).wait_recv()

            def add(index, _):
                _, rows = piece_rows(0, group, index)
                local = pl.ds(pl.multiple_of(index * pieces[0], pieces[0]), pieces[0])
                arrived_rows = pair_landing.at[group][local, :]
                mine[rows, :] = (mine[rows, :].astype(F32) + arrived_rows.astype(F32)).astype(BF16)
                return 0

            lax.fori_loop(0, line, add, 0)

        @pl.when((turn >= 1) & (turn <= line))
        def _():
            passing(0, group, turn - 1)

        @pl.when(turn == line)
        def _():
            arrived(0, group)
            spread_own(0, group)

        @pl.when(turn > line)
        def _():
            spreading(0, group, turn - line)

    def event1(group, turn):
        @pl.when(turn < line)
        def _():
            passing(1, group, turn)

        @pl.when(turn == line - 1)
        def _():
            arrived(1, group)
            swap(group).start()

        @pl.when(turn == line)
        def _():
            swap(group).wait()
            _, rows = piece_rows(1, group, z)
            mine[rows, :] = (
                mine[rows, :].astype(F32) + cross_landing[group].astype(F32)
            ).astype(BF16)
            spread_own(1, group)

        @pl.when(turn > line)
        def _():
            spreading(1, group, turn - line)

    spare = firsts[1] + counts[1] * sizes[1] - BLOCKS * half
    if spare:
        mine[pl.ds(BLOCKS * half, spare), :] = jnp.zeros((spare, channels), BF16)
    order = [(COMPUTE, 0, 0)]
    for kind, group, turn in event_order(line, half):
        if kind == COMPUTE:
            order += [(COMPUTE, group + 1, 0)] * (group + 1 < BLOCKS) + [(COMPUTE, group, 1)]
        else:
            order.append((kind, group, turn))
    codes = [kind * 1024 + group * 64 + turn for kind, group, turn in order]
    steps = len(codes)
    words = tuple(a + 4096 * b for a, b in zip(codes[::2], (codes + [0])[1::2], strict=True))

    def take(index, _):
        word = lookup(index // 2, words)
        code = jnp.where(index % 2 == 0, word % 4096, word // 4096)
        kind, group, turn = code // 1024, code // 64 % 16, code % 64

        @pl.when(kind == COMPUTE)
        def _():
            pl.when(turn == 0)(lambda: for_partner(group))
            pl.when(turn == 1)(lambda: for_me(group))

            @pl.when((turn == 1) & (group == BLOCKS // 2))
            def _():
                small_pair.wait()
                small[0] = totals[core] + small[1]
                lax.fori_loop(1, count, small_start, 0)

        pl.when(kind == 0)(lambda: event0(group, turn))
        pl.when(kind == 1)(lambda: event1(group, turn))
        return 0

    lax.fori_loop(0, steps, take, 0)
    small[0] = lax.fori_loop(1, count, small_add, small[0])
    total_copy = pltpu.make_async_copy(small.at[0], total_hbm, small_sem.at[0])
    total_copy.start()

    def over_done(group, _):
        over(group).wait_send()
        return 0

    for block in range(BLOCKS - 2, BLOCKS):
        pair_copy(jnp.int32(block)).wait_send()
    lax.fori_loop(0, counts[0], over_done, 0)
    for kind in range(2):

        def group_done(group, _):
            def step_done(step, _):
                for direction in range(2):
                    behind = z if direction == 0 else line - 1 - z

                    @pl.when(step < line - 1 - behind)
                    def _():
                        sum_copy(kind, group, direction, step).wait_send()

                    @pl.when((step <= behind) & (behind < line - 1))
                    def _():
                        spread_copy(kind, group, direction, step, 0).wait_send()

                return 0

            return lax.fori_loop(0, line - 1, step_done, 0)

        lax.fori_loop(0, counts[kind], group_done, 0)

    def taken(rows, sem):
        if rows:
            ref = mine.at[pl.ds(0, rows)]
            pltpu.make_async_copy(ref, ref, sem.at[0]).wait()

    paired = [PLACES[block] < PAIRED for block in range(BLOCKS)]
    whole = [half // 2 if pair else half for pair in paired]
    by_kind = (range(C_BLOCKS, BLOCKS), range(C_BLOCKS))
    for own in range(2):

        @pl.when(core == own)
        def _():
            local = sum(whole[block] for block in by_kind[own])
            crossed = sum(half // 2 for block in range(BLOCKS) if paired[block])
            other = sum(whole[block] for block in by_kind[1 - own])
            taken(local, give_sem)
            taken(other + crossed, give_send)
            taken(len(by_kind[own]) * channels - local, give_recv)

    total_copy.wait()


def pool_plan(count, channels, length, slots):
    half, line = channels // 2, count // 2
    pieces, sizes, counts = reduce_plan(line, half)
    heights = (
        counts[0] * sizes[0] + counts[1] * sizes[1],
        2 * half,
        counts[0] * sizes[0] // 2,
        counts[1] * pieces[1],
        *[counts[kind] * (line + 1) * pieces[kind] for kind in range(2)],
    )
    starts = [sum(heights[:at]) for at in range(len(heights))]
    return starts, max(sum(heights), slots * channels + 3 * length)


def chain(sections, count, x, cotangent, w_in, w_out, gain, bias, rates, wkv, state):
    length, channels = x.shape[2:]
    hidden_blocks = w_in.shape[2] // channels
    chunks = length // CHUNK
    anywhere = pl.BlockSpec(memory_space=pl.ANY)
    dma = pltpu.SemaphoreType.DMA
    slots = 9 + hidden_blocks
    line = count // 2
    _, _, counts = reduce_plan(line, channels // 2)
    hops = [dma((counts[kind], 2, line - 1)) for kind in range(2)]
    _, pool_rows = pool_plan(count, channels, length, slots)
    return pl.pallas_call(
        functools.partial(chain_kernel, sections, length, channels, hidden_blocks, count),
        out_shape=(
            jax.ShapeDtypeStruct((2, length, channels), BF16),
            jax.ShapeDtypeStruct((2, length, channels), BF16),
            jax.ShapeDtypeStruct((2, 8, channels), F32),
            jax.ShapeDtypeStruct((EARLY, length, channels), BF16),
            jax.ShapeDtypeStruct((channels, 4 * channels), BF16),
            jax.ShapeDtypeStruct(((C_BLOCKS - 4) * channels, channels), BF16),
            jax.ShapeDtypeStruct((8, channels), F32),
        ),
        in_specs=[anywhere] * 9,
        out_specs=(anywhere,) * 7,
        scratch_shapes=[
            pltpu.VMEM((pool_rows, channels), BF16),
            pltpu.VMEM((2, EARLY, CHUNK, channels), BF16),
            pltpu.VMEM((LATE, length, channels), BF16),
            pltpu.VMEM((2, length, channels), F32),
            pltpu.VMEM((length, channels), BF16),
            pltpu.VMEM((5, CHUNK, channels), F32),
            pltpu.VMEM((2 * CHUNK, 2 * channels), BF16),
            pltpu.VMEM((2, CHUNK, channels), F32),
            pltpu.VMEM((2, CHUNK, 2 * CHUNK), BF16),
            pltpu.VMEM((2, 1, channels), F32),
            pltpu.VMEM((2, 1, channels), F32),
            pltpu.VMEM((2, 3, 1, channels), F32),
            pltpu.VMEM((2, 2, channels), F32),
            pltpu.VMEM((2, 3, 2, 1, channels), F32),
            pltpu.VMEM((2, length // ROWS, channels), F32),
            pltpu.VMEM((8, channels), F32),
            pltpu.VMEM((8, channels), F32),
            pltpu.VMEM((2, 8, channels), F32),
            pltpu.VMEM((2, 8, 8, channels), F32),
            pltpu.VMEM((2, 8, channels), F32),
            dma((slots,)),
            dma((slots,)),
            dma((2, 5)),
            dma((5,)),
            dma((chunks,)),
            dma((chunks,)),
            dma((chunks,)),
            dma((chunks,)),
            dma((2 + chunks,)),
            dma((2 + chunks,)),
            dma((2 + chunks,)),
            dma((2,)),
            dma((2, chunks)),
            pltpu.VMEM((count + 1, 8, channels), F32),
            pltpu.SemaphoreType.REGULAR,
            dma((4,)),
            dma((BLOCKS,)),
            dma((BLOCKS,)),
            dma((sum(counts),)),
            dma((sum(counts),)),
            hops[0],
            hops[0],
            hops[1],
            hops[1],
            hops[0],
            hops[0],
            hops[1],
            hops[1],
            dma((1,)),
            dma((1,)),
            dma((1,)),
            dma((count + 1,)),
            dma((count + 1,)),
        ],
        compiler_params=pltpu.CompilerParams(
            collective_id=0, has_side_effects=True, vmem_limit_bytes=VMEM_BYTES
        ),
    )(x, cotangent, w_in, w_out, gain, bias, rates, wkv, state)


def finish_kernel(
    steps,
    in_short,
    out_short,
    outs_in,
    grads_in,
    fin,
    total,
    in_wide,
    out_wide,
    outs,
    grads,
    states,
    normed,
    gain,
    bias,
    rates,
    wkv,
):
    holds_channel_mix = lax.axis_index("section") % 2 == 1
    step = pl.program_id(0)

    @pl.when(step == 0)
    def _():
        for micro in range(2):
            normed[0, micro] = fin[micro, 0:1]
            for row in range(2):
                states[0, row, micro] = fin[micro, 1 + row : 2 + row]
        gain[...] = total[GAIN : GAIN + 1]
        bias[...] = total[BIAS : BIAS + 1]
        for row in range(3):
            rates[row] = total[RATES + row : RATES + row + 1]
        wkv[0] = total[DECAY : DECAY + 2]

    in_wide[...] = in_short[...].astype(F32)
    out_wide[...] = jnp.where(holds_channel_mix, out_short[...].astype(F32), 0.0)
    outs[0, :, 0] = outs_in[...]
    grads[0, :, 0] = grads_in[...]


def finished_outputs(in_short, out_short, outs, grads, fin, total):
    steps = 8
    length, channels = outs.shape[1:]
    whole = pl.BlockSpec(memory_space=pltpu.VMEM)
    kept = pl.BlockSpec((2, length // steps, channels), lambda i: (0, i, 0))
    placed = pl.BlockSpec((1, 2, 1, length // steps, channels), lambda i: (0, 0, 0, i, 0))

    def spec(array):
        rows, columns = array.shape
        return pl.BlockSpec((rows // steps, columns), lambda i: (i, 0))

    def shape(*sizes, dtype=F32):
        return jax.ShapeDtypeStruct(sizes, dtype)

    in_wide, out_wide, *rest = pl.pallas_call(
        functools.partial(finish_kernel, steps),
        grid=(steps,),
        out_shape=(
            shape(*in_short.shape),
            shape(*out_short.shape),
            shape(1, 2, 1, length, channels, dtype=BF16),
            shape(1, 2, 1, length, channels, dtype=BF16),
            shape(1, 2, 2, 1, channels),
            shape(1, 2, 1, channels),
            shape(1, channels),
            shape(1, channels),
            shape(3, 1, channels),
            shape(1, 2, channels),
        ),
        in_specs=[spec(in_short), spec(out_short), kept, kept, whole, whole],
        out_specs=(spec(in_short), spec(out_short), placed, placed) + (whole,) * 6,
        compiler_params=pltpu.CompilerParams(vmem_limit_bytes=VMEM_BYTES),
    )(in_short, out_short, outs, grads, fin, total)
    *rest, rates, wkv = rest
    return in_wide, out_wide, *rest, jnp.swapaxes(rates, 0, 1), wkv


def shards(
    block_input,
    carried_state,
    output_cotangent,
    in_weight,
    out_weight,
    norm_gain,
    norm_bias,
    mix_rates,
    wkv_params,
):
    sections = lax.axis_size("section")
    outs, grads, fin, _, in_short, out_short, total = chain(
        sections,
        lax.axis_size("dp"),
        block_input,
        output_cotangent,
        in_weight,
        out_weight,
        norm_gain,
        norm_bias,
        jnp.swapaxes(mix_rates, 0, 1),
        wkv_params,
        carried_state,
    )
    in_grad, out_grad, outs, grads, states, normed, gain, bias, rates, wkv = finished_outputs(
        in_short, out_short, outs, grads, fin, total
    )
    return outs, states, normed, grads, in_grad[None], out_grad[None], gain, bias, rates, wkv


def solution(mesh):
    return jax.shard_map(
        shards,
        mesh=mesh,
        in_specs=(
            P(None, "dp", None, None),
            P("section", None, None, "dp", None),
            P(None, "dp", None, None),
            P("section", None, None),
            P("section", None, None),
            P("section", None),
            P("section", None),
            P("section", None, None),
            P("section", None, None),
        ),
        out_specs=(
            P("section", None, "dp", None, None),
            P("section", None, None, "dp", None),
            P("section", None, "dp", None),
            P("section", None, "dp", None, None),
            P("section", None, None),
            P("section", None, None),
            P("section", None),
            P("section", None),
            P("section", None, None),
            P("section", None, None),
        ),
        check_vma=False,
    )
```

```python
import functools

import jax
import jax.numpy as jnp
from jax import lax
from jax.experimental import pallas as pl
from jax.experimental.pallas import tpu as pltpu
from jax.sharding import PartitionSpec as P

MESH = pl.DeviceIdType.MESH
F32 = jnp.float32
BF16 = jnp.bfloat16
CHUNK = 256
ROWS = 32
UNROLL = 4
VMEM_BYTES = (64 << 20) - (128 << 10)

T_MIX0, T_MIX2, T_MIX1, T_GATED, C_MIX0, C_MIX1 = 0, 1, 2, 3, 4, 5
EARLY = 6
T_DK, T_DV, T_DQ, T_G, C_DKV, C_DQ, C_HID, C_DPRE = 0, 1, 2, 3, 4, 5, 6, 10
LATE = 14
GAIN, BIAS, RATES, DECAY, BONUS = 0, 1, 2, 5, 6


def nn(left, right):
    return jnp.dot(left, right, preferred_element_type=F32)


def nt(left, right):
    return lax.dot_general(left, right, (((1,), (1,)), ((), ())), preferred_element_type=F32)


def tn(left, right):
    return lax.dot_general(left, right, (((0,), (0,)), ((), ())), preferred_element_type=F32)


class Stack:
    def __init__(self, buffer, start, *heights):
        self.buffer, self.start, self.heights = buffer, start, heights

    @property
    def at(self):
        return Places(self)

    def __getitem__(self, index):
        return self.at[index][...]


class Places:
    def __init__(self, stack):
        self.stack = stack

    def __getitem__(self, index):
        index = index if isinstance(index, tuple) else (index,)
        start, height = self.stack.start, self.stack.heights[-1]
        for place, tall in zip(index, self.stack.heights, strict=True):
            start = start + place * tall
        if not isinstance(start, int):
            start = pl.multiple_of(start, 16)
        return self.stack.buffer.at[pl.ds(start, height)]


def folded(rows):
    total = rows[0:8]
    for start in range(8, rows.shape[0], 8):
        total = total + rows[start : start + 8]
    return total


def chain_kernel(
    sections,
    length,
    channels,
    hidden_blocks,
    count,
    x_hbm,
    cot_hbm,
    w_in_hbm,
    w_out_hbm,
    gain_hbm,
    bias_hbm,
    rates_hbm,
    wkv_hbm,
    state_hbm,
    outs_hbm,
    grads_hbm,
    fin_hbm,
    early_hbm,
    in_hbm,
    out_hbm,
    total_hbm,
    pool,
    early,
    kept,
    states,
    upstream,
    wide,
    pairs,
    tables,
    triangles,
    gains,
    biases,
    rates,
    wkvs,
    starts,
    previous,
    carry,
    carry_next,
    fin,
    sums,
    totals,
    weight_sem,
    weight_send,
    small_sem,
    small_send,
    entry_sem,
    entry_send,
    up_sem,
    up_send,
    out_sem,
    out_send,
    out_recv,
    early_sem,
    *reducing,
):
    section = lax.axis_index("section")
    dp_index = lax.axis_index("dp")
    core = section % 2
    stage = section // 2
    stages = sections // 2
    partner = {"section": section + 1 - 2 * core}
    chunks = length // CHUNK
    blocks = CHUNK // ROWS
    time_blocks = 4
    last_stage = stage == stages - 1
    weights = Stack(pool, 0, channels)
    after_weights = (9 + hidden_blocks) * channels
    entry = pool.at[pl.ds(after_weights, length)]
    hs = Stack(pool, after_weights + length, length)
    mid, top = hs.at[0], hs.at[1]

    barrier = pltpu.get_barrier_semaphore()
    across = {"dp": dp_index + 1 - 2 * (dp_index % 2)}
    for device in (partner, partner | across):
        pl.semaphore_signal(barrier, inc=1, device_id=device, device_id_type=MESH)

    def greet(offset, _):
        peer = {"dp": lax.rem(dp_index + offset, count)}
        pl.semaphore_signal(barrier, inc=1, device_id=peer, device_id_type=MESH)
        return 0

    lax.fori_loop(1, count, greet, 0)

    @pl.when(stage > 0)
    def _():
        for other in (section - 2, section - 1 - 2 * core):
            pl.semaphore_signal(barrier, inc=1, device_id={"section": other}, device_id_type=MESH)

    @pl.when(stage < stages - 1)
    def _():
        for other in (section + 2, section + 3 - 2 * core):
            pl.semaphore_signal(barrier, inc=1, device_id={"section": other}, device_id_type=MESH)

    def entry_copy(chunk):
        rows = pl.ds(chunk * CHUNK, CHUNK)
        return pltpu.make_async_copy(
            x_hbm.at[core, 0, rows], entry.at[rows], entry_sem.at[chunk]
        )

    def up_copy(chunk):
        rows = pl.ds(chunk * CHUNK, CHUNK)
        return pltpu.make_async_copy(
            cot_hbm.at[core, 0, rows], upstream.at[rows], up_sem.at[chunk]
        )

    @pl.when(stage == 0)
    def _():
        for chunk in range(chunks):
            entry_copy(chunk).start()

    @pl.when(last_stage)
    def _():
        for chunk in range(chunks):
            up_copy(chunk).start()

    small_pairs = (
        (gain_hbm, gains.at[core]),
        (bias_hbm, biases.at[core]),
        (rates_hbm, rates.at[core]),
        (wkv_hbm.at[0], wkvs.at[core]),
        (state_hbm.at[0], starts.at[core]),
    )
    small_copies = [
        pltpu.make_async_copy(source, target, small_sem.at[0, at])
        for at, (source, target) in enumerate(small_pairs)
    ]
    for copy in small_copies:
        copy.start()

    def in_block(index):
        return w_in_hbm.at[0, :, pl.ds(index * channels, channels)]

    def out_block(index):
        return w_out_hbm.at[0, pl.ds(index * channels, channels), :]

    for index in range(4):
        slot = core * time_blocks + index
        pltpu.make_async_copy(in_block(index), weights.at[slot], weight_sem.at[slot]).start()

    @pl.when(core == 1)
    def _():
        for index in range(hidden_blocks + 1):
            slot = 8 + index
            pltpu.make_async_copy(
                out_block(index), weights.at[slot], weight_sem.at[slot]
            ).start()

    has_previous = jnp.where(stage > 0, 1, 0)
    has_next = jnp.where(stage < stages - 1, 1, 0)
    pl.semaphore_wait(barrier, 1 + count + 2 * (has_previous + has_next))

    small_remotes = [
        pltpu.make_async_remote_copy(
            src_ref=source,
            dst_ref=target,
            send_sem=small_send.at[at],
            recv_sem=small_sem.at[1, at],
            device_id=partner,
            device_id_type=MESH,
        )
        for at, (source, target) in enumerate(small_pairs)
    ]

    def in_remote(index):
        slot = core * time_blocks + index
        return pltpu.make_async_remote_copy(
            src_ref=in_block(index),
            dst_ref=weights.at[slot],
            send_sem=weight_send.at[slot],
            recv_sem=weight_sem.at[slot],
            device_id=partner,
            device_id_type=MESH,
        )

    def out_remote(index):
        slot = 8 + index
        return pltpu.make_async_remote_copy(
            src_ref=out_block(index),
            dst_ref=weights.at[slot],
            send_sem=weight_send.at[slot],
            recv_sem=weight_sem.at[slot],
            device_id=partner,
            device_id_type=MESH,
        )

    for copy in small_remotes:
        copy.start()
    for index in range(4):
        in_remote(index).start()

    @pl.when(core == 1)
    def _():
        for index in (hidden_blocks, *range(hidden_blocks)):
            out_remote(index).start()

    row_at = lax.broadcasted_iota(jnp.int32, (CHUNK, 2 * CHUNK), 0)
    column_at = lax.broadcasted_iota(jnp.int32, (CHUNK, 2 * CHUNK), 1)
    column_at = jnp.where(column_at >= CHUNK, column_at - CHUNK, column_at)
    triangles[0] = jnp.where(row_at > column_at, 1.0, 0.0).astype(BF16)
    triangles[1] = jnp.where(row_at < column_at, 1.0, 0.0).astype(BF16)
    sums[...] = jnp.zeros_like(sums)
    fin[...] = jnp.zeros_like(fin)

    for copy in small_copies:
        copy.wait()
    for copy in small_remotes:
        copy.wait_recv()

    rate = jnp.exp(wkvs[0, 0:1, :])
    step = jnp.exp(-rate)
    lift = jnp.exp(wkvs[0, 1:2, :])

    def table_rows(index, _):
        start = pl.multiple_of(index * ROWS, ROWS)
        place = (lax.broadcasted_iota(jnp.int32, (ROWS, channels), 0) + start).astype(F32)
        tables[0, pl.ds(start, ROWS), :] = jnp.exp(-(CHUNK - 1.0 - place) * rate)
        tables[1, pl.ds(start, ROWS), :] = jnp.exp(-place * rate)
        return 0

    lax.fori_loop(0, blocks, table_rows, 0)

    for row in range(3):
        carry[row : row + 1] = starts[0, row, core]
    carry[3:4] = starts[1, 0, core]

    def weight_wait(slot):
        pltpu.make_async_copy(weights.at[slot], weights.at[slot], weight_sem.at[slot]).wait()

    def stats(tokens):
        center = tokens - jnp.mean(tokens, axis=-1, keepdims=True)
        spread = jnp.mean(center * center, axis=-1, keepdims=True)
        root = lax.rsqrt(spread + 1e-05)
        return center * root, root

    row_index = lax.broadcasted_iota(jnp.int32, (ROWS, channels), 0)

    def token_mix(kind, source, base, side, slots, carry_row):
        gain, bias = gains[kind], biases[kind]

        def body(index, before):
            start = pl.multiple_of(base + index * ROWS, ROWS)
            rows = pl.ds(start, ROWS)
            unit, _ = stats(source[rows, :].astype(F32))
            normed = unit * gain + bias
            previous[kind, pl.ds(start // ROWS, 1), :] = before
            shifted = jnp.where(
                row_index == 0, jnp.broadcast_to(before, normed.shape), pltpu.roll(normed, 1, 0)
            )
            gap = normed - shifted
            for rate_row, slot in slots:
                early[side, slot, pl.ds(pl.multiple_of(index * ROWS, ROWS), ROWS), :] = (
                    shifted + gap * rates[kind, rate_row]
                ).astype(BF16)
            return normed[ROWS - 1 : ROWS, :]

        carry[carry_row : carry_row + 1] = lax.fori_loop(
            0, blocks, body, carry[carry_row : carry_row + 1], unroll=UNROLL
        )

    def early_copy(chunk):
        rows = pl.ds(pl.multiple_of(chunk * CHUNK, CHUNK), CHUNK)
        side = chunk % 2
        return pltpu.make_async_copy(
            early.at[side], early_hbm.at[:, rows], early_sem.at[side]
        )

    def forward_chunk(chunk, _):
        base = pl.multiple_of(chunk * CHUNK, CHUNK)
        rows = pl.ds(base, CHUNK)
        side = chunk % 2

        @pl.when(chunk >= 2)
        def _():
            early_copy(chunk - 2).wait()

        pltpu.make_async_copy(entry.at[rows], entry.at[rows], entry_sem.at[chunk]).wait()

        token_mix(0, entry, base, side, ((0, T_MIX0), (2, T_MIX2), (1, T_MIX1)), 0)

        for slot in range(3):

            @pl.when(chunk == 0)
            def _():
                weight_wait(slot)

            wide[slot] = nn(early[side, slot], weights[slot])

        def weighted(index, _):
            start = pl.multiple_of(index * ROWS, ROWS)
            local = pl.ds(start, ROWS)
            whole = pl.ds(pl.multiple_of(base + start, ROWS), ROWS)
            value = wide[1, local, :]
            power = jnp.exp(wide[0, local, :])
            wide[0, local, :] = power
            scaled = power * tables[0, local, :]
            pairs[local, pl.ds(0, channels)] = (scaled * value).astype(BF16)
            pairs[local, pl.ds(channels, channels)] = scaled.astype(BF16)
            kept[T_DK, whole, :] = power.astype(BF16)
            kept[T_DV, whole, :] = value.astype(BF16)
            return 0

        lax.fori_loop(0, blocks, weighted, 0)
        wide[3] = nn(triangles[0, :, pl.ds(0, CHUNK)], pairs[pl.ds(0, CHUNK), pl.ds(0, channels)])
        wide[4] = nn(
            triangles[0, :, pl.ds(0, CHUNK)], pairs[pl.ds(0, CHUNK), pl.ds(channels, channels)]
        )
        upper, lower = carry[1:2], carry[2:3]

        def averaged(index, _):
            start = pl.multiple_of(index * ROWS, ROWS)
            local = pl.ds(start, ROWS)
            whole = pl.ds(pl.multiple_of(base + start, ROWS), ROWS)
            place = (row_index + start).astype(F32)
            grown = jnp.exp((CHUNK - place) * rate)
            faded = tables[1, local, :]
            power, value = wide[0, local, :], wide[1, local, :]
            before_upper = grown * wide[3, local, :] + faded * upper
            before_lower = grown * wide[4, local, :] + faded * lower
            now = power * lift
            average = (before_upper + now * value) / (before_lower + now)
            gate = jax.nn.sigmoid(wide[2, local, :])
            states[0, whole, :] = before_upper
            states[1, whole, :] = before_lower
            kept[T_DQ, whole, :] = gate.astype(BF16)
            early[side, T_GATED, local, :] = (gate * average).astype(BF16)
            tail = slice(ROWS - 8, ROWS)
            after_upper = step * before_upper[tail] + power[tail] * value[tail]
            after_lower = step * before_lower[tail] + power[tail]
            carry_next[0:1] = after_upper[7:8]
            carry_next[1:2] = after_lower[7:8]
            return 0

        lax.fori_loop(0, blocks, averaged, 0)
        carry[1:3] = carry_next[0:2]

        @pl.when(chunk == 0)
        def _():
            weight_wait(3)

        mid[rows, :] = (
            entry[rows, :].astype(F32) + nn(early[side, T_GATED], weights[3])
        ).astype(BF16)

        token_mix(1, mid, base, side, ((0, C_MIX0), (1, C_MIX1)), 3)

        for index in range(hidden_blocks):

            @pl.when(chunk == 0)
            def _():
                weight_wait(4 + index)

            pre = nn(early[side, C_MIX0], weights[4 + index])
            kept[C_HID + index, rows, :] = jnp.square(jnp.maximum(pre, 0.0)).astype(BF16)

        @pl.when(chunk == 0)
        def _():
            weight_wait(8 + hidden_blocks)

        early_copy(chunk).start()
        wide[1] = nn(early[side, C_MIX1], weights[8 + hidden_blocks])

        @pl.when(chunk == 0)
        def _():
            for index in range(hidden_blocks):
                weight_wait(8 + index)

        total = nn(kept[C_HID, rows, :], weights[8])
        for index in range(1, hidden_blocks):
            total = total + nn(kept[C_HID + index, rows, :], weights[8 + index])
        wide[0] = total

        def joined(index, _):
            start = pl.multiple_of(index * ROWS, ROWS)
            local = pl.ds(start, ROWS)
            whole = pl.ds(pl.multiple_of(base + start, ROWS), ROWS)
            gate = jax.nn.sigmoid(wide[1, local, :])
            value = wide[0, local, :]
            kept[C_DKV, whole, :] = gate.astype(BF16)
            kept[C_DQ, whole, :] = value.astype(BF16)
            top[whole, :] = (mid[whole, :].astype(F32) + gate * value).astype(BF16)
            return 0

        lax.fori_loop(0, blocks, joined, 0)

        @pl.when(stage < stages - 1)
        def _():
            entry_remote(chunk).start()

        return 0

    def entry_remote(chunk):
        rows = pl.ds(pl.multiple_of(chunk * CHUNK, CHUNK), CHUNK)
        return pltpu.make_async_remote_copy(
            src_ref=top.at[rows],
            dst_ref=entry.at[rows],
            send_sem=entry_send.at[chunk],
            recv_sem=entry_sem.at[chunk],
            device_id={"section": section + 2},
            device_id_type=MESH,
        )

    def up_remote(chunk):
        rows = pl.ds(pl.multiple_of(chunk * CHUNK, CHUNK), CHUNK)
        return pltpu.make_async_remote_copy(
            src_ref=upstream.at[rows],
            dst_ref=upstream.at[rows],
            send_sem=up_send.at[chunk],
            recv_sem=up_sem.at[chunk],
            device_id={"section": section - 2},
            device_id_type=MESH,
        )

    lax.fori_loop(0, chunks, forward_chunk, 0)
    early_copy(chunks - 2).wait()
    early_copy(chunks - 1).wait()

    def mix_back(side, chunk):
        return pltpu.make_async_copy(
            early_hbm.at[C_MIX0 + side, pl.ds(chunk * CHUNK, CHUNK)],
            early.at[side, chunk],
            back_sem.at[side, chunk],
        )

    back_sem, reducing = reducing[0], reducing[1:]
    for side in range(2):
        for chunk in range(chunks):
            mix_back(side, chunk).start()

    fin[0, 0:1] = carry[0:1]
    fin[0, 1:3] = carry[1:3]
    fin[1, 0:1] = carry[3:4]

    def to_owner(index, own_src, other_src, dst):
        own = pltpu.make_async_copy(own_src, dst, out_sem.at[index])
        other = pltpu.make_async_remote_copy(
            src_ref=other_src,
            dst_ref=dst,
            send_sem=out_send.at[index],
            recv_sem=out_recv.at[index],
            device_id=partner,
            device_id_type=MESH,
        )
        return own, other

    outs_copies = to_owner(0, hs.at[core], hs.at[1 - core], outs_hbm.at[core])
    fin_copies = to_owner(1, fin.at[core], fin.at[1 - core], fin_hbm.at[core])
    for copy in outs_copies + fin_copies:
        copy.start()

    carry[0:4] = jnp.zeros((4, channels), F32)

    def norm_back(kind, source, base, mixes, above, target, carry_row):
        gain, bias = gains[kind], biases[kind]

        def body(index, after):
            back = blocks - 1 - index
            local = pl.ds(pl.multiple_of(back * ROWS, ROWS), ROWS)
            start = pl.multiple_of(base + back * ROWS, ROWS)
            rows = pl.ds(start, ROWS)
            unit, root = stats(source[rows, :].astype(F32))
            normed = unit * gain + bias
            before = previous[kind, pl.ds(start // ROWS, 1), :]
            shifted = jnp.where(
                row_index == 0, jnp.broadcast_to(before, normed.shape), pltpu.roll(normed, 1, 0)
            )
            gap = normed - shifted
            straight = jnp.zeros_like(normed)
            total = jnp.zeros_like(normed)
            for rate_row, slot in mixes:
                mix = wide[slot, local, :]
                straight = straight + mix * rates[kind, rate_row]
                total = total + mix
                sums[kind, RATES + rate_row] += folded(mix * gap)
            late = total - straight
            moved = jnp.where(
                row_index == ROWS - 1,
                jnp.broadcast_to(after, late.shape),
                pltpu.roll(late, ROWS - 1, 0),
            )
            d_normed = straight + moved
            sums[kind, GAIN] += folded(d_normed * unit)
            sums[kind, BIAS] += folded(d_normed)
            d_unit = d_normed * gain
            d_tokens = (
                d_unit
                - jnp.mean(d_unit, axis=-1, keepdims=True)
                - unit * jnp.mean(d_unit * unit, axis=-1, keepdims=True)
            ) * root
            target[rows, :] = (above[rows, :].astype(F32) + d_tokens).astype(BF16)
            return late[0:1, :]

        carry[carry_row : carry_row + 1] = lax.fori_loop(
            0, blocks, body, carry[carry_row : carry_row + 1], unroll=UNROLL
        )

    def grad_copies(chunk, kind):
        rows = pl.ds(pl.multiple_of(chunk * CHUNK, CHUNK), CHUNK)
        sources = (upstream.at[rows], kept.at[T_G, rows])
        return to_owner(
            2 + chunk, sources[kind], sources[1 - kind], grads_hbm.at[core, rows]
        )

    def backward_chunk(turn, _):
        chunk = chunks - 1 - turn
        base = pl.multiple_of(chunk * CHUNK, CHUNK)
        rows = pl.ds(base, CHUNK)
        pltpu.make_async_copy(upstream.at[rows], upstream.at[rows], up_sem.at[chunk]).wait()

        def split(index, _):
            whole = pl.ds(pl.multiple_of(base + index * ROWS, ROWS), ROWS)
            above = upstream[whole, :].astype(F32)
            gate = kept[C_DKV, whole, :].astype(F32)
            value = kept[C_DQ, whole, :].astype(F32)
            d_value = above * gate
            kept[C_DKV, whole, :] = d_value.astype(BF16)
            kept[C_DQ, whole, :] = (d_value * value * (1.0 - gate)).astype(BF16)
            return 0

        lax.fori_loop(0, blocks, split, 0)

        for index in range(hidden_blocks):
            d_hidden = nt(kept[C_DKV, rows, :], weights[8 + index])
            slope = jnp.sqrt(kept[C_HID + index, rows, :].astype(F32))
            kept[C_DPRE + index, rows, :] = (d_hidden * (2.0 * slope)).astype(BF16)
        total = nt(kept[C_DPRE, rows, :], weights[4])
        for index in range(1, hidden_blocks):
            total = total + nt(kept[C_DPRE + index, rows, :], weights[4 + index])
        wide[0] = total
        wide[1] = nt(kept[C_DQ, rows, :], weights[8 + hidden_blocks])
        norm_back(1, mid, base, ((0, 0), (1, 1)), upstream, kept.at[T_G], 3)

        wide[0] = nt(kept[T_G, rows, :], weights[3])

        def inputs(index, _):
            start = pl.multiple_of(index * ROWS, ROWS)
            local = pl.ds(start, ROWS)
            whole = pl.ds(pl.multiple_of(base + start, ROWS), ROWS)
            power = kept[T_DK, whole, :].astype(F32)
            value = kept[T_DV, whole, :].astype(F32)
            gate = kept[T_DQ, whole, :].astype(F32)
            now = power * lift
            inverse = 1.0 / (states[1, whole, :] + now)
            average = (states[0, whole, :] + now * value) * inverse
            d_average = wide[0, local, :] * gate
            kept[T_DQ, whole, :] = (d_average * average * (1.0 - gate)).astype(BF16)
            unit = d_average * inverse
            wide[1, local, :] = unit
            wide[2, local, :] = average
            scaled = unit * tables[1, local, :]
            for column, term in ((0, scaled), (channels, -scaled * average)):
                high = term.astype(BF16)
                pairs[local, pl.ds(column, channels)] = high
                pairs[pl.ds(pl.multiple_of(CHUNK + start, ROWS), ROWS), pl.ds(column, channels)] = (
                    term - high.astype(F32)
                ).astype(BF16)
            return 0

        lax.fori_loop(0, blocks, inputs, 0)
        wide[3] = nn(triangles[1], pairs[:, pl.ds(0, channels)])
        wide[4] = nn(triangles[1], pairs[:, pl.ds(channels, channels)])
        alpha_after, beta_after = carry[1:2], carry[2:3]

        def outputs(index, _):
            start = pl.multiple_of((blocks - 1 - index) * ROWS, ROWS)
            local = pl.ds(start, ROWS)
            whole = pl.ds(pl.multiple_of(base + start, ROWS), ROWS)
            place = (row_index + start).astype(F32)
            grown = jnp.exp((place + 1.0) * rate)
            faded = tables[0, local, :]
            alpha = grown * wide[3, local, :] + faded * alpha_after
            beta = grown * wide[4, local, :] + faded * beta_after
            unit, average = wide[1, local, :], wide[2, local, :]
            power = kept[T_DK, whole, :].astype(F32)
            value = kept[T_DV, whole, :].astype(F32)
            weighed = unit * (power * lift)
            own = weighed * (value - average)
            kept[T_DK, whole, :] = (own + power * (alpha * value + beta)).astype(BF16)
            kept[T_DV, whole, :] = (weighed + power * alpha).astype(BF16)
            sums[0, BONUS] += folded(own)
            sums[0, DECAY] += folded(
                alpha * states[0, whole, :] + beta * states[1, whole, :]
            )
            carry_next[0:1] = unit[0:1] + step * alpha[0:1]
            carry_next[1:2] = step * beta[0:1] - unit[0:1] * average[0:1]
            return 0

        lax.fori_loop(0, blocks, outputs, 0)
        carry[1:3] = carry_next[0:2]
        wide[0] = nt(kept[T_DK, rows, :], weights[0])
        wide[1] = nt(kept[T_DQ, rows, :], weights[2])
        wide[2] = nt(kept[T_DV, rows, :], weights[1])
        norm_back(
            0, entry, base, ((0, 0), (1, 1), (2, 2)), kept.at[T_G], upstream, 0
        )

        @pl.when(stage > 0)
        def _():
            up_remote(chunk).start()

        for kind in range(2):

            @pl.when(core == kind)
            def _():
                for copy in grad_copies(chunk, kind):
                    copy.start()

        return 0

    lax.fori_loop(0, chunks, backward_chunk, 0)

    sums[0, DECAY] = sums[0, DECAY] * (-rate * step)
    for kind in range(2):
        for row in range(7):
            totals[kind, row : row + 1] = jnp.sum(sums[kind, row], axis=0, keepdims=True)
        totals[kind, 7:8] = jnp.zeros((1, channels), F32)

    for copy in outs_copies:
        copy.wait()

    @pl.when(stage < stages - 1)
    def _():
        for chunk in range(chunks):
            entry_remote(chunk).wait_send()

    reduce_phase(
        sections, count, channels, pool, early, kept, early_hbm, totals, mix_back, in_hbm, out_hbm, total_hbm, *reducing
    )

    for copy in fin_copies:
        copy.wait()
    for chunk in range(chunks):
        for copy in grad_copies(chunk, 0):
            copy.wait()
    for copy in small_remotes:
        copy.wait_send()
    for index in range(4):
        in_remote(index).wait_send()

    @pl.when(core == 1)
    def _():
        for index in range(hidden_blocks + 1):
            out_remote(index).wait_send()

    @pl.when(stage > 0)
    def _():
        for chunk in range(chunks):
            up_remote(chunk).wait_send()


C_BLOCKS = 9
T_BLOCKS = 4
BLOCKS = C_BLOCKS + T_BLOCKS
PLACES = (8, 9, 0, 1, 2, 10, 3, 11, 4, 5, 6, 12, 7)
PAIRED = 8
LENT = 3


def lookup(index, table):
    value = jnp.int32(table[0])
    for at, entry in enumerate(table[1:], 1):
        value = jnp.where(index == at, entry, value)
    return value


def reduce_plan(line, half):
    pieces = (max(16, half // (2 * line)), max(16, half // line))
    sizes = (2 * line * pieces[0], line * pieces[1])
    counts = (-(-PAIRED * half // sizes[0]), -(-(BLOCKS - PAIRED) * half // sizes[1]))
    return pieces, sizes, counts


def lends(sections, line, half):
    return sections == 4 and line == 4 and reduce_plan(line, half)[1:] == ((half, half), (8, 5))


def ready_times(first, size, count, half):
    made = {place: time for time, place in enumerate(PLACES)}
    times = []
    for group in range(count):
        begin, end = first + group * size, first + (group + 1) * size
        times.append(
            max(made[place] for place in range(BLOCKS) if place * half < end and begin < (place + 1) * half)
        )
    return tuple(times)


COMPUTE = 2
ORDERS_OF_FOUR = (
    (
        2000, 1000, 2010, 1010, 2020, 1001, 2030, 2040, 20, 1011, 1002, 2050, 1020, 2060, 2070, 1003,
        21, 1012, 2080, 40, 1021, 2090, 1004, 2100, 22, 1013, 2110, 1022, 41, 10, 1005, 2120,
        1014, 23, 1023, 42, 1006, 11, 1040, 1015, 24, 1024, 43, 1007, 50, 1041, 0, 12,
        1016, 1025, 25, 51, 1042, 1, 1017, 52, 1026, 13, 26, 1043, 2, 53, 1027, 27,
        3, 60, 14, 1044, 4, 70, 1030, 15, 61, 1045, 5, 54, 1031, 16, 62, 1046,
        71, 6, 55, 1047, 1032, 72, 17, 56, 7, 63, 57, 73, 1033, 44, 64, 74,
        45, 65, 75, 46, 1034, 76, 66, 47, 1035, 77, 67, 1036, 1037,
    ),
    (
        2000, 1000, 2010, 1010, 2020, 1001, 2030, 2040, 20, 1011, 1002, 2050, 1020, 2060, 2070, 1003,
        21, 1012, 2080, 40, 1021, 2090, 2100, 1004, 22, 1013, 2110, 1022, 41, 10, 2120, 1005,
        1014, 23, 1023, 42, 1006, 11, 1040, 1015, 24, 1024, 43, 1007, 50, 1041, 0, 12,
        1016, 1025, 25, 1050, 51, 1042, 1, 30, 1017, 52, 1026, 1051, 13, 26, 1043, 2,
        53, 1027, 31, 1052, 27, 3, 60, 14, 32, 1044, 4, 1053, 1030, 15, 61, 33,
        70, 1045, 5, 1054, 54, 1031, 16, 62, 1046, 71, 6, 1055, 55, 1047, 1032, 72,
        17, 56, 63, 1056, 7, 57, 73, 1033, 34, 44, 64, 1057, 35, 74, 45, 65,
        75, 36, 46, 1034, 76, 66, 37, 47, 1035, 77, 67, 1036, 1037,
    ),
    (
        2000, 1000, 2010, 1010, 2020, 1001, 2030, 2040, 20, 1011, 1002, 2050, 1020, 2060, 2070, 1003,
        21, 1012, 2080, 40, 1021, 2090, 2100, 1004, 22, 1013, 2110, 1022, 41, 10, 2120, 1005,
        1014, 23, 1023, 42, 1006, 11, 1040, 1015, 24, 1024, 43, 1007, 50, 1041, 0, 12,
        1016, 1025, 25, 51, 1042, 1, 30, 1017, 52, 1026, 13, 26, 1043, 2, 53, 1027,
        31, 27, 3, 60, 14, 32, 1044, 4, 1030, 15, 61, 33, 70, 1045, 5, 54,
        1031, 16, 62, 1046, 71, 6, 55, 1047, 1032, 72, 17, 56, 63, 7, 57, 73,
        1033, 34, 44, 64, 35, 74, 45, 65, 75, 36, 46, 1034, 76, 66, 37, 47,
        1035, 77, 67, 1036, 1037,
    ),
)


def event_order(line, half):
    _, sizes, counts = reduce_plan(line, half)
    firsts = (0, counts[0] * sizes[0])
    steps = [(block, 0, (COMPUTE, block, 0)) for block in range(BLOCKS)]
    for kind in range(2):
        times = ready_times(firsts[kind], sizes[kind], counts[kind], half)
        for group, time in enumerate(times):
            steps += [(time + turn, 1 + kind, (kind, group, turn)) for turn in range(2 * line)]
    return [step for _, _, step in sorted(steps)]


def stage_orders(sections, line, half):
    if lends(sections, line, half):
        return [[(code // 1000, code // 10 % 100, code % 10) for code in order] for order in ORDERS_OF_FOUR]
    return [event_order(line, half)]


def reduce_phase(
    sections,
    count,
    channels,
    pool,
    early,
    kept,
    early_hbm,
    totals,
    mix_back,
    in_hbm,
    out_hbm,
    total_hbm,
    small,
    ready_sem,
    back_sem,
    pair_sem,
    pair_send,
    y_sem,
    y_send,
    sum_sem0,
    sum_send0,
    sum_sem1,
    sum_send1,
    spread_sem0,
    spread_send0,
    spread_sem1,
    spread_send1,
    lend_sem,
    lend_send,
    give_sem,
    give_send,
    give_recv,
    small_sem,
    small_send,
):
    section = lax.axis_index("section")
    dp_index = lax.axis_index("dp")
    core = section % 2
    line = count // 2
    z, y = dp_index // 2, dp_index % 2
    half = channels // 2
    pieces, sizes, counts = reduce_plan(line, half)
    firsts = (0, counts[0] * sizes[0])
    lent = lends(sections, line, half)
    lender, borrower = section == 1, section == sections - 1
    partner = {"section": section + 1 - 2 * core}
    across = {"dp": dp_index + 1 - 2 * y}

    def peer(offset):
        return {"dp": lax.rem(dp_index + offset, count)}

    length, chunks = kept.shape[1], early.shape[1] - 2
    starts, _ = pool_plan(sections, count, channels, length, 0)
    mine = pool.at[pl.ds(starts[0], starts[1] - starts[0])]
    theirs = Stack(pool, starts[1], half)
    pair_landing = Stack(pool, starts[2], sizes[0] // 2)
    cross_landing = Stack(pool, starts[3], pieces[1])
    passed = [Stack(pool, starts[4 + kind], (line + 1) * pieces[kind], pieces[kind]) for kind in range(2)]

    def landing(kind, direction, group, step):
        return passed[kind].at[group, step if direction == 0 else line - step]

    right_peer, left_peer = {"dp": dp_index + 2}, {"dp": dp_index - 2}

    def ready(device):
        pl.semaphore_signal(ready_sem, inc=1, device_id=device, device_id_type=MESH)

    ready(partner)
    ready(across)
    pl.when(z < line - 1)(lambda: ready(right_peer))
    pl.when(z > 0)(lambda: ready(left_peer))
    neighbours = 2 + jnp.where(z < line - 1, 1, 0) + jnp.where(z > 0, 1, 0)
    if lent:
        pl.when(borrower)(lambda: ready({"section": section - 2}))
        neighbours = neighbours + jnp.where(lender, 1, 0)

    small_pair = pltpu.make_async_remote_copy(
        src_ref=totals.at[1 - core],
        dst_ref=small.at[1],
        send_sem=small_send.at[0],
        recv_sem=small_sem.at[1],
        device_id=partner,
        device_id_type=MESH,
    )

    def small_copy(offset):
        return pltpu.make_async_remote_copy(
            src_ref=small.at[0],
            dst_ref=small.at[1 + offset],
            send_sem=small_send.at[offset],
            recv_sem=small_sem.at[1 + offset],
            device_id=peer(offset),
            device_id_type=MESH,
        )

    def small_start(offset, _):
        small_copy(offset).start()
        return 0

    def small_add(offset, total):
        small_copy(offset).wait()
        return total + small[1 + offset]

    def product(block, which, use):
        columns = pl.ds(pl.multiple_of(which * half, 128), half)
        turn = block - C_BLOCKS
        mixed = (block < 4) | (block == 8)

        @pl.when(mixed)
        def _():
            side = jnp.where(block == 8, 1, 0)
            left = early[side, pl.ds(0, chunks), :, columns].reshape(length, half)
            use(tn(left, kept[jnp.where(block == 8, C_DQ, C_DPRE + block)]))

        @pl.when(~mixed)
        def _():
            left = jnp.where(block < 8, C_HID + block - 4, C_DPRE + turn)
            use(tn(kept[left, :, columns], kept[jnp.where(block < 8, C_DKV, T_DK + turn)]))

    def time_mix_back(turn):
        return pltpu.make_async_copy(
            early_hbm.at[T_MIX0 + turn], kept.at[C_DPRE + turn], back_sem.at[turn]
        )

    def block_rows(block):
        return pl.ds(pl.multiple_of(lookup(block, PLACES) * half, half), half)

    def pair_copy(block):
        return pltpu.make_async_remote_copy(
            src_ref=theirs.at[block % 2],
            dst_ref=mine.at[block_rows(block)],
            send_sem=pair_send.at[block],
            recv_sem=pair_sem.at[block],
            device_id=partner,
            device_id_type=MESH,
        )

    def for_partner(block):
        for side, first in ((0, 0), (1, 8)):

            @pl.when(block == first)
            def _():
                for chunk in range(chunks):
                    mix_back(side, chunk).wait()

        pl.when(block >= C_BLOCKS)(lambda: time_mix_back(block - C_BLOCKS).wait())
        pl.when(block >= 2)(lambda: pair_copy(block - 2).wait_send())

        def store(gradient):
            theirs.at[block % 2][...] = gradient.astype(BF16)

        product(block, 1 - core, store)

        @pl.when(block == 0)
        def _():
            pl.semaphore_wait(ready_sem, neighbours)
            small_pair.start()

        pair_copy(block).start()

    def lend_copy():
        return pltpu.make_async_remote_copy(
            src_ref=mine.at[pl.ds(LENT * half, half)],
            dst_ref=mine.at[pl.ds(BLOCKS * half, half)],
            send_sem=lend_send.at[0],
            recv_sem=lend_sem.at[0],
            device_id={"section": section + 2},
            device_id_type=MESH,
        )

    def for_me(block):
        rows = block_rows(block)

        def add(gradient):
            pair_copy(block).wait_recv()
            mine[rows, :] = (gradient + mine[rows, :].astype(F32)).astype(BF16)

        product(block, core, add)
        if lent:
            pl.when(lender & (block == PLACES.index(LENT)))(lambda: lend_copy().start())
        pl.when(block < 4)(lambda: time_mix_back(block).start())

    blocks_at = tuple(PLACES.index(place) for place in (*range(BLOCKS), LENT))

    def give(kind, group, start):
        size = pieces[kind]
        rows = pl.ds(pl.multiple_of(start, size), size)
        place = start // half if half % sizes[kind] else firsts[kind] // half + group * sizes[kind] // half
        block = lookup(place, blocks_at)
        row = core * half + start - place * half

        def copies(owner, target):
            foreign = kind == 1 and lent and group == counts[1]

            @pl.when((owner == core) & ~jnp.bool_(foreign))
            def _():
                pltpu.make_async_copy(mine.at[rows], target, give_sem.at[0]).start()

            def remote(device):
                return pltpu.make_async_remote_copy(
                    src_ref=mine.at[rows],
                    dst_ref=target,
                    send_sem=give_send.at[0],
                    recv_sem=give_recv.at[0],
                    device_id=device,
                    device_id_type=MESH,
                )

            @pl.when((owner != core) & ~jnp.bool_(foreign))
            def _():
                remote(partner).start()

            if kind == 1 and lent:
                pl.when(foreign)(lambda: remote({"section": section - core + owner - 2}).start())

            if kind == 0:
                remote({"section": section - core + owner, "dp": dp_index + 1 - 2 * y}).start()

        def to_in(owner, column):
            columns = pl.ds(pl.multiple_of(column * channels, channels), channels)
            copies(owner, in_hbm.at[pl.ds(pl.multiple_of(row, size), size), columns])

        def to_out():
            within = (block - 4) * channels + row
            copies(1, out_hbm.at[pl.ds(pl.multiple_of(within, size), size)])

        of_time = block >= C_BLOCKS
        pl.when((block < 4) | (of_time & (place < BLOCKS)))(
            lambda: to_in(jnp.where(of_time, 0, 1), jnp.where(of_time, block - C_BLOCKS, block))
        )
        pl.when((block >= 4) & ~of_time)(to_out)

    sum_sems = ((sum_sem0, sum_send0), (sum_sem1, sum_send1))
    spread_sems = ((spread_sem0, spread_send0), (spread_sem1, spread_send1))

    def piece_rows(kind, group, index):
        start = firsts[kind] + group * sizes[kind] + index * pieces[kind]
        if kind == 0:
            start = start + y * (sizes[0] // 2)
        return start, pl.ds(pl.multiple_of(start, pieces[kind]), pieces[kind])

    def sum_copy(kind, group, direction, step):
        place = landing(kind, direction, group, step)
        receive, send = sum_sems[kind]
        return pltpu.make_async_remote_copy(
            src_ref=place,
            dst_ref=place,
            send_sem=send.at[group, direction, step],
            recv_sem=receive.at[group, direction, step],
            device_id=(right_peer, left_peer)[direction],
            device_id_type=MESH,
        )

    def spread_copy(kind, group, direction, step, index):
        _, rows = piece_rows(kind, group, index)
        receive, send = spread_sems[kind]
        return pltpu.make_async_remote_copy(
            src_ref=mine.at[rows],
            dst_ref=mine.at[rows],
            send_sem=send.at[group, direction, step],
            recv_sem=receive.at[group, direction, step],
            device_id=(right_peer, left_peer)[direction],
            device_id_type=MESH,
        )

    def passing(kind, group, turn):
        for direction in range(2):
            behind = z if direction == 0 else line - 1 - z
            step = turn - behind
            index = line - 1 - step if direction == 0 else step
            place = landing(kind, direction, group, step)
            _, rows = piece_rows(kind, group, index)

            @pl.when((step >= 0) & (behind == 0) & (step < line - 1))
            def _():
                place[...] = mine[rows, :]
                sum_copy(kind, group, direction, step).start()

            @pl.when((step >= 0) & (behind > 0))
            def _():
                sum_copy(kind, group, direction, step).wait_recv()

                @pl.when(turn < line - 1)
                def _():
                    place[...] = (place[...].astype(F32) + mine[rows, :].astype(F32)).astype(BF16)
                    sum_copy(kind, group, direction, step).start()

    def arrived(kind, group):
        _, rows = piece_rows(kind, group, z)
        total = mine[rows, :].astype(F32)
        from_left = landing(kind, 0, group, jnp.minimum(line - 1 - z, line - 2))
        from_right = landing(kind, 1, group, jnp.minimum(z, line - 2))
        mine[rows, :] = total.astype(BF16)

        @pl.when(z == 0)
        def _():
            mine[rows, :] = (total + from_right[...].astype(F32)).astype(BF16)

        @pl.when(z == line - 1)
        def _():
            mine[rows, :] = (total + from_left[...].astype(F32)).astype(BF16)

        @pl.when((z > 0) & (z < line - 1))
        def _():
            mine[rows, :] = (
                total + from_left[...].astype(F32) + from_right[...].astype(F32)
            ).astype(BF16)

    def finished(kind, group, index):
        start, _ = piece_rows(kind, group, index)
        give(kind, group, start)

    def spread_own(kind, group):
        @pl.when(z < line - 1)
        def _():
            spread_copy(kind, group, 0, 0, z).start()

        @pl.when(z > 0)
        def _():
            spread_copy(kind, group, 1, 0, z).start()

        finished(kind, group, z)

    def spreading(kind, group, hop):
        for direction in range(2):
            index = z - hop if direction == 0 else z + hop
            onward = z < line - 1 if direction == 0 else z > 0
            exists = index >= 0 if direction == 0 else index < line

            @pl.when(exists)
            def _():
                spread_copy(kind, group, direction, hop - 1, index).wait_recv()

                @pl.when(onward)
                def _():
                    spread_copy(kind, group, direction, hop, index).start()

                finished(kind, group, index)

    def over(group):
        start = group * sizes[0] + (1 - y) * (sizes[0] // 2)
        return pltpu.make_async_remote_copy(
            src_ref=mine.at[pl.ds(pl.multiple_of(start, pieces[0]), sizes[0] // 2)],
            dst_ref=pair_landing.at[group],
            send_sem=y_send.at[group],
            recv_sem=y_sem.at[group],
            device_id=across,
            device_id_type=MESH,
        )

    def swap(group):
        _, rows = piece_rows(1, group, z)
        return pltpu.make_async_remote_copy(
            src_ref=mine.at[rows],
            dst_ref=cross_landing.at[group],
            send_sem=y_send.at[counts[0] + group],
            recv_sem=y_sem.at[counts[0] + group],
            device_id=across,
            device_id_type=MESH,
        )

    def event0(group, turn):
        @pl.when(turn == 0)
        def _():
            over(group).start()

        @pl.when(turn == 1)
        def _():
            over(group).wait_recv()

            def add(index, _):
                _, rows = piece_rows(0, group, index)
                local = pl.ds(pl.multiple_of(index * pieces[0], pieces[0]), pieces[0])
                arrived_rows = pair_landing.at[group][local, :]
                mine[rows, :] = (mine[rows, :].astype(F32) + arrived_rows.astype(F32)).astype(BF16)
                return 0

            lax.fori_loop(0, line, add, 0)

        @pl.when((turn >= 1) & (turn <= line))
        def _():
            passing(0, group, turn - 1)

        @pl.when(turn == line)
        def _():
            arrived(0, group)
            spread_own(0, group)

        @pl.when(turn > line)
        def _():
            spreading(0, group, turn - line)

    def event1(group, turn):
        if lent:
            pl.when((turn == 0) & (group == counts[1]))(lambda: lend_copy().wait_recv())

        @pl.when(turn < line)
        def _():
            passing(1, group, turn)

        @pl.when(turn == line - 1)
        def _():
            arrived(1, group)
            swap(group).start()

        @pl.when(turn == line)
        def _():
            swap(group).wait()
            _, rows = piece_rows(1, group, z)
            mine[rows, :] = (
                mine[rows, :].astype(F32) + cross_landing[group].astype(F32)
            ).astype(BF16)
            spread_own(1, group)

        @pl.when(turn > line)
        def _():
            spreading(1, group, turn - line)

    spare = firsts[1] + counts[1] * sizes[1] - BLOCKS * half
    if spare:
        mine[pl.ds(BLOCKS * half, spare), :] = jnp.zeros((spare, channels), BF16)
    tables = []
    for events in stage_orders(sections, line, half):
        order = [(COMPUTE, 0, 0)]
        for kind, group, turn in events:
            if kind == COMPUTE:
                order += [(COMPUTE, group + 1, 0)] * (group + 1 < BLOCKS) + [(COMPUTE, group, 1)]
            else:
                order.append((kind, group, turn))
        tables.append([kind * 1024 + group * 64 + turn for kind, group, turn in order])
    most = max(len(table) for table in tables)
    packed = []
    for table in tables:
        filled = table + [0] * (most + most % 2 - len(table))
        packed.append(tuple(a + 4096 * b for a, b in zip(filled[::2], filled[1::2], strict=True)))

    def mine_of(values):
        if len(values) == 1:
            return values[0]
        if len(set(values)) == 1:
            return jnp.int32(values[0])
        return jnp.where(lender, values[0], jnp.where(borrower, values[1], values[2]))

    steps = mine_of([len(table) for table in tables])

    def take(index, _):
        word = jnp.int32(0)
        for at, values in enumerate(zip(*packed, strict=True)):
            word = jnp.where(index // 2 == at, mine_of(values), word)
        code = jnp.where(index % 2 == 0, word % 4096, word // 4096)
        kind, group, turn = code // 1024, code // 64 % 16, code % 64

        @pl.when(kind == COMPUTE)
        def _():
            pl.when(turn == 0)(lambda: for_partner(group))
            pl.when(turn == 1)(lambda: for_me(group))

            @pl.when((turn == 1) & (group == BLOCKS // 2))
            def _():
                small_pair.wait()
                small[0] = totals[core] + small[1]
                lax.fori_loop(1, count, small_start, 0)

        pl.when(kind == 0)(lambda: event0(group, turn))
        pl.when(kind == 1)(lambda: event1(group, turn))
        return 0

    lax.fori_loop(0, steps, take, 0)
    small[0] = lax.fori_loop(1, count, small_add, small[0])
    total_copy = pltpu.make_async_copy(small.at[0], total_hbm, small_sem.at[0])
    total_copy.start()

    def summed_here(kind, group):
        if not lent:
            return group >= 0
        return (borrower | (group != counts[1])) if kind else (~lender | (group != LENT))

    def over_done(group, _):
        pl.when(summed_here(0, group))(lambda: over(group).wait_send())
        return 0

    for block in range(BLOCKS - 2, BLOCKS):
        pair_copy(jnp.int32(block)).wait_send()
    lax.fori_loop(0, counts[0], over_done, 0)
    for kind in range(2):

        def group_done(group, _):
            def step_done(step, _):
                for direction in range(2):
                    behind = z if direction == 0 else line - 1 - z

                    @pl.when((step < line - 1 - behind) & summed_here(kind, group))
                    def _():
                        sum_copy(kind, group, direction, step).wait_send()

                    @pl.when((step <= behind) & (behind < line - 1) & summed_here(kind, group))
                    def _():
                        spread_copy(kind, group, direction, step, 0).wait_send()

                return 0

            return lax.fori_loop(0, line - 1, step_done, 0)

        lax.fori_loop(0, counts[kind] + kind * lent, group_done, 0)

    if lent:
        pl.when(lender)(lambda: lend_copy().wait_send())

    def taken(rows, sem):
        if rows:
            ref = mine.at[pl.ds(0, rows)]
            pltpu.make_async_copy(ref, ref, sem.at[0]).wait()

    paired = [PLACES[block] < PAIRED for block in range(BLOCKS)]
    whole = [half // 2 if pair else half for pair in paired]
    by_kind = (range(C_BLOCKS, BLOCKS), range(C_BLOCKS))
    for own in range(2):
        for last in range(2):
            local = sum(whole[block] for block in by_kind[own])
            crossed = sum(half // 2 for block in range(BLOCKS) if paired[block])
            other = sum(whole[block] for block in by_kind[1 - own])
            if lent and own and last:
                other += half
            elif lent and own:
                crossed -= half // 2
                local -= whole[PLACES.index(LENT)]
            received = len(by_kind[own]) * channels - local

            @pl.when((core == own) & ((section >= 2) == bool(last)))
            def _(local=local, sent=other + crossed, received=received):
                taken(local, give_sem)
                taken(sent, give_send)
                taken(received, give_recv)

    total_copy.wait()


def pool_plan(sections, count, channels, length, slots):
    half, line = channels // 2, count // 2
    pieces, sizes, counts = reduce_plan(line, half)
    counts = (counts[0], counts[1] + lends(sections, line, half))
    heights = (
        counts[0] * sizes[0] + counts[1] * sizes[1],
        2 * half,
        counts[0] * sizes[0] // 2,
        counts[1] * pieces[1],
        *[counts[kind] * (line + 1) * pieces[kind] for kind in range(2)],
    )
    starts = [sum(heights[:at]) for at in range(len(heights))]
    return starts, max(sum(heights), slots * channels + 3 * length)


def chain(sections, count, x, cotangent, w_in, w_out, gain, bias, rates, wkv, state):
    length, channels = x.shape[2:]
    hidden_blocks = w_in.shape[2] // channels
    chunks = length // CHUNK
    anywhere = pl.BlockSpec(memory_space=pl.ANY)
    dma = pltpu.SemaphoreType.DMA
    slots = 9 + hidden_blocks
    line = count // 2
    _, _, counts = reduce_plan(line, channels // 2)
    counts = (counts[0], counts[1] + lends(sections, line, channels // 2))
    hops = [dma((counts[kind], 2, line - 1)) for kind in range(2)]
    _, pool_rows = pool_plan(sections, count, channels, length, slots)
    return pl.pallas_call(
        functools.partial(chain_kernel, sections, length, channels, hidden_blocks, count),
        out_shape=(
            jax.ShapeDtypeStruct((2, length, channels), BF16),
            jax.ShapeDtypeStruct((2, length, channels), BF16),
            jax.ShapeDtypeStruct((2, 8, channels), F32),
            jax.ShapeDtypeStruct((EARLY, length, channels), BF16),
            jax.ShapeDtypeStruct((channels, 4 * channels), BF16),
            jax.ShapeDtypeStruct(((C_BLOCKS - 4) * channels, channels), BF16),
            jax.ShapeDtypeStruct((8, channels), F32),
        ),
        in_specs=[anywhere] * 9,
        out_specs=(anywhere,) * 7,
        scratch_shapes=[
            pltpu.VMEM((pool_rows, channels), BF16),
            pltpu.VMEM((2, EARLY, CHUNK, channels), BF16),
            pltpu.VMEM((LATE, length, channels), BF16),
            pltpu.VMEM((2, length, channels), F32),
            pltpu.VMEM((length, channels), BF16),
            pltpu.VMEM((5, CHUNK, channels), F32),
            pltpu.VMEM((2 * CHUNK, 2 * channels), BF16),
            pltpu.VMEM((2, CHUNK, channels), F32),
            pltpu.VMEM((2, CHUNK, 2 * CHUNK), BF16),
            pltpu.VMEM((2, 1, channels), F32),
            pltpu.VMEM((2, 1, channels), F32),
            pltpu.VMEM((2, 3, 1, channels), F32),
            pltpu.VMEM((2, 2, channels), F32),
            pltpu.VMEM((2, 3, 2, 1, channels), F32),
            pltpu.VMEM((2, length // ROWS, channels), F32),
            pltpu.VMEM((8, channels), F32),
            pltpu.VMEM((8, channels), F32),
            pltpu.VMEM((2, 8, channels), F32),
            pltpu.VMEM((2, 8, 8, channels), F32),
            pltpu.VMEM((2, 8, channels), F32),
            dma((slots,)),
            dma((slots,)),
            dma((2, 5)),
            dma((5,)),
            dma((chunks,)),
            dma((chunks,)),
            dma((chunks,)),
            dma((chunks,)),
            dma((2 + chunks,)),
            dma((2 + chunks,)),
            dma((2 + chunks,)),
            dma((2,)),
            dma((2, chunks)),
            pltpu.VMEM((count + 1, 8, channels), F32),
            pltpu.SemaphoreType.REGULAR,
            dma((4,)),
            dma((BLOCKS,)),
            dma((BLOCKS,)),
            dma((sum(counts),)),
            dma((sum(counts),)),
            hops[0],
            hops[0],
            hops[1],
            hops[1],
            hops[0],
            hops[0],
            hops[1],
            hops[1],
            dma((1,)),
            dma((1,)),
            dma((1,)),
            dma((1,)),
            dma((1,)),
            dma((count + 1,)),
            dma((count + 1,)),
        ],
        compiler_params=pltpu.CompilerParams(
            collective_id=0, has_side_effects=True, vmem_limit_bytes=VMEM_BYTES
        ),
    )(x, cotangent, w_in, w_out, gain, bias, rates, wkv, state)


def finish_kernel(
    in_short,
    out_short,
    outs_in,
    grads_in,
    fin,
    total,
    in_wide,
    out_wide,
    outs,
    grads,
    states,
    normed,
    gain,
    bias,
    rates,
    wkv,
    in_held,
    out_held,
    in_made,
    out_made,
    tokens_held,
    load_sem,
    store_sem,
):
    holds_channel_mix = lax.axis_index("section") % 2 == 1
    sources, targets = (in_short, out_short), (in_wide, out_wide)
    held, made = (in_held, out_held), (in_made, out_made)
    parts = 8
    jobs = [(which, part) for part in range(parts) for which in range(2)]

    def rows_of(which, part):
        tall = sources[which].shape[0] // parts
        return pl.ds(part * tall, tall)

    def load(which, part):
        rows = rows_of(which, part)
        return pltpu.make_async_copy(
            sources[which].at[rows], held[which].at[rows], load_sem.at[which, part]
        )

    def store(which, part):
        rows = rows_of(which, part)
        return pltpu.make_async_copy(
            made[which].at[rows], targets[which].at[rows], store_sem.at[which, part]
        )

    def start(which, part):
        if which:
            pl.when(holds_channel_mix)(lambda: load(which, part).start())
        else:
            load(which, part).start()

    token_loads = [
        pltpu.make_async_copy(source, tokens_held.at[at], load_sem.at[2, at])
        for at, source in enumerate((outs_in, grads_in))
    ]
    token_stores = [
        pltpu.make_async_copy(tokens_held.at[at], target.at[0, :, 0], store_sem.at[2, at])
        for at, target in enumerate((outs, grads))
    ]
    ahead = 6
    for job in jobs[:2]:
        start(*job)
    for copy in token_loads:
        copy.start()
    for job in jobs[2:ahead]:
        start(*job)
    for micro in range(2):
        normed[0, micro] = fin[micro, 0:1]
        for row in range(2):
            states[0, row, micro] = fin[micro, 1 + row : 2 + row]
    gain[...] = total[GAIN : GAIN + 1]
    bias[...] = total[BIAS : BIAS + 1]
    for row in range(3):
        rates[row] = total[RATES + row : RATES + row + 1]
    wkv[0] = total[DECAY : DECAY + 2]
    for at, (which, part) in enumerate(jobs):
        tall = sources[which].shape[0] // parts
        step = 32 if which == 0 else 96

        def widen(index, _):
            rows = pl.ds(pl.multiple_of(part * tall + index * step, step), step)
            made[which][rows, :] = held[which][rows, :].astype(F32)
            return 0

        def clear(index, _):
            rows = pl.ds(pl.multiple_of(part * tall + index * step, step), step)
            made[which][rows, :] = jnp.zeros((step, made[which].shape[1]), F32)
            return 0

        def widened():
            load(which, part).wait()
            lax.fori_loop(0, tall // step, widen, 0)

        if which:
            pl.when(holds_channel_mix)(widened)

            @pl.when(~holds_channel_mix)
            def _():
                lax.fori_loop(0, tall // step, clear, 0)

        else:
            widened()
        if at + ahead < len(jobs):
            start(*jobs[at + ahead])
        store(which, part).start()
        if at < 2:
            token_loads[at].wait()
            token_stores[at].start()
    for job in jobs:
        store(*job).wait()
    for copy in token_stores:
        copy.wait()


def finished_outputs(in_short, out_short, outs, grads, fin, total):
    length, channels = outs.shape[1:]
    whole = pl.BlockSpec(memory_space=pltpu.VMEM)
    anywhere = pl.BlockSpec(memory_space=pl.ANY)

    def shape(*sizes, dtype=F32):
        return jax.ShapeDtypeStruct(sizes, dtype)

    in_wide, out_wide, *rest = pl.pallas_call(
        finish_kernel,
        out_shape=(
            shape(*in_short.shape),
            shape(*out_short.shape),
            shape(1, 2, 1, length, channels, dtype=BF16),
            shape(1, 2, 1, length, channels, dtype=BF16),
            shape(1, 2, 2, 1, channels),
            shape(1, 2, 1, channels),
            shape(1, channels),
            shape(1, channels),
            shape(3, 1, channels),
            shape(1, 2, channels),
        ),
        in_specs=[anywhere] * 4 + [whole] * 2,
        out_specs=(anywhere,) * 4 + (whole,) * 6,
        scratch_shapes=[
            pltpu.VMEM(in_short.shape, BF16),
            pltpu.VMEM(out_short.shape, BF16),
            pltpu.VMEM(in_short.shape, F32),
            pltpu.VMEM(out_short.shape, F32),
            pltpu.VMEM((2, 2, length, channels), BF16),
            pltpu.SemaphoreType.DMA((3, 8)),
            pltpu.SemaphoreType.DMA((3, 8)),
        ],
        compiler_params=pltpu.CompilerParams(vmem_limit_bytes=VMEM_BYTES),
    )(in_short, out_short, outs, grads, fin, total)
    *rest, rates, wkv = rest
    return in_wide, out_wide, *rest, jnp.swapaxes(rates, 0, 1), wkv


def shards(
    block_input,
    carried_state,
    output_cotangent,
    in_weight,
    out_weight,
    norm_gain,
    norm_bias,
    mix_rates,
    wkv_params,
):
    sections = lax.axis_size("section")
    outs, grads, fin, _, in_short, out_short, total = chain(
        sections,
        lax.axis_size("dp"),
        block_input,
        output_cotangent,
        in_weight,
        out_weight,
        norm_gain,
        norm_bias,
        jnp.swapaxes(mix_rates, 0, 1),
        wkv_params,
        carried_state,
    )
    in_grad, out_grad, outs, grads, states, normed, gain, bias, rates, wkv = finished_outputs(
        in_short, out_short, outs, grads, fin, total
    )
    return outs, states, normed, grads, in_grad[None], out_grad[None], gain, bias, rates, wkv


def solution(mesh):
    return jax.shard_map(
        shards,
        mesh=mesh,
        in_specs=(
            P(None, "dp", None, None),
            P("section", None, None, "dp", None),
            P(None, "dp", None, None),
            P("section", None, None),
            P("section", None, None),
            P("section", None),
            P("section", None),
            P("section", None, None),
            P("section", None, None),
        ),
        out_specs=(
            P("section", None, "dp", None, None),
            P("section", None, None, "dp", None),
            P("section", None, "dp", None),
            P("section", None, "dp", None, None),
            P("section", None, None),
            P("section", None, None),
            P("section", None),
            P("section", None),
            P("section", None, None),
            P("section", None, None),
        ),
        check_vma=False,
    )
```

```python
import functools

import jax
import jax.numpy as jnp
from jax import lax
from jax.experimental import pallas as pl
from jax.experimental.pallas import tpu as pltpu
from jax.sharding import PartitionSpec as P

MESH = pl.DeviceIdType.MESH
F32 = jnp.float32
BF16 = jnp.bfloat16
CHUNK = 256
ROWS = 64
UNROLL = 2
TALL = 64
VMEM_BYTES = (64 << 20) - (128 << 10)

T_MIX0, T_MIX2, T_MIX1, T_GATED, C_MIX0, C_MIX1 = 0, 1, 2, 3, 4, 5
EARLY = 6
T_DK, T_DV, T_DQ, T_G, C_DKV, C_DQ, C_HID, C_DPRE = 0, 1, 2, 3, 4, 5, 6, 10
LATE = 14
GAIN, BIAS, RATES, DECAY, BONUS = 0, 1, 2, 5, 6


def nn(left, right):
    return jnp.dot(left, right, preferred_element_type=F32)


def nt(left, right):
    return lax.dot_general(left, right, (((1,), (1,)), ((), ())), preferred_element_type=F32)


def tn(left, right):
    return lax.dot_general(left, right, (((0,), (0,)), ((), ())), preferred_element_type=F32)


class Stack:
    def __init__(self, buffer, start, *heights):
        self.buffer, self.start, self.heights = buffer, start, heights

    @property
    def at(self):
        return Places(self)

    def __getitem__(self, index):
        return self.at[index][...]


class Places:
    def __init__(self, stack):
        self.stack = stack

    def __getitem__(self, index):
        index = index if isinstance(index, tuple) else (index,)
        start, height = self.stack.start, self.stack.heights[-1]
        for place, tall in zip(index, self.stack.heights, strict=True):
            start = start + place * tall
        if not isinstance(start, int):
            start = pl.multiple_of(start, 16)
        return self.stack.buffer.at[pl.ds(start, height)]


def folded(rows):
    total = rows[0:8]
    for start in range(8, rows.shape[0], 8):
        total = total + rows[start : start + 8]
    return total


def chain_kernel(
    sections,
    length,
    channels,
    hidden_blocks,
    count,
    x_hbm,
    cot_hbm,
    w_in_hbm,
    w_out_hbm,
    gain_hbm,
    bias_hbm,
    rates_hbm,
    wkv_hbm,
    state_hbm,
    outs_hbm,
    grads_hbm,
    fin_hbm,
    early_hbm,
    in_hbm,
    out_hbm,
    total_hbm,
    pool,
    early,
    kept,
    states,
    upstream,
    wide,
    pairs,
    tables,
    triangles,
    gains,
    biases,
    rates,
    wkvs,
    starts,
    previous,
    carry,
    carry_next,
    fin,
    sums,
    totals,
    weight_sem,
    weight_send,
    small_sem,
    small_send,
    entry_sem,
    entry_send,
    up_sem,
    up_send,
    out_sem,
    out_send,
    out_recv,
    early_sem,
    *reducing,
):
    section = lax.axis_index("section")
    dp_index = lax.axis_index("dp")
    core = section % 2
    stage = section // 2
    stages = sections // 2
    partner = {"section": section + 1 - 2 * core}
    chunks = length // CHUNK
    blocks = CHUNK // ROWS
    tall_blocks = CHUNK // TALL
    time_blocks = 4
    last_stage = stage == stages - 1
    weights = Stack(pool, 0, channels)
    after_weights = (9 + hidden_blocks) * channels
    entry = pool.at[pl.ds(after_weights, length)]
    hs = Stack(pool, after_weights + length, length)
    mid, top = hs.at[0], hs.at[1]

    barrier = pltpu.get_barrier_semaphore()
    across = {"dp": dp_index + 1 - 2 * (dp_index % 2)}
    for device in (partner, partner | across):
        pl.semaphore_signal(barrier, inc=1, device_id=device, device_id_type=MESH)

    def greet(offset, _):
        peer = {"dp": lax.rem(dp_index + offset, count)}
        pl.semaphore_signal(barrier, inc=1, device_id=peer, device_id_type=MESH)
        return 0

    lax.fori_loop(1, count, greet, 0)

    @pl.when(stage > 0)
    def _():
        for other in (section - 2, section - 1 - 2 * core):
            pl.semaphore_signal(barrier, inc=1, device_id={"section": other}, device_id_type=MESH)

    @pl.when(stage < stages - 1)
    def _():
        for other in (section + 2, section + 3 - 2 * core):
            pl.semaphore_signal(barrier, inc=1, device_id={"section": other}, device_id_type=MESH)

    def entry_copy(chunk):
        rows = pl.ds(chunk * CHUNK, CHUNK)
        return pltpu.make_async_copy(
            x_hbm.at[core, 0, rows], entry.at[rows], entry_sem.at[chunk]
        )

    def up_copy(chunk):
        rows = pl.ds(chunk * CHUNK, CHUNK)
        return pltpu.make_async_copy(
            cot_hbm.at[core, 0, rows], upstream.at[rows], up_sem.at[chunk]
        )

    @pl.when(stage == 0)
    def _():
        for chunk in range(chunks):
            entry_copy(chunk).start()

    @pl.when(last_stage)
    def _():
        for chunk in range(chunks):
            up_copy(chunk).start()

    small_pairs = (
        (gain_hbm, gains.at[core]),
        (bias_hbm, biases.at[core]),
        (rates_hbm, rates.at[core]),
        (wkv_hbm.at[0], wkvs.at[core]),
        (state_hbm.at[0], starts.at[core]),
    )
    small_copies = [
        pltpu.make_async_copy(source, target, small_sem.at[0, at])
        for at, (source, target) in enumerate(small_pairs)
    ]
    for copy in small_copies:
        copy.start()

    def in_block(index):
        return w_in_hbm.at[0, :, pl.ds(index * channels, channels)]

    def out_block(index):
        return w_out_hbm.at[0, pl.ds(index * channels, channels), :]

    for index in range(4):
        slot = core * time_blocks + index
        pltpu.make_async_copy(in_block(index), weights.at[slot], weight_sem.at[slot]).start()

    @pl.when(core == 1)
    def _():
        for index in range(hidden_blocks + 1):
            slot = 8 + index
            pltpu.make_async_copy(
                out_block(index), weights.at[slot], weight_sem.at[slot]
            ).start()

    has_previous = jnp.where(stage > 0, 1, 0)
    has_next = jnp.where(stage < stages - 1, 1, 0)
    pl.semaphore_wait(barrier, 1 + count + 2 * (has_previous + has_next))

    small_remotes = [
        pltpu.make_async_remote_copy(
            src_ref=source,
            dst_ref=target,
            send_sem=small_send.at[at],
            recv_sem=small_sem.at[1, at],
            device_id=partner,
            device_id_type=MESH,
        )
        for at, (source, target) in enumerate(small_pairs)
    ]

    def in_remote(index):
        slot = core * time_blocks + index
        return pltpu.make_async_remote_copy(
            src_ref=in_block(index),
            dst_ref=weights.at[slot],
            send_sem=weight_send.at[slot],
            recv_sem=weight_sem.at[slot],
            device_id=partner,
            device_id_type=MESH,
        )

    def out_remote(index):
        slot = 8 + index
        return pltpu.make_async_remote_copy(
            src_ref=out_block(index),
            dst_ref=weights.at[slot],
            send_sem=weight_send.at[slot],
            recv_sem=weight_sem.at[slot],
            device_id=partner,
            device_id_type=MESH,
        )

    for copy in small_remotes:
        copy.start()
    for index in range(4):
        in_remote(index).start()

    @pl.when(core == 1)
    def _():
        for index in (hidden_blocks, *range(hidden_blocks)):
            out_remote(index).start()

    row_at = lax.broadcasted_iota(jnp.int32, (CHUNK, 2 * CHUNK), 0)
    column_at = lax.broadcasted_iota(jnp.int32, (CHUNK, 2 * CHUNK), 1)
    column_at = jnp.where(column_at >= CHUNK, column_at - CHUNK, column_at)
    triangles[0] = jnp.where(row_at > column_at, 1.0, 0.0).astype(BF16)
    triangles[1] = jnp.where(row_at < column_at, 1.0, 0.0).astype(BF16)
    sums[...] = jnp.zeros_like(sums)
    fin[...] = jnp.zeros_like(fin)

    for copy in small_copies:
        copy.wait()
    for copy in small_remotes:
        copy.wait_recv()

    rate = jnp.exp(wkvs[0, 0:1, :])
    step = jnp.exp(-rate)
    lift = jnp.exp(wkvs[0, 1:2, :])

    def table_rows(index, _):
        start = pl.multiple_of(index * ROWS, ROWS)
        place = (lax.broadcasted_iota(jnp.int32, (ROWS, channels), 0) + start).astype(F32)
        tables[0, pl.ds(start, ROWS), :] = jnp.exp(-(CHUNK - 1.0 - place) * rate)
        tables[1, pl.ds(start, ROWS), :] = jnp.exp(-place * rate)
        return 0

    lax.fori_loop(0, blocks, table_rows, 0)

    for row in range(3):
        carry[row : row + 1] = starts[0, row, core]
    carry[3:4] = starts[1, 0, core]

    def weight_wait(slot):
        pltpu.make_async_copy(weights.at[slot], weights.at[slot], weight_sem.at[slot]).wait()

    def stats(tokens):
        center = tokens - jnp.mean(tokens, axis=-1, keepdims=True)
        spread = jnp.mean(center * center, axis=-1, keepdims=True)
        root = lax.rsqrt(spread + 1e-05)
        return center * root, root

    row_index = lax.broadcasted_iota(jnp.int32, (ROWS, channels), 0)
    tall_index = lax.broadcasted_iota(jnp.int32, (TALL, channels), 0)

    def token_mix(kind, source, base, side, slots, carry_row):
        gain, bias = gains[kind], biases[kind]

        def body(index, before):
            start = pl.multiple_of(base + index * ROWS, ROWS)
            rows = pl.ds(start, ROWS)
            unit, _ = stats(source[rows, :].astype(F32))
            normed = unit * gain + bias
            previous[kind, pl.ds(start // ROWS, 1), :] = before
            shifted = jnp.where(
                row_index == 0, jnp.broadcast_to(before, normed.shape), pltpu.roll(normed, 1, 0)
            )
            gap = normed - shifted
            for rate_row, slot in slots:
                early[side, slot, pl.ds(pl.multiple_of(index * ROWS, ROWS), ROWS), :] = (
                    shifted + gap * rates[kind, rate_row]
                ).astype(BF16)
            return normed[ROWS - 1 : ROWS, :]

        carry[carry_row : carry_row + 1] = lax.fori_loop(
            0, blocks, body, carry[carry_row : carry_row + 1], unroll=UNROLL
        )

    def early_copy(chunk):
        rows = pl.ds(pl.multiple_of(chunk * CHUNK, CHUNK), CHUNK)
        side = chunk % 2
        return pltpu.make_async_copy(
            early.at[side], early_hbm.at[:, rows], early_sem.at[side]
        )

    def forward_chunk(chunk, _):
        base = pl.multiple_of(chunk * CHUNK, CHUNK)
        rows = pl.ds(base, CHUNK)
        side = chunk % 2

        @pl.when(chunk >= 2)
        def _():
            early_copy(chunk - 2).wait()

        pltpu.make_async_copy(entry.at[rows], entry.at[rows], entry_sem.at[chunk]).wait()

        token_mix(0, entry, base, side, ((0, T_MIX0), (2, T_MIX2), (1, T_MIX1)), 0)

        for slot in range(3):

            @pl.when(chunk == 0)
            def _():
                weight_wait(slot)

            wide[slot] = nn(early[side, slot], weights[slot])

        def weighted(index, _):
            start = pl.multiple_of(index * TALL, TALL)
            local = pl.ds(start, TALL)
            whole = pl.ds(pl.multiple_of(base + start, TALL), TALL)
            value = wide[1, local, :]
            power = jnp.exp(wide[0, local, :])
            wide[0, local, :] = power
            scaled = power * tables[0, local, :]
            pairs[local, pl.ds(0, channels)] = (scaled * value).astype(BF16)
            pairs[local, pl.ds(channels, channels)] = scaled.astype(BF16)
            kept[T_DK, whole, :] = power.astype(BF16)
            kept[T_DV, whole, :] = value.astype(BF16)
            return 0

        lax.fori_loop(0, tall_blocks, weighted, 0)
        wide[3] = nn(triangles[0, :, pl.ds(0, CHUNK)], pairs[pl.ds(0, CHUNK), pl.ds(0, channels)])
        wide[4] = nn(
            triangles[0, :, pl.ds(0, CHUNK)], pairs[pl.ds(0, CHUNK), pl.ds(channels, channels)]
        )
        upper, lower = carry[1:2], carry[2:3]

        def averaged(index, _):
            start = pl.multiple_of(index * TALL, TALL)
            local = pl.ds(start, TALL)
            whole = pl.ds(pl.multiple_of(base + start, TALL), TALL)
            place = (tall_index + start).astype(F32)
            grown = jnp.exp((CHUNK - place) * rate)
            faded = tables[1, local, :]
            power, value = wide[0, local, :], wide[1, local, :]
            before_upper = grown * wide[3, local, :] + faded * upper
            before_lower = grown * wide[4, local, :] + faded * lower
            now = power * lift
            average = (before_upper + now * value) / (before_lower + now)
            gate = jax.nn.sigmoid(wide[2, local, :])
            states[0, whole, :] = before_upper
            states[1, whole, :] = before_lower
            kept[T_DQ, whole, :] = gate.astype(BF16)
            early[side, T_GATED, local, :] = (gate * average).astype(BF16)
            tail = slice(TALL - 8, TALL)
            after_upper = step * before_upper[tail] + power[tail] * value[tail]
            after_lower = step * before_lower[tail] + power[tail]
            carry_next[0:1] = after_upper[7:8]
            carry_next[1:2] = after_lower[7:8]
            return 0

        lax.fori_loop(0, tall_blocks, averaged, 0)
        carry[1:3] = carry_next[0:2]

        @pl.when(chunk == 0)
        def _():
            weight_wait(3)

        mid[rows, :] = (
            entry[rows, :].astype(F32) + nn(early[side, T_GATED], weights[3])
        ).astype(BF16)

        token_mix(1, mid, base, side, ((0, C_MIX0), (1, C_MIX1)), 3)

        for index in range(hidden_blocks):

            @pl.when(chunk == 0)
            def _():
                weight_wait(4 + index)

            pre = nn(early[side, C_MIX0], weights[4 + index])
            kept[C_HID + index, rows, :] = jnp.square(jnp.maximum(pre, 0.0)).astype(BF16)

        @pl.when(chunk == 0)
        def _():
            weight_wait(8 + hidden_blocks)

        early_copy(chunk).start()
        wide[1] = nn(early[side, C_MIX1], weights[8 + hidden_blocks])

        @pl.when(chunk == 0)
        def _():
            for index in range(hidden_blocks):
                weight_wait(8 + index)

        total = nn(kept[C_HID, rows, :], weights[8])
        for index in range(1, hidden_blocks):
            total = total + nn(kept[C_HID + index, rows, :], weights[8 + index])
        wide[0] = total

        def joined(index, _):
            start = pl.multiple_of(index * TALL, TALL)
            local = pl.ds(start, TALL)
            whole = pl.ds(pl.multiple_of(base + start, TALL), TALL)
            gate = jax.nn.sigmoid(wide[1, local, :])
            value = wide[0, local, :]
            kept[C_DKV, whole, :] = gate.astype(BF16)
            kept[C_DQ, whole, :] = value.astype(BF16)
            top[whole, :] = (mid[whole, :].astype(F32) + gate * value).astype(BF16)
            return 0

        lax.fori_loop(0, tall_blocks, joined, 0)

        @pl.when(stage < stages - 1)
        def _():
            entry_remote(chunk).start()

        return 0

    def entry_remote(chunk):
        rows = pl.ds(pl.multiple_of(chunk * CHUNK, CHUNK), CHUNK)
        return pltpu.make_async_remote_copy(
            src_ref=top.at[rows],
            dst_ref=entry.at[rows],
            send_sem=entry_send.at[chunk],
            recv_sem=entry_sem.at[chunk],
            device_id={"section": section + 2},
            device_id_type=MESH,
        )

    def up_remote(chunk):
        rows = pl.ds(pl.multiple_of(chunk * CHUNK, CHUNK), CHUNK)
        return pltpu.make_async_remote_copy(
            src_ref=upstream.at[rows],
            dst_ref=upstream.at[rows],
            send_sem=up_send.at[chunk],
            recv_sem=up_sem.at[chunk],
            device_id={"section": section - 2},
            device_id_type=MESH,
        )

    lax.fori_loop(0, chunks, forward_chunk, 0)
    early_copy(chunks - 2).wait()
    early_copy(chunks - 1).wait()

    def mix_back(side, chunk):
        return pltpu.make_async_copy(
            early_hbm.at[C_MIX0 + side, pl.ds(chunk * CHUNK, CHUNK)],
            early.at[side, chunk],
            back_sem.at[side, chunk],
        )

    back_sem, reducing = reducing[0], reducing[1:]
    for side in range(2):
        for chunk in range(chunks):
            mix_back(side, chunk).start()

    fin[0, 0:1] = carry[0:1]
    fin[0, 1:3] = carry[1:3]
    fin[1, 0:1] = carry[3:4]

    def to_owner(index, own_src, other_src, dst):
        own = pltpu.make_async_copy(own_src, dst, out_sem.at[index])
        other = pltpu.make_async_remote_copy(
            src_ref=other_src,
            dst_ref=dst,
            send_sem=out_send.at[index],
            recv_sem=out_recv.at[index],
            device_id=partner,
            device_id_type=MESH,
        )
        return own, other

    outs_copies = to_owner(0, hs.at[core], hs.at[1 - core], outs_hbm.at[core])
    fin_copies = to_owner(1, fin.at[core], fin.at[1 - core], fin_hbm.at[core])
    for copy in outs_copies + fin_copies:
        copy.start()

    carry[0:4] = jnp.zeros((4, channels), F32)

    def norm_back(kind, source, base, mixes, above, target, carry_row):
        gain, bias = gains[kind], biases[kind]

        def body(index, after):
            back = blocks - 1 - index
            local = pl.ds(pl.multiple_of(back * ROWS, ROWS), ROWS)
            start = pl.multiple_of(base + back * ROWS, ROWS)
            rows = pl.ds(start, ROWS)
            unit, root = stats(source[rows, :].astype(F32))
            normed = unit * gain + bias
            before = previous[kind, pl.ds(start // ROWS, 1), :]
            shifted = jnp.where(
                row_index == 0, jnp.broadcast_to(before, normed.shape), pltpu.roll(normed, 1, 0)
            )
            gap = normed - shifted
            straight = jnp.zeros_like(normed)
            total = jnp.zeros_like(normed)
            for rate_row, slot in mixes:
                mix = wide[slot, local, :]
                straight = straight + mix * rates[kind, rate_row]
                total = total + mix
                sums[kind, RATES + rate_row] += folded(mix * gap)
            late = total - straight
            moved = jnp.where(
                row_index == ROWS - 1,
                jnp.broadcast_to(after, late.shape),
                pltpu.roll(late, ROWS - 1, 0),
            )
            d_normed = straight + moved
            sums[kind, GAIN] += folded(d_normed * unit)
            sums[kind, BIAS] += folded(d_normed)
            d_unit = d_normed * gain
            d_tokens = (
                d_unit
                - jnp.mean(d_unit, axis=-1, keepdims=True)
                - unit * jnp.mean(d_unit * unit, axis=-1, keepdims=True)
            ) * root
            target[rows, :] = (above[rows, :].astype(F32) + d_tokens).astype(BF16)
            return late[0:1, :]

        carry[carry_row : carry_row + 1] = lax.fori_loop(
            0, blocks, body, carry[carry_row : carry_row + 1], unroll=UNROLL
        )

    def grad_copies(chunk, kind):
        rows = pl.ds(pl.multiple_of(chunk * CHUNK, CHUNK), CHUNK)
        sources = (upstream.at[rows], kept.at[T_G, rows])
        return to_owner(
            2 + chunk, sources[kind], sources[1 - kind], grads_hbm.at[core, rows]
        )

    def backward_chunk(turn, _):
        chunk = chunks - 1 - turn
        base = pl.multiple_of(chunk * CHUNK, CHUNK)
        rows = pl.ds(base, CHUNK)
        pltpu.make_async_copy(upstream.at[rows], upstream.at[rows], up_sem.at[chunk]).wait()

        def split(index, _):
            whole = pl.ds(pl.multiple_of(base + index * TALL, TALL), TALL)
            above = upstream[whole, :].astype(F32)
            gate = kept[C_DKV, whole, :].astype(F32)
            value = kept[C_DQ, whole, :].astype(F32)
            d_value = above * gate
            kept[C_DKV, whole, :] = d_value.astype(BF16)
            kept[C_DQ, whole, :] = (d_value * value * (1.0 - gate)).astype(BF16)
            return 0

        lax.fori_loop(0, tall_blocks, split, 0)

        for index in range(hidden_blocks):
            d_hidden = nt(kept[C_DKV, rows, :], weights[8 + index])
            slope = jnp.sqrt(kept[C_HID + index, rows, :].astype(F32))
            kept[C_DPRE + index, rows, :] = (d_hidden * (2.0 * slope)).astype(BF16)
        total = nt(kept[C_DPRE, rows, :], weights[4])
        for index in range(1, hidden_blocks):
            total = total + nt(kept[C_DPRE + index, rows, :], weights[4 + index])
        wide[0] = total
        wide[1] = nt(kept[C_DQ, rows, :], weights[8 + hidden_blocks])
        norm_back(1, mid, base, ((0, 0), (1, 1)), upstream, kept.at[T_G], 3)

        wide[0] = nt(kept[T_G, rows, :], weights[3])

        def inputs(index, _):
            start = pl.multiple_of(index * TALL, TALL)
            local = pl.ds(start, TALL)
            whole = pl.ds(pl.multiple_of(base + start, TALL), TALL)
            power = kept[T_DK, whole, :].astype(F32)
            value = kept[T_DV, whole, :].astype(F32)
            gate = kept[T_DQ, whole, :].astype(F32)
            now = power * lift
            inverse = 1.0 / (states[1, whole, :] + now)
            average = (states[0, whole, :] + now * value) * inverse
            d_average = wide[0, local, :] * gate
            kept[T_DQ, whole, :] = (d_average * average * (1.0 - gate)).astype(BF16)
            unit = d_average * inverse
            wide[1, local, :] = unit
            wide[2, local, :] = average
            scaled = unit * tables[1, local, :]
            for column, term in ((0, scaled), (channels, -scaled * average)):
                high = term.astype(BF16)
                pairs[local, pl.ds(column, channels)] = high
                pairs[pl.ds(pl.multiple_of(CHUNK + start, TALL), TALL), pl.ds(column, channels)] = (
                    term - high.astype(F32)
                ).astype(BF16)
            return 0

        lax.fori_loop(0, tall_blocks, inputs, 0)
        wide[3] = nn(triangles[1], pairs[:, pl.ds(0, channels)])
        wide[4] = nn(triangles[1], pairs[:, pl.ds(channels, channels)])
        alpha_after, beta_after = carry[1:2], carry[2:3]

        def outputs(index, _):
            start = pl.multiple_of((tall_blocks - 1 - index) * TALL, TALL)
            local = pl.ds(start, TALL)
            whole = pl.ds(pl.multiple_of(base + start, TALL), TALL)
            place = (tall_index + start).astype(F32)
            grown = jnp.exp((place + 1.0) * rate)
            faded = tables[0, local, :]
            alpha = grown * wide[3, local, :] + faded * alpha_after
            beta = grown * wide[4, local, :] + faded * beta_after
            unit, average = wide[1, local, :], wide[2, local, :]
            power = kept[T_DK, whole, :].astype(F32)
            value = kept[T_DV, whole, :].astype(F32)
            weighed = unit * (power * lift)
            own = weighed * (value - average)
            kept[T_DK, whole, :] = (own + power * (alpha * value + beta)).astype(BF16)
            kept[T_DV, whole, :] = (weighed + power * alpha).astype(BF16)
            sums[0, BONUS] += folded(own)
            sums[0, DECAY] += folded(
                alpha * states[0, whole, :] + beta * states[1, whole, :]
            )
            carry_next[0:1] = unit[0:1] + step * alpha[0:1]
            carry_next[1:2] = step * beta[0:1] - unit[0:1] * average[0:1]
            return 0

        lax.fori_loop(0, tall_blocks, outputs, 0)
        carry[1:3] = carry_next[0:2]
        wide[0] = nt(kept[T_DK, rows, :], weights[0])
        wide[1] = nt(kept[T_DQ, rows, :], weights[2])
        wide[2] = nt(kept[T_DV, rows, :], weights[1])
        norm_back(
            0, entry, base, ((0, 0), (1, 1), (2, 2)), kept.at[T_G], upstream, 0
        )

        @pl.when(stage > 0)
        def _():
            up_remote(chunk).start()

        for kind in range(2):

            @pl.when(core == kind)
            def _():
                for copy in grad_copies(chunk, kind):
                    copy.start()

        return 0

    lax.fori_loop(0, chunks, backward_chunk, 0)

    sums[0, DECAY] = sums[0, DECAY] * (-rate * step)
    for kind in range(2):
        for row in range(7):
            totals[kind, row : row + 1] = jnp.sum(sums[kind, row], axis=0, keepdims=True)
        totals[kind, 7:8] = jnp.zeros((1, channels), F32)

    for copy in outs_copies:
        copy.wait()

    @pl.when(stage < stages - 1)
    def _():
        for chunk in range(chunks):
            entry_remote(chunk).wait_send()

    reduce_phase(
        sections, count, channels, pool, early, kept, early_hbm, totals, mix_back, in_hbm, out_hbm, total_hbm, *reducing
    )

    for copy in fin_copies:
        copy.wait()
    for chunk in range(chunks):
        for copy in grad_copies(chunk, 0):
            copy.wait()
    for copy in small_remotes:
        copy.wait_send()
    for index in range(4):
        in_remote(index).wait_send()

    @pl.when(core == 1)
    def _():
        for index in range(hidden_blocks + 1):
            out_remote(index).wait_send()

    @pl.when(stage > 0)
    def _():
        for chunk in range(chunks):
            up_remote(chunk).wait_send()


C_BLOCKS = 9
T_BLOCKS = 4
BLOCKS = C_BLOCKS + T_BLOCKS
PLACES = (8, 9, 0, 1, 2, 10, 3, 11, 4, 5, 6, 12, 7)
PAIRED = 8
LENT = 3


def lookup(index, table):
    value = jnp.int32(table[0])
    for at, entry in enumerate(table[1:], 1):
        value = jnp.where(index == at, entry, value)
    return value


def reduce_plan(line, half):
    pieces = (max(16, half // (2 * line)), max(16, half // line))
    sizes = (2 * line * pieces[0], line * pieces[1])
    counts = (-(-PAIRED * half // sizes[0]), -(-(BLOCKS - PAIRED) * half // sizes[1]))
    return pieces, sizes, counts


def lends(sections, line, half):
    return sections == 4 and line == 4 and reduce_plan(line, half)[1:] == ((half, half), (8, 5))


def ready_times(first, size, count, half):
    made = {place: time for time, place in enumerate(PLACES)}
    times = []
    for group in range(count):
        begin, end = first + group * size, first + (group + 1) * size
        times.append(
            max(made[place] for place in range(BLOCKS) if place * half < end and begin < (place + 1) * half)
        )
    return tuple(times)


COMPUTE = 2
ORDERS_OF_FOUR = (
    (
        2000, 1000, 2010, 1010, 2020, 1001, 2030, 2040, 20, 1011, 1002, 2050, 1020, 2060, 2070, 1003,
        21, 1012, 2080, 40, 1021, 2090, 1004, 2100, 22, 1013, 2110, 1022, 41, 10, 1005, 2120,
        1014, 23, 1023, 42, 1006, 11, 1040, 1015, 24, 1024, 43, 1007, 50, 1041, 0, 12,
        1016, 1025, 25, 51, 1042, 1, 1017, 52, 1026, 13, 26, 1043, 2, 53, 1027, 27,
        3, 60, 14, 1044, 4, 70, 1030, 15, 61, 1045, 5, 54, 1031, 16, 62, 1046,
        71, 6, 55, 1047, 1032, 72, 17, 56, 7, 63, 57, 73, 1033, 44, 64, 74,
        45, 65, 75, 46, 1034, 76, 66, 47, 1035, 77, 67, 1036, 1037,
    ),
    (
        2000, 1000, 2010, 1010, 2020, 1001, 2030, 2040, 20, 1011, 1002, 2050, 1020, 2060, 2070, 1003,
        21, 1012, 2080, 40, 1021, 2090, 2100, 1004, 22, 1013, 2110, 1022, 41, 10, 2120, 1005,
        1014, 23, 1023, 42, 1006, 11, 1040, 1015, 24, 1024, 43, 1007, 50, 1041, 0, 12,
        1016, 1025, 25, 1050, 51, 1042, 1, 30, 1017, 52, 1026, 1051, 13, 26, 1043, 2,
        53, 1027, 31, 1052, 27, 3, 60, 14, 32, 1044, 4, 1053, 1030, 15, 61, 33,
        70, 1045, 5, 1054, 54, 1031, 16, 62, 1046, 71, 6, 1055, 55, 1047, 1032, 72,
        17, 56, 63, 1056, 7, 57, 73, 1033, 34, 44, 64, 1057, 35, 74, 45, 65,
        75, 36, 46, 1034, 76, 66, 37, 47, 1035, 77, 67, 1036, 1037,
    ),
    (
        2000, 1000, 2010, 1010, 2020, 1001, 2030, 2040, 20, 1011, 1002, 2050, 1020, 2060, 2070, 1003,
        21, 1012, 2080, 40, 1021, 2090, 2100, 1004, 22, 1013, 2110, 1022, 41, 10, 2120, 1005,
        1014, 23, 1023, 42, 1006, 11, 1040, 1015, 24, 1024, 43, 1007, 50, 1041, 0, 12,
        1016, 1025, 25, 51, 1042, 1, 30, 1017, 52, 1026, 13, 26, 1043, 2, 53, 1027,
        31, 27, 3, 60, 14, 32, 1044, 4, 1030, 15, 61, 33, 70, 1045, 5, 54,
        1031, 16, 62, 1046, 71, 6, 55, 1047, 1032, 72, 17, 56, 63, 7, 57, 73,
        1033, 34, 44, 64, 35, 74, 45, 65, 75, 36, 46, 1034, 76, 66, 37, 47,
        1035, 77, 67, 1036, 1037,
    ),
)


def event_order(line, half):
    _, sizes, counts = reduce_plan(line, half)
    firsts = (0, counts[0] * sizes[0])
    steps = [(block, 0, (COMPUTE, block, 0)) for block in range(BLOCKS)]
    for kind in range(2):
        times = ready_times(firsts[kind], sizes[kind], counts[kind], half)
        for group, time in enumerate(times):
            steps += [(time + turn, 1 + kind, (kind, group, turn)) for turn in range(2 * line)]
    return [step for _, _, step in sorted(steps)]


def stage_orders(sections, line, half):
    if lends(sections, line, half):
        return [[(code // 1000, code // 10 % 100, code % 10) for code in order] for order in ORDERS_OF_FOUR]
    return [event_order(line, half)]


def reduce_phase(
    sections,
    count,
    channels,
    pool,
    early,
    kept,
    early_hbm,
    totals,
    mix_back,
    in_hbm,
    out_hbm,
    total_hbm,
    small,
    ready_sem,
    back_sem,
    pair_sem,
    pair_send,
    y_sem,
    y_send,
    sum_sem0,
    sum_send0,
    sum_sem1,
    sum_send1,
    spread_sem0,
    spread_send0,
    spread_sem1,
    spread_send1,
    lend_sem,
    lend_send,
    give_sem,
    give_send,
    give_recv,
    small_sem,
    small_send,
):
    section = lax.axis_index("section")
    dp_index = lax.axis_index("dp")
    core = section % 2
    line = count // 2
    z, y = dp_index // 2, dp_index % 2
    half = channels // 2
    pieces, sizes, counts = reduce_plan(line, half)
    firsts = (0, counts[0] * sizes[0])
    lent = lends(sections, line, half)
    lender, borrower = section == 1, section == sections - 1
    partner = {"section": section + 1 - 2 * core}
    across = {"dp": dp_index + 1 - 2 * y}

    def peer(offset):
        return {"dp": lax.rem(dp_index + offset, count)}

    length, chunks = kept.shape[1], early.shape[1] - 2
    starts, _ = pool_plan(sections, count, channels, length, 0)
    mine = pool.at[pl.ds(starts[0], starts[1] - starts[0])]
    theirs = Stack(pool, starts[1], half)
    pair_landing = Stack(pool, starts[2], sizes[0] // 2)
    cross_landing = Stack(pool, starts[3], pieces[1])
    passed = [Stack(pool, starts[4 + kind], (line + 1) * pieces[kind], pieces[kind]) for kind in range(2)]

    def landing(kind, direction, group, step):
        return passed[kind].at[group, step if direction == 0 else line - step]

    right_peer, left_peer = {"dp": dp_index + 2}, {"dp": dp_index - 2}

    def ready(device):
        pl.semaphore_signal(ready_sem, inc=1, device_id=device, device_id_type=MESH)

    ready(partner)
    ready(across)
    pl.when(z < line - 1)(lambda: ready(right_peer))
    pl.when(z > 0)(lambda: ready(left_peer))
    neighbours = 2 + jnp.where(z < line - 1, 1, 0) + jnp.where(z > 0, 1, 0)
    if lent:
        pl.when(borrower)(lambda: ready({"section": section - 2}))
        neighbours = neighbours + jnp.where(lender, 1, 0)

    small_pair = pltpu.make_async_remote_copy(
        src_ref=totals.at[1 - core],
        dst_ref=small.at[1],
        send_sem=small_send.at[0],
        recv_sem=small_sem.at[1],
        device_id=partner,
        device_id_type=MESH,
    )

    def small_copy(offset):
        return pltpu.make_async_remote_copy(
            src_ref=small.at[0],
            dst_ref=small.at[1 + offset],
            send_sem=small_send.at[offset],
            recv_sem=small_sem.at[1 + offset],
            device_id=peer(offset),
            device_id_type=MESH,
        )

    def small_start(offset, _):
        small_copy(offset).start()
        return 0

    def small_add(offset, total):
        small_copy(offset).wait()
        return total + small[1 + offset]

    def product(block, which, use):
        columns = pl.ds(pl.multiple_of(which * half, 128), half)
        turn = block - C_BLOCKS
        mixed = (block < 4) | (block == 8)

        @pl.when(mixed)
        def _():
            side = jnp.where(block == 8, 1, 0)
            left = early[side, pl.ds(0, chunks), :, columns].reshape(length, half)
            use(tn(left, kept[jnp.where(block == 8, C_DQ, C_DPRE + block)]))

        @pl.when(~mixed)
        def _():
            left = jnp.where(block < 8, C_HID + block - 4, C_DPRE + turn)
            use(tn(kept[left, :, columns], kept[jnp.where(block < 8, C_DKV, T_DK + turn)]))

    def time_mix_back(turn):
        return pltpu.make_async_copy(
            early_hbm.at[T_MIX0 + turn], kept.at[C_DPRE + turn], back_sem.at[turn]
        )

    def block_rows(block):
        return pl.ds(pl.multiple_of(lookup(block, PLACES) * half, half), half)

    def pair_copy(block):
        return pltpu.make_async_remote_copy(
            src_ref=theirs.at[block % 2],
            dst_ref=mine.at[block_rows(block)],
            send_sem=pair_send.at[block],
            recv_sem=pair_sem.at[block],
            device_id=partner,
            device_id_type=MESH,
        )

    def for_partner(block):
        for side, first in ((0, 0), (1, 8)):

            @pl.when(block == first)
            def _():
                for chunk in range(chunks):
                    mix_back(side, chunk).wait()

        pl.when(block >= C_BLOCKS)(lambda: time_mix_back(block - C_BLOCKS).wait())
        pl.when(block >= 2)(lambda: pair_copy(block - 2).wait_send())

        def store(gradient):
            theirs.at[block % 2][...] = gradient.astype(BF16)

        product(block, 1 - core, store)

        @pl.when(block == 0)
        def _():
            pl.semaphore_wait(ready_sem, neighbours)
            small_pair.start()

        pair_copy(block).start()

    def lend_copy():
        return pltpu.make_async_remote_copy(
            src_ref=mine.at[pl.ds(LENT * half, half)],
            dst_ref=mine.at[pl.ds(BLOCKS * half, half)],
            send_sem=lend_send.at[0],
            recv_sem=lend_sem.at[0],
            device_id={"section": section + 2},
            device_id_type=MESH,
        )

    def for_me(block):
        rows = block_rows(block)

        def add(gradient):
            pair_copy(block).wait_recv()
            mine[rows, :] = (gradient + mine[rows, :].astype(F32)).astype(BF16)

        product(block, core, add)
        if lent:
            pl.when(lender & (block == PLACES.index(LENT)))(lambda: lend_copy().start())
        pl.when(block < 4)(lambda: time_mix_back(block).start())

    blocks_at = tuple(PLACES.index(place) for place in (*range(BLOCKS), LENT))

    def give(kind, group, start):
        size = pieces[kind]
        rows = pl.ds(pl.multiple_of(start, size), size)
        place = start // half if half % sizes[kind] else firsts[kind] // half + group * sizes[kind] // half
        block = lookup(place, blocks_at)
        row = core * half + start - place * half

        def copies(owner, target):
            foreign = kind == 1 and lent and group == counts[1]

            @pl.when((owner == core) & ~jnp.bool_(foreign))
            def _():
                pltpu.make_async_copy(mine.at[rows], target, give_sem.at[0]).start()

            def remote(device):
                return pltpu.make_async_remote_copy(
                    src_ref=mine.at[rows],
                    dst_ref=target,
                    send_sem=give_send.at[0],
                    recv_sem=give_recv.at[0],
                    device_id=device,
                    device_id_type=MESH,
                )

            @pl.when((owner != core) & ~jnp.bool_(foreign))
            def _():
                remote(partner).start()

            if kind == 1 and lent:
                pl.when(foreign)(lambda: remote({"section": section - core + owner - 2}).start())

            if kind == 0:
                remote({"section": section - core + owner, "dp": dp_index + 1 - 2 * y}).start()

        def to_in(owner, column):
            columns = pl.ds(pl.multiple_of(column * channels, channels), channels)
            copies(owner, in_hbm.at[pl.ds(pl.multiple_of(row, size), size), columns])

        def to_out():
            within = (block - 4) * channels + row
            copies(1, out_hbm.at[pl.ds(pl.multiple_of(within, size), size)])

        of_time = block >= C_BLOCKS
        pl.when((block < 4) | (of_time & (place < BLOCKS)))(
            lambda: to_in(jnp.where(of_time, 0, 1), jnp.where(of_time, block - C_BLOCKS, block))
        )
        pl.when((block >= 4) & ~of_time)(to_out)

    sum_sems = ((sum_sem0, sum_send0), (sum_sem1, sum_send1))
    spread_sems = ((spread_sem0, spread_send0), (spread_sem1, spread_send1))

    def piece_rows(kind, group, index):
        start = firsts[kind] + group * sizes[kind] + index * pieces[kind]
        if kind == 0:
            start = start + y * (sizes[0] // 2)
        return start, pl.ds(pl.multiple_of(start, pieces[kind]), pieces[kind])

    def sum_copy(kind, group, direction, step):
        place = landing(kind, direction, group, step)
        receive, send = sum_sems[kind]
        return pltpu.make_async_remote_copy(
            src_ref=place,
            dst_ref=place,
            send_sem=send.at[group, direction, step],
            recv_sem=receive.at[group, direction, step],
            device_id=(right_peer, left_peer)[direction],
            device_id_type=MESH,
        )

    def spread_copy(kind, group, direction, step, index):
        _, rows = piece_rows(kind, group, index)
        receive, send = spread_sems[kind]
        return pltpu.make_async_remote_copy(
            src_ref=mine.at[rows],
            dst_ref=mine.at[rows],
            send_sem=send.at[group, direction, step],
            recv_sem=receive.at[group, direction, step],
            device_id=(right_peer, left_peer)[direction],
            device_id_type=MESH,
        )

    def passing(kind, group, turn):
        for direction in range(2):
            behind = z if direction == 0 else line - 1 - z
            step = turn - behind
            index = line - 1 - step if direction == 0 else step
            place = landing(kind, direction, group, step)
            _, rows = piece_rows(kind, group, index)

            @pl.when((step >= 0) & (behind == 0) & (step < line - 1))
            def _():
                place[...] = mine[rows, :]
                sum_copy(kind, group, direction, step).start()

            @pl.when((step >= 0) & (behind > 0))
            def _():
                sum_copy(kind, group, direction, step).wait_recv()

                @pl.when(turn < line - 1)
                def _():
                    place[...] = (place[...].astype(F32) + mine[rows, :].astype(F32)).astype(BF16)
                    sum_copy(kind, group, direction, step).start()

    def arrived(kind, group):
        _, rows = piece_rows(kind, group, z)
        total = mine[rows, :].astype(F32)
        from_left = landing(kind, 0, group, jnp.minimum(line - 1 - z, line - 2))
        from_right = landing(kind, 1, group, jnp.minimum(z, line - 2))
        mine[rows, :] = total.astype(BF16)

        @pl.when(z == 0)
        def _():
            mine[rows, :] = (total + from_right[...].astype(F32)).astype(BF16)

        @pl.when(z == line - 1)
        def _():
            mine[rows, :] = (total + from_left[...].astype(F32)).astype(BF16)

        @pl.when((z > 0) & (z < line - 1))
        def _():
            mine[rows, :] = (
                total + from_left[...].astype(F32) + from_right[...].astype(F32)
            ).astype(BF16)

    def finished(kind, group, index):
        start, _ = piece_rows(kind, group, index)
        give(kind, group, start)

    def spread_own(kind, group):
        @pl.when(z < line - 1)
        def _():
            spread_copy(kind, group, 0, 0, z).start()

        @pl.when(z > 0)
        def _():
            spread_copy(kind, group, 1, 0, z).start()

        finished(kind, group, z)

    def spreading(kind, group, hop):
        for direction in range(2):
            index = z - hop if direction == 0 else z + hop
            onward = z < line - 1 if direction == 0 else z > 0
            exists = index >= 0 if direction == 0 else index < line

            @pl.when(exists)
            def _():
                spread_copy(kind, group, direction, hop - 1, index).wait_recv()

                @pl.when(onward)
                def _():
                    spread_copy(kind, group, direction, hop, index).start()

                finished(kind, group, index)

    def over(group):
        start = group * sizes[0] + (1 - y) * (sizes[0] // 2)
        return pltpu.make_async_remote_copy(
            src_ref=mine.at[pl.ds(pl.multiple_of(start, pieces[0]), sizes[0] // 2)],
            dst_ref=pair_landing.at[group],
            send_sem=y_send.at[group],
            recv_sem=y_sem.at[group],
            device_id=across,
            device_id_type=MESH,
        )

    def swap(group):
        _, rows = piece_rows(1, group, z)
        return pltpu.make_async_remote_copy(
            src_ref=mine.at[rows],
            dst_ref=cross_landing.at[group],
            send_sem=y_send.at[counts[0] + group],
            recv_sem=y_sem.at[counts[0] + group],
            device_id=across,
            device_id_type=MESH,
        )

    def event0(group, turn):
        @pl.when(turn == 0)
        def _():
            over(group).start()

        @pl.when(turn == 1)
        def _():
            over(group).wait_recv()

            def add(index, _):
                _, rows = piece_rows(0, group, index)
                local = pl.ds(pl.multiple_of(index * pieces[0], pieces[0]), pieces[0])
                arrived_rows = pair_landing.at[group][local, :]
                mine[rows, :] = (mine[rows, :].astype(F32) + arrived_rows.astype(F32)).astype(BF16)
                return 0

            lax.fori_loop(0, line, add, 0)

        @pl.when((turn >= 1) & (turn <= line))
        def _():
            passing(0, group, turn - 1)

        @pl.when(turn == line)
        def _():
            arrived(0, group)
            spread_own(0, group)

        @pl.when(turn > line)
        def _():
            spreading(0, group, turn - line)

    def event1(group, turn):
        if lent:
            pl.when((turn == 0) & (group == counts[1]))(lambda: lend_copy().wait_recv())

        @pl.when(turn < line)
        def _():
            passing(1, group, turn)

        @pl.when(turn == line - 1)
        def _():
            arrived(1, group)
            swap(group).start()

        @pl.when(turn == line)
        def _():
            swap(group).wait()
            _, rows = piece_rows(1, group, z)
            mine[rows, :] = (
                mine[rows, :].astype(F32) + cross_landing[group].astype(F32)
            ).astype(BF16)
            spread_own(1, group)

        @pl.when(turn > line)
        def _():
            spreading(1, group, turn - line)

    spare = firsts[1] + counts[1] * sizes[1] - BLOCKS * half
    if spare:
        mine[pl.ds(BLOCKS * half, spare), :] = jnp.zeros((spare, channels), BF16)
    tables = []
    for events in stage_orders(sections, line, half):
        order = [(COMPUTE, 0, 0)]
        for kind, group, turn in events:
            if kind == COMPUTE:
                order += [(COMPUTE, group + 1, 0)] * (group + 1 < BLOCKS) + [(COMPUTE, group, 1)]
            else:
                order.append((kind, group, turn))
        tables.append([kind * 1024 + group * 64 + turn for kind, group, turn in order])
    most = max(len(table) for table in tables)
    packed = []
    for table in tables:
        filled = table + [0] * (most + most % 2 - len(table))
        packed.append(tuple(a + 4096 * b for a, b in zip(filled[::2], filled[1::2], strict=True)))

    def mine_of(values):
        if len(values) == 1:
            return values[0]
        if len(set(values)) == 1:
            return jnp.int32(values[0])
        return jnp.where(lender, values[0], jnp.where(borrower, values[1], values[2]))

    steps = mine_of([len(table) for table in tables])

    def take(index, _):
        word = jnp.int32(0)
        for at, values in enumerate(zip(*packed, strict=True)):
            word = jnp.where(index // 2 == at, mine_of(values), word)
        code = jnp.where(index % 2 == 0, word % 4096, word // 4096)
        kind, group, turn = code // 1024, code // 64 % 16, code % 64

        @pl.when(kind == COMPUTE)
        def _():
            pl.when(turn == 0)(lambda: for_partner(group))
            pl.when(turn == 1)(lambda: for_me(group))

            @pl.when((turn == 1) & (group == BLOCKS // 2))
            def _():
                small_pair.wait()
                small[0] = totals[core] + small[1]
                lax.fori_loop(1, count, small_start, 0)

        pl.when(kind == 0)(lambda: event0(group, turn))
        pl.when(kind == 1)(lambda: event1(group, turn))
        return 0

    lax.fori_loop(0, steps, take, 0)
    small[0] = lax.fori_loop(1, count, small_add, small[0])
    total_copy = pltpu.make_async_copy(small.at[0], total_hbm, small_sem.at[0])
    total_copy.start()

    def summed_here(kind, group):
        if not lent:
            return group >= 0
        return (borrower | (group != counts[1])) if kind else (~lender | (group != LENT))

    def over_done(group, _):
        pl.when(summed_here(0, group))(lambda: over(group).wait_send())
        return 0

    for block in range(BLOCKS - 2, BLOCKS):
        pair_copy(jnp.int32(block)).wait_send()
    lax.fori_loop(0, counts[0], over_done, 0)
    for kind in range(2):

        def group_done(group, _):
            def step_done(step, _):
                for direction in range(2):
                    behind = z if direction == 0 else line - 1 - z

                    @pl.when((step < line - 1 - behind) & summed_here(kind, group))
                    def _():
                        sum_copy(kind, group, direction, step).wait_send()

                    @pl.when((step <= behind) & (behind < line - 1) & summed_here(kind, group))
                    def _():
                        spread_copy(kind, group, direction, step, 0).wait_send()

                return 0

            return lax.fori_loop(0, line - 1, step_done, 0)

        lax.fori_loop(0, counts[kind] + kind * lent, group_done, 0)

    if lent:
        pl.when(lender)(lambda: lend_copy().wait_send())

    def taken(rows, sem):
        if rows:
            ref = mine.at[pl.ds(0, rows)]
            pltpu.make_async_copy(ref, ref, sem.at[0]).wait()

    paired = [PLACES[block] < PAIRED for block in range(BLOCKS)]
    whole = [half // 2 if pair else half for pair in paired]
    by_kind = (range(C_BLOCKS, BLOCKS), range(C_BLOCKS))
    for own in range(2):
        for last in range(2):
            local = sum(whole[block] for block in by_kind[own])
            crossed = sum(half // 2 for block in range(BLOCKS) if paired[block])
            other = sum(whole[block] for block in by_kind[1 - own])
            if lent and own and last:
                other += half
            elif lent and own:
                crossed -= half // 2
                local -= whole[PLACES.index(LENT)]
            received = len(by_kind[own]) * channels - local

            @pl.when((core == own) & ((section >= 2) == bool(last)))
            def _(local=local, sent=other + crossed, received=received):
                taken(local, give_sem)
                taken(sent, give_send)
                taken(received, give_recv)

    total_copy.wait()


def pool_plan(sections, count, channels, length, slots):
    half, line = channels // 2, count // 2
    pieces, sizes, counts = reduce_plan(line, half)
    counts = (counts[0], counts[1] + lends(sections, line, half))
    heights = (
        counts[0] * sizes[0] + counts[1] * sizes[1],
        2 * half,
        counts[0] * sizes[0] // 2,
        counts[1] * pieces[1],
        *[counts[kind] * (line + 1) * pieces[kind] for kind in range(2)],
    )
    starts = [sum(heights[:at]) for at in range(len(heights))]
    return starts, max(sum(heights), slots * channels + 3 * length)


def chain(sections, count, x, cotangent, w_in, w_out, gain, bias, rates, wkv, state):
    length, channels = x.shape[2:]
    hidden_blocks = w_in.shape[2] // channels
    chunks = length // CHUNK
    anywhere = pl.BlockSpec(memory_space=pl.ANY)
    dma = pltpu.SemaphoreType.DMA
    slots = 9 + hidden_blocks
    line = count // 2
    _, _, counts = reduce_plan(line, channels // 2)
    counts = (counts[0], counts[1] + lends(sections, line, channels // 2))
    hops = [dma((counts[kind], 2, line - 1)) for kind in range(2)]
    _, pool_rows = pool_plan(sections, count, channels, length, slots)
    return pl.pallas_call(
        functools.partial(chain_kernel, sections, length, channels, hidden_blocks, count),
        out_shape=(
            jax.ShapeDtypeStruct((2, length, channels), BF16),
            jax.ShapeDtypeStruct((2, length, channels), BF16),
            jax.ShapeDtypeStruct((2, 8, channels), F32),
            jax.ShapeDtypeStruct((EARLY, length, channels), BF16),
            jax.ShapeDtypeStruct((channels, 4 * channels), BF16),
            jax.ShapeDtypeStruct(((C_BLOCKS - 4) * channels, channels), BF16),
            jax.ShapeDtypeStruct((8, channels), F32),
        ),
        in_specs=[anywhere] * 9,
        out_specs=(anywhere,) * 7,
        scratch_shapes=[
            pltpu.VMEM((pool_rows, channels), BF16),
            pltpu.VMEM((2, EARLY, CHUNK, channels), BF16),
            pltpu.VMEM((LATE, length, channels), BF16),
            pltpu.VMEM((2, length, channels), F32),
            pltpu.VMEM((length, channels), BF16),
            pltpu.VMEM((5, CHUNK, channels), F32),
            pltpu.VMEM((2 * CHUNK, 2 * channels), BF16),
            pltpu.VMEM((2, CHUNK, channels), F32),
            pltpu.VMEM((2, CHUNK, 2 * CHUNK), BF16),
            pltpu.VMEM((2, 1, channels), F32),
            pltpu.VMEM((2, 1, channels), F32),
            pltpu.VMEM((2, 3, 1, channels), F32),
            pltpu.VMEM((2, 2, channels), F32),
            pltpu.VMEM((2, 3, 2, 1, channels), F32),
            pltpu.VMEM((2, length // ROWS, channels), F32),
            pltpu.VMEM((8, channels), F32),
            pltpu.VMEM((8, channels), F32),
            pltpu.VMEM((2, 8, channels), F32),
            pltpu.VMEM((2, 8, 8, channels), F32),
            pltpu.VMEM((2, 8, channels), F32),
            dma((slots,)),
            dma((slots,)),
            dma((2, 5)),
            dma((5,)),
            dma((chunks,)),
            dma((chunks,)),
            dma((chunks,)),
            dma((chunks,)),
            dma((2 + chunks,)),
            dma((2 + chunks,)),
            dma((2 + chunks,)),
            dma((2,)),
            dma((2, chunks)),
            pltpu.VMEM((count + 1, 8, channels), F32),
            pltpu.SemaphoreType.REGULAR,
            dma((4,)),
            dma((BLOCKS,)),
            dma((BLOCKS,)),
            dma((sum(counts),)),
            dma((sum(counts),)),
            hops[0],
            hops[0],
            hops[1],
            hops[1],
            hops[0],
            hops[0],
            hops[1],
            hops[1],
            dma((1,)),
            dma((1,)),
            dma((1,)),
            dma((1,)),
            dma((1,)),
            dma((count + 1,)),
            dma((count + 1,)),
        ],
        compiler_params=pltpu.CompilerParams(
            collective_id=0, has_side_effects=True, vmem_limit_bytes=VMEM_BYTES
        ),
    )(x, cotangent, w_in, w_out, gain, bias, rates, wkv, state)


def finish_kernel(
    in_short,
    out_short,
    outs_in,
    grads_in,
    fin,
    total,
    in_wide,
    out_wide,
    outs,
    grads,
    states,
    normed,
    gain,
    bias,
    rates,
    wkv,
    in_held,
    out_held,
    in_made,
    out_made,
    tokens_held,
    load_sem,
    store_sem,
):
    holds_channel_mix = lax.axis_index("section") % 2 == 1
    sources, targets = (in_short, out_short), (in_wide, out_wide)
    held, made = (in_held, out_held), (in_made, out_made)
    parts = 8
    jobs = [(which, part) for part in range(parts) for which in range(2)]

    def rows_of(which, part):
        tall = sources[which].shape[0] // parts
        return pl.ds(part * tall, tall)

    def load(which, part):
        rows = rows_of(which, part)
        return pltpu.make_async_copy(
            sources[which].at[rows], held[which].at[rows], load_sem.at[which, part]
        )

    def store(which, part):
        rows = rows_of(which, part)
        return pltpu.make_async_copy(
            made[which].at[rows], targets[which].at[rows], store_sem.at[which, part]
        )

    def start(which, part):
        if which:
            pl.when(holds_channel_mix)(lambda: load(which, part).start())
        else:
            load(which, part).start()

    token_loads = [
        pltpu.make_async_copy(source, tokens_held.at[at], load_sem.at[2, at])
        for at, source in enumerate((outs_in, grads_in))
    ]
    token_stores = [
        pltpu.make_async_copy(tokens_held.at[at], target.at[0, :, 0], store_sem.at[2, at])
        for at, target in enumerate((outs, grads))
    ]
    ahead = 6
    for job in jobs[:2]:
        start(*job)
    for copy in token_loads:
        copy.start()
    for job in jobs[2:ahead]:
        start(*job)
    for micro in range(2):
        normed[0, micro] = fin[micro, 0:1]
        for row in range(2):
            states[0, row, micro] = fin[micro, 1 + row : 2 + row]
    gain[...] = total[GAIN : GAIN + 1]
    bias[...] = total[BIAS : BIAS + 1]
    for row in range(3):
        rates[row] = total[RATES + row : RATES + row + 1]
    wkv[0] = total[DECAY : DECAY + 2]
    for at, (which, part) in enumerate(jobs):
        tall = sources[which].shape[0] // parts
        step = 32 if which == 0 else 96

        def widen(index, _):
            rows = pl.ds(pl.multiple_of(part * tall + index * step, step), step)
            made[which][rows, :] = held[which][rows, :].astype(F32)
            return 0

        def clear(index, _):
            rows = pl.ds(pl.multiple_of(part * tall + index * step, step), step)
            made[which][rows, :] = jnp.zeros((step, made[which].shape[1]), F32)
            return 0

        def widened():
            load(which, part).wait()
            lax.fori_loop(0, tall // step, widen, 0)

        if which:
            pl.when(holds_channel_mix)(widened)

            @pl.when(~holds_channel_mix)
            def _():
                lax.fori_loop(0, tall // step, clear, 0)

        else:
            widened()
        if at + ahead < len(jobs):
            start(*jobs[at + ahead])
        store(which, part).start()
        if at < 2:
            token_loads[at].wait()
            token_stores[at].start()
    for job in jobs:
        store(*job).wait()
    for copy in token_stores:
        copy.wait()


def finished_outputs(in_short, out_short, outs, grads, fin, total):
    length, channels = outs.shape[1:]
    whole = pl.BlockSpec(memory_space=pltpu.VMEM)
    anywhere = pl.BlockSpec(memory_space=pl.ANY)

    def shape(*sizes, dtype=F32):
        return jax.ShapeDtypeStruct(sizes, dtype)

    in_wide, out_wide, *rest = pl.pallas_call(
        finish_kernel,
        out_shape=(
            shape(*in_short.shape),
            shape(*out_short.shape),
            shape(1, 2, 1, length, channels, dtype=BF16),
            shape(1, 2, 1, length, channels, dtype=BF16),
            shape(1, 2, 2, 1, channels),
            shape(1, 2, 1, channels),
            shape(1, channels),
            shape(1, channels),
            shape(3, 1, channels),
            shape(1, 2, channels),
        ),
        in_specs=[anywhere] * 4 + [whole] * 2,
        out_specs=(anywhere,) * 4 + (whole,) * 6,
        scratch_shapes=[
            pltpu.VMEM(in_short.shape, BF16),
            pltpu.VMEM(out_short.shape, BF16),
            pltpu.VMEM(in_short.shape, F32),
            pltpu.VMEM(out_short.shape, F32),
            pltpu.VMEM((2, 2, length, channels), BF16),
            pltpu.SemaphoreType.DMA((3, 8)),
            pltpu.SemaphoreType.DMA((3, 8)),
        ],
        compiler_params=pltpu.CompilerParams(vmem_limit_bytes=VMEM_BYTES),
    )(in_short, out_short, outs, grads, fin, total)
    *rest, rates, wkv = rest
    return in_wide, out_wide, *rest, jnp.swapaxes(rates, 0, 1), wkv


def shards(
    block_input,
    carried_state,
    output_cotangent,
    in_weight,
    out_weight,
    norm_gain,
    norm_bias,
    mix_rates,
    wkv_params,
):
    sections = lax.axis_size("section")
    outs, grads, fin, _, in_short, out_short, total = chain(
        sections,
        lax.axis_size("dp"),
        block_input,
        output_cotangent,
        in_weight,
        out_weight,
        norm_gain,
        norm_bias,
        jnp.swapaxes(mix_rates, 0, 1),
        wkv_params,
        carried_state,
    )
    in_grad, out_grad, outs, grads, states, normed, gain, bias, rates, wkv = finished_outputs(
        in_short, out_short, outs, grads, fin, total
    )
    return outs, states, normed, grads, in_grad[None], out_grad[None], gain, bias, rates, wkv


def solution(mesh):
    return jax.shard_map(
        shards,
        mesh=mesh,
        in_specs=(
            P(None, "dp", None, None),
            P("section", None, None, "dp", None),
            P(None, "dp", None, None),
            P("section", None, None),
            P("section", None, None),
            P("section", None),
            P("section", None),
            P("section", None, None),
            P("section", None, None),
        ),
        out_specs=(
            P("section", None, "dp", None, None),
            P("section", None, None, "dp", None),
            P("section", None, "dp", None),
            P("section", None, "dp", None, None),
            P("section", None, None),
            P("section", None, None),
            P("section", None),
            P("section", None),
            P("section", None, None),
            P("section", None, None),
        ),
        check_vma=False,
    )
```

```python
import functools

import jax
import jax.numpy as jnp
from jax import lax
from jax.experimental import pallas as pl
from jax.experimental.pallas import tpu as pltpu
from jax.sharding import PartitionSpec as P

MESH = pl.DeviceIdType.MESH
F32 = jnp.float32
BF16 = jnp.bfloat16
CHUNK = 256
ROWS = 64
UNROLL = 2
TALL = 64
VMEM_BYTES = (64 << 20) - (128 << 10)

T_MIX0, T_MIX2, T_MIX1, T_GATED, C_MIX0, C_MIX1 = 0, 1, 2, 3, 4, 5
EARLY = 6
T_DK, T_DV, T_DQ, T_G, C_DKV, C_DQ, C_HID, C_DPRE = 0, 1, 2, 3, 4, 5, 6, 10
LATE = 14
GAIN, BIAS, RATES, DECAY, BONUS = 0, 1, 2, 5, 6


def nn(left, right):
    return jnp.dot(left, right, preferred_element_type=F32)


def nt(left, right):
    return lax.dot_general(left, right, (((1,), (1,)), ((), ())), preferred_element_type=F32)


def tn(left, right):
    return lax.dot_general(left, right, (((0,), (0,)), ((), ())), preferred_element_type=F32)


class Stack:
    def __init__(self, buffer, start, *heights):
        self.buffer, self.start, self.heights = buffer, start, heights

    @property
    def at(self):
        return Places(self)

    def __getitem__(self, index):
        return self.at[index][...]


class Places:
    def __init__(self, stack):
        self.stack = stack

    def __getitem__(self, index):
        index = index if isinstance(index, tuple) else (index,)
        start, height = self.stack.start, self.stack.heights[-1]
        for place, tall in zip(index, self.stack.heights, strict=True):
            start = start + place * tall
        if not isinstance(start, int):
            start = pl.multiple_of(start, 16)
        return self.stack.buffer.at[pl.ds(start, height)]


def folded(rows):
    total = rows[0:8]
    for start in range(8, rows.shape[0], 8):
        total = total + rows[start : start + 8]
    return total


def chain_kernel(
    sections,
    length,
    channels,
    hidden_blocks,
    count,
    x_hbm,
    cot_hbm,
    w_in_hbm,
    w_out_hbm,
    gain_hbm,
    bias_hbm,
    rates_hbm,
    wkv_hbm,
    state_hbm,
    outs_hbm,
    grads_hbm,
    fin_hbm,
    early_hbm,
    in_hbm,
    out_hbm,
    total_hbm,
    pool,
    early,
    kept,
    states,
    upstream,
    wide,
    pairs,
    tables,
    triangles,
    gains,
    biases,
    rates,
    wkvs,
    starts,
    previous,
    carry,
    carry_next,
    fin,
    sums,
    totals,
    weight_sem,
    weight_send,
    small_sem,
    small_send,
    entry_sem,
    entry_send,
    up_sem,
    up_send,
    out_sem,
    out_send,
    out_recv,
    early_sem,
    *reducing,
):
    section = lax.axis_index("section")
    dp_index = lax.axis_index("dp")
    core = section % 2
    stage = section // 2
    stages = sections // 2
    partner = {"section": section + 1 - 2 * core}
    chunks = length // CHUNK
    blocks = CHUNK // ROWS
    tall_blocks = CHUNK // TALL
    time_blocks = 4
    last_stage = stage == stages - 1
    weights = Stack(pool, 0, channels)
    after_weights = (9 + hidden_blocks) * channels
    entry = pool.at[pl.ds(after_weights, length)]
    hs = Stack(pool, after_weights + length, length)
    mid, top = hs.at[0], hs.at[1]

    barrier = pltpu.get_barrier_semaphore()
    across = {"dp": dp_index + 1 - 2 * (dp_index % 2)}
    for device in (partner, partner | across):
        pl.semaphore_signal(barrier, inc=1, device_id=device, device_id_type=MESH)

    def greet(offset, _):
        peer = {"dp": lax.rem(dp_index + offset, count)}
        pl.semaphore_signal(barrier, inc=1, device_id=peer, device_id_type=MESH)
        return 0

    lax.fori_loop(1, count, greet, 0)

    @pl.when(stage > 0)
    def _():
        for other in (section - 2, section - 1 - 2 * core):
            pl.semaphore_signal(barrier, inc=1, device_id={"section": other}, device_id_type=MESH)

    @pl.when(stage < stages - 1)
    def _():
        for other in (section + 2, section + 3 - 2 * core):
            pl.semaphore_signal(barrier, inc=1, device_id={"section": other}, device_id_type=MESH)

    def entry_copy(chunk):
        rows = pl.ds(chunk * CHUNK, CHUNK)
        return pltpu.make_async_copy(
            x_hbm.at[core, 0, rows], entry.at[rows], entry_sem.at[chunk]
        )

    def up_copy(chunk):
        rows = pl.ds(chunk * CHUNK, CHUNK)
        return pltpu.make_async_copy(
            cot_hbm.at[core, 0, rows], upstream.at[rows], up_sem.at[chunk]
        )

    @pl.when(stage == 0)
    def _():
        for chunk in range(chunks):
            entry_copy(chunk).start()

    @pl.when(last_stage)
    def _():
        for chunk in range(chunks):
            up_copy(chunk).start()

    small_pairs = (
        (gain_hbm, gains.at[core]),
        (bias_hbm, biases.at[core]),
        (rates_hbm, rates.at[core]),
        (wkv_hbm.at[0], wkvs.at[core]),
        (state_hbm.at[0], starts.at[core]),
    )
    small_copies = [
        pltpu.make_async_copy(source, target, small_sem.at[0, at])
        for at, (source, target) in enumerate(small_pairs)
    ]
    for copy in small_copies:
        copy.start()

    def in_block(index):
        return w_in_hbm.at[0, :, pl.ds(index * channels, channels)]

    def out_block(index):
        return w_out_hbm.at[0, pl.ds(index * channels, channels), :]

    def load_in():
        for index in range(4):
            slot = core * time_blocks + index
            pltpu.make_async_copy(in_block(index), weights.at[slot], weight_sem.at[slot]).start()

    def load_out():
        for index in range(hidden_blocks + 1):
            slot = 8 + index
            pltpu.make_async_copy(
                out_block(index), weights.at[slot], weight_sem.at[slot]
            ).start()

    pl.when(core == 0)(load_in)
    has_previous = jnp.where(stage > 0, 1, 0)
    has_next = jnp.where(stage < stages - 1, 1, 0)
    pl.semaphore_wait(barrier, 1 + count + 2 * (has_previous + has_next))

    small_remotes = [
        pltpu.make_async_remote_copy(
            src_ref=source,
            dst_ref=target,
            send_sem=small_send.at[at],
            recv_sem=small_sem.at[1, at],
            device_id=partner,
            device_id_type=MESH,
        )
        for at, (source, target) in enumerate(small_pairs)
    ]

    def in_remote(index):
        slot = core * time_blocks + index
        return pltpu.make_async_remote_copy(
            src_ref=in_block(index),
            dst_ref=weights.at[slot],
            send_sem=weight_send.at[slot],
            recv_sem=weight_sem.at[slot],
            device_id=partner,
            device_id_type=MESH,
        )

    def out_remote(index):
        slot = 8 + index
        return pltpu.make_async_remote_copy(
            src_ref=out_block(index),
            dst_ref=weights.at[slot],
            send_sem=weight_send.at[slot],
            recv_sem=weight_sem.at[slot],
            device_id=partner,
            device_id_type=MESH,
        )

    for copy in small_remotes:
        copy.start()
    for index in range(4):
        in_remote(index).start()

    @pl.when(core == 1)
    def _():
        for index in (hidden_blocks, *range(hidden_blocks)):
            out_remote(index).start()
        load_in()
        load_out()

    row_at = lax.broadcasted_iota(jnp.int32, (CHUNK, 2 * CHUNK), 0)
    column_at = lax.broadcasted_iota(jnp.int32, (CHUNK, 2 * CHUNK), 1)
    column_at = jnp.where(column_at >= CHUNK, column_at - CHUNK, column_at)
    triangles[0] = jnp.where(row_at > column_at, 1.0, 0.0).astype(BF16)
    triangles[1] = jnp.where(row_at < column_at, 1.0, 0.0).astype(BF16)
    sums[...] = jnp.zeros_like(sums)
    fin[...] = jnp.zeros_like(fin)

    for copy in small_copies:
        copy.wait()
    for copy in small_remotes:
        copy.wait_recv()

    rate = jnp.exp(wkvs[0, 0:1, :])
    step = jnp.exp(-rate)
    lift = jnp.exp(wkvs[0, 1:2, :])

    def table_rows(index, _):
        start = pl.multiple_of(index * ROWS, ROWS)
        place = (lax.broadcasted_iota(jnp.int32, (ROWS, channels), 0) + start).astype(F32)
        tables[0, pl.ds(start, ROWS), :] = jnp.exp(-(CHUNK - 1.0 - place) * rate)
        tables[1, pl.ds(start, ROWS), :] = jnp.exp(-place * rate)
        return 0

    lax.fori_loop(0, blocks, table_rows, 0)

    for row in range(3):
        carry[row : row + 1] = starts[0, row, core]
    carry[3:4] = starts[1, 0, core]

    def weight_wait(slot):
        pltpu.make_async_copy(weights.at[slot], weights.at[slot], weight_sem.at[slot]).wait()

    def stats(tokens):
        center = tokens - jnp.mean(tokens, axis=-1, keepdims=True)
        spread = jnp.mean(center * center, axis=-1, keepdims=True)
        root = lax.rsqrt(spread + 1e-05)
        return center * root, root

    row_index = lax.broadcasted_iota(jnp.int32, (ROWS, channels), 0)
    tall_index = lax.broadcasted_iota(jnp.int32, (TALL, channels), 0)

    def token_mix(kind, source, base, side, slots, carry_row):
        gain, bias = gains[kind], biases[kind]

        def body(index, before):
            start = pl.multiple_of(base + index * ROWS, ROWS)
            rows = pl.ds(start, ROWS)
            unit, _ = stats(source[rows, :].astype(F32))
            normed = unit * gain + bias
            previous[kind, pl.ds(start // ROWS, 1), :] = before
            shifted = jnp.where(
                row_index == 0, jnp.broadcast_to(before, normed.shape), pltpu.roll(normed, 1, 0)
            )
            gap = normed - shifted
            for rate_row, slot in slots:
                early[side, slot, pl.ds(pl.multiple_of(index * ROWS, ROWS), ROWS), :] = (
                    shifted + gap * rates[kind, rate_row]
                ).astype(BF16)
            return normed[ROWS - 1 : ROWS, :]

        carry[carry_row : carry_row + 1] = lax.fori_loop(
            0, blocks, body, carry[carry_row : carry_row + 1], unroll=UNROLL
        )

    def early_copy(chunk):
        rows = pl.ds(pl.multiple_of(chunk * CHUNK, CHUNK), CHUNK)
        side = chunk % 2
        return pltpu.make_async_copy(
            early.at[side], early_hbm.at[:, rows], early_sem.at[side]
        )

    def forward_chunk(chunk, _):
        base = pl.multiple_of(chunk * CHUNK, CHUNK)
        rows = pl.ds(base, CHUNK)
        side = chunk % 2

        @pl.when(chunk >= 2)
        def _():
            early_copy(chunk - 2).wait()

        pltpu.make_async_copy(entry.at[rows], entry.at[rows], entry_sem.at[chunk]).wait()

        token_mix(0, entry, base, side, ((0, T_MIX0), (2, T_MIX2), (1, T_MIX1)), 0)

        for slot in range(3):

            @pl.when(chunk == 0)
            def _():
                weight_wait(slot)

            wide[slot] = nn(early[side, slot], weights[slot])

        def weighted(index, _):
            start = pl.multiple_of(index * TALL, TALL)
            local = pl.ds(start, TALL)
            whole = pl.ds(pl.multiple_of(base + start, TALL), TALL)
            value = wide[1, local, :]
            power = jnp.exp(wide[0, local, :])
            wide[0, local, :] = power
            scaled = power * tables[0, local, :]
            pairs[local, pl.ds(0, channels)] = (scaled * value).astype(BF16)
            pairs[local, pl.ds(channels, channels)] = scaled.astype(BF16)
            kept[T_DK, whole, :] = power.astype(BF16)
            kept[T_DV, whole, :] = value.astype(BF16)
            return 0

        lax.fori_loop(0, tall_blocks, weighted, 0)
        wide[3] = nn(triangles[0, :, pl.ds(0, CHUNK)], pairs[pl.ds(0, CHUNK), pl.ds(0, channels)])
        wide[4] = nn(
            triangles[0, :, pl.ds(0, CHUNK)], pairs[pl.ds(0, CHUNK), pl.ds(channels, channels)]
        )
        upper, lower = carry[1:2], carry[2:3]

        def averaged(index, _):
            start = pl.multiple_of(index * TALL, TALL)
            local = pl.ds(start, TALL)
            whole = pl.ds(pl.multiple_of(base + start, TALL), TALL)
            place = (tall_index + start).astype(F32)
            grown = jnp.exp((CHUNK - place) * rate)
            faded = tables[1, local, :]
            power, value = wide[0, local, :], wide[1, local, :]
            before_upper = grown * wide[3, local, :] + faded * upper
            before_lower = grown * wide[4, local, :] + faded * lower
            now = power * lift
            average = (before_upper + now * value) / (before_lower + now)
            gate = jax.nn.sigmoid(wide[2, local, :])
            states[0, whole, :] = before_upper
            states[1, whole, :] = before_lower
            kept[T_DQ, whole, :] = gate.astype(BF16)
            early[side, T_GATED, local, :] = (gate * average).astype(BF16)
            tail = slice(TALL - 8, TALL)
            after_upper = step * before_upper[tail] + power[tail] * value[tail]
            after_lower = step * before_lower[tail] + power[tail]
            carry_next[0:1] = after_upper[7:8]
            carry_next[1:2] = after_lower[7:8]
            return 0

        lax.fori_loop(0, tall_blocks, averaged, 0)
        carry[1:3] = carry_next[0:2]

        @pl.when(chunk == 0)
        def _():
            weight_wait(3)

        mid[rows, :] = (
            entry[rows, :].astype(F32) + nn(early[side, T_GATED], weights[3])
        ).astype(BF16)

        token_mix(1, mid, base, side, ((0, C_MIX0), (1, C_MIX1)), 3)

        for index in range(hidden_blocks):

            @pl.when(chunk == 0)
            def _():
                weight_wait(4 + index)

            pre = nn(early[side, C_MIX0], weights[4 + index])
            kept[C_HID + index, rows, :] = jnp.square(jnp.maximum(pre, 0.0)).astype(BF16)

        @pl.when(chunk == 0)
        def _():
            weight_wait(8 + hidden_blocks)

        early_copy(chunk).start()
        wide[1] = nn(early[side, C_MIX1], weights[8 + hidden_blocks])

        @pl.when(chunk == 0)
        def _():
            for index in range(hidden_blocks):
                weight_wait(8 + index)

        total = nn(kept[C_HID, rows, :], weights[8])
        for index in range(1, hidden_blocks):
            total = total + nn(kept[C_HID + index, rows, :], weights[8 + index])
        wide[0] = total

        def joined(index, _):
            start = pl.multiple_of(index * TALL, TALL)
            local = pl.ds(start, TALL)
            whole = pl.ds(pl.multiple_of(base + start, TALL), TALL)
            gate = jax.nn.sigmoid(wide[1, local, :])
            value = wide[0, local, :]
            kept[C_DKV, whole, :] = gate.astype(BF16)
            kept[C_DQ, whole, :] = value.astype(BF16)
            top[whole, :] = (mid[whole, :].astype(F32) + gate * value).astype(BF16)
            return 0

        lax.fori_loop(0, tall_blocks, joined, 0)

        @pl.when(stage < stages - 1)
        def _():
            entry_remote(chunk).start()

        return 0

    def entry_remote(chunk):
        rows = pl.ds(pl.multiple_of(chunk * CHUNK, CHUNK), CHUNK)
        return pltpu.make_async_remote_copy(
            src_ref=top.at[rows],
            dst_ref=entry.at[rows],
            send_sem=entry_send.at[chunk],
            recv_sem=entry_sem.at[chunk],
            device_id={"section": section + 2},
            device_id_type=MESH,
        )

    def up_remote(chunk):
        rows = pl.ds(pl.multiple_of(chunk * CHUNK, CHUNK), CHUNK)
        return pltpu.make_async_remote_copy(
            src_ref=upstream.at[rows],
            dst_ref=upstream.at[rows],
            send_sem=up_send.at[chunk],
            recv_sem=up_sem.at[chunk],
            device_id={"section": section - 2},
            device_id_type=MESH,
        )

    lax.fori_loop(0, chunks, forward_chunk, 0)
    early_copy(chunks - 2).wait()
    early_copy(chunks - 1).wait()

    def mix_back(side, chunk):
        return pltpu.make_async_copy(
            early_hbm.at[C_MIX0 + side, pl.ds(chunk * CHUNK, CHUNK)],
            early.at[side, chunk],
            back_sem.at[side, chunk],
        )

    back_sem, reducing = reducing[0], reducing[1:]
    for side in range(2):
        for chunk in range(chunks):
            mix_back(side, chunk).start()

    fin[0, 0:1] = carry[0:1]
    fin[0, 1:3] = carry[1:3]
    fin[1, 0:1] = carry[3:4]

    def to_owner(index, own_src, other_src, dst):
        own = pltpu.make_async_copy(own_src, dst, out_sem.at[index])
        other = pltpu.make_async_remote_copy(
            src_ref=other_src,
            dst_ref=dst,
            send_sem=out_send.at[index],
            recv_sem=out_recv.at[index],
            device_id=partner,
            device_id_type=MESH,
        )
        return own, other

    outs_copies = to_owner(0, hs.at[core], hs.at[1 - core], outs_hbm.at[core])
    fin_copies = to_owner(1, fin.at[core], fin.at[1 - core], fin_hbm.at[core])
    for copy in outs_copies + fin_copies:
        copy.start()

    carry[0:4] = jnp.zeros((4, channels), F32)

    def norm_back(kind, source, base, mixes, above, target, carry_row):
        gain, bias = gains[kind], biases[kind]

        def body(index, after):
            back = blocks - 1 - index
            local = pl.ds(pl.multiple_of(back * ROWS, ROWS), ROWS)
            start = pl.multiple_of(base + back * ROWS, ROWS)
            rows = pl.ds(start, ROWS)
            unit, root = stats(source[rows, :].astype(F32))
            normed = unit * gain + bias
            before = previous[kind, pl.ds(start // ROWS, 1), :]
            shifted = jnp.where(
                row_index == 0, jnp.broadcast_to(before, normed.shape), pltpu.roll(normed, 1, 0)
            )
            gap = normed - shifted
            straight = jnp.zeros_like(normed)
            total = jnp.zeros_like(normed)
            for rate_row, slot in mixes:
                mix = wide[slot, local, :]
                straight = straight + mix * rates[kind, rate_row]
                total = total + mix
                sums[kind, RATES + rate_row] += folded(mix * gap)
            late = total - straight
            moved = jnp.where(
                row_index == ROWS - 1,
                jnp.broadcast_to(after, late.shape),
                pltpu.roll(late, ROWS - 1, 0),
            )
            d_normed = straight + moved
            sums[kind, GAIN] += folded(d_normed * unit)
            sums[kind, BIAS] += folded(d_normed)
            d_unit = d_normed * gain
            d_tokens = (
                d_unit
                - jnp.mean(d_unit, axis=-1, keepdims=True)
                - unit * jnp.mean(d_unit * unit, axis=-1, keepdims=True)
            ) * root
            target[rows, :] = (above[rows, :].astype(F32) + d_tokens).astype(BF16)
            return late[0:1, :]

        carry[carry_row : carry_row + 1] = lax.fori_loop(
            0, blocks, body, carry[carry_row : carry_row + 1], unroll=UNROLL
        )

    def grad_copies(chunk, kind):
        rows = pl.ds(pl.multiple_of(chunk * CHUNK, CHUNK), CHUNK)
        sources = (upstream.at[rows], kept.at[T_G, rows])
        return to_owner(
            2 + chunk, sources[kind], sources[1 - kind], grads_hbm.at[core, rows]
        )

    def backward_chunk(turn, _):
        chunk = chunks - 1 - turn
        base = pl.multiple_of(chunk * CHUNK, CHUNK)
        rows = pl.ds(base, CHUNK)
        pltpu.make_async_copy(upstream.at[rows], upstream.at[rows], up_sem.at[chunk]).wait()

        def split(index, _):
            whole = pl.ds(pl.multiple_of(base + index * TALL, TALL), TALL)
            above = upstream[whole, :].astype(F32)
            gate = kept[C_DKV, whole, :].astype(F32)
            value = kept[C_DQ, whole, :].astype(F32)
            d_value = above * gate
            kept[C_DKV, whole, :] = d_value.astype(BF16)
            kept[C_DQ, whole, :] = (d_value * value * (1.0 - gate)).astype(BF16)
            return 0

        lax.fori_loop(0, tall_blocks, split, 0)

        for index in range(hidden_blocks):
            d_hidden = nt(kept[C_DKV, rows, :], weights[8 + index])
            slope = jnp.sqrt(kept[C_HID + index, rows, :].astype(F32))
            kept[C_DPRE + index, rows, :] = (d_hidden * (2.0 * slope)).astype(BF16)
        total = nt(kept[C_DPRE, rows, :], weights[4])
        for index in range(1, hidden_blocks):
            total = total + nt(kept[C_DPRE + index, rows, :], weights[4 + index])
        wide[0] = total
        wide[1] = nt(kept[C_DQ, rows, :], weights[8 + hidden_blocks])
        norm_back(1, mid, base, ((0, 0), (1, 1)), upstream, kept.at[T_G], 3)

        wide[0] = nt(kept[T_G, rows, :], weights[3])

        def inputs(index, _):
            start = pl.multiple_of(index * TALL, TALL)
            local = pl.ds(start, TALL)
            whole = pl.ds(pl.multiple_of(base + start, TALL), TALL)
            power = kept[T_DK, whole, :].astype(F32)
            value = kept[T_DV, whole, :].astype(F32)
            gate = kept[T_DQ, whole, :].astype(F32)
            now = power * lift
            inverse = 1.0 / (states[1, whole, :] + now)
            average = (states[0, whole, :] + now * value) * inverse
            d_average = wide[0, local, :] * gate
            kept[T_DQ, whole, :] = (d_average * average * (1.0 - gate)).astype(BF16)
            unit = d_average * inverse
            wide[1, local, :] = unit
            wide[2, local, :] = average
            scaled = unit * tables[1, local, :]
            for column, term in ((0, scaled), (channels, -scaled * average)):
                high = term.astype(BF16)
                pairs[local, pl.ds(column, channels)] = high
                pairs[pl.ds(pl.multiple_of(CHUNK + start, TALL), TALL), pl.ds(column, channels)] = (
                    term - high.astype(F32)
                ).astype(BF16)
            return 0

        lax.fori_loop(0, tall_blocks, inputs, 0)
        wide[3] = nn(triangles[1], pairs[:, pl.ds(0, channels)])
        wide[4] = nn(triangles[1], pairs[:, pl.ds(channels, channels)])
        alpha_after, beta_after = carry[1:2], carry[2:3]

        def outputs(index, _):
            start = pl.multiple_of((tall_blocks - 1 - index) * TALL, TALL)
            local = pl.ds(start, TALL)
            whole = pl.ds(pl.multiple_of(base + start, TALL), TALL)
            place = (tall_index + start).astype(F32)
            grown = jnp.exp((place + 1.0) * rate)
            faded = tables[0, local, :]
            alpha = grown * wide[3, local, :] + faded * alpha_after
            beta = grown * wide[4, local, :] + faded * beta_after
            unit, average = wide[1, local, :], wide[2, local, :]
            power = kept[T_DK, whole, :].astype(F32)
            value = kept[T_DV, whole, :].astype(F32)
            weighed = unit * (power * lift)
            own = weighed * (value - average)
            kept[T_DK, whole, :] = (own + power * (alpha * value + beta)).astype(BF16)
            kept[T_DV, whole, :] = (weighed + power * alpha).astype(BF16)
            sums[0, BONUS] += folded(own)
            sums[0, DECAY] += folded(
                alpha * states[0, whole, :] + beta * states[1, whole, :]
            )
            carry_next[0:1] = unit[0:1] + step * alpha[0:1]
            carry_next[1:2] = step * beta[0:1] - unit[0:1] * average[0:1]
            return 0

        lax.fori_loop(0, tall_blocks, outputs, 0)
        carry[1:3] = carry_next[0:2]
        wide[0] = nt(kept[T_DK, rows, :], weights[0])
        wide[1] = nt(kept[T_DQ, rows, :], weights[2])
        wide[2] = nt(kept[T_DV, rows, :], weights[1])
        norm_back(
            0, entry, base, ((0, 0), (1, 1), (2, 2)), kept.at[T_G], upstream, 0
        )

        @pl.when(stage > 0)
        def _():
            up_remote(chunk).start()

        for kind in range(2):

            @pl.when(core == kind)
            def _():
                for copy in grad_copies(chunk, kind):
                    copy.start()

        return 0

    lax.fori_loop(0, chunks, backward_chunk, 0)

    sums[0, DECAY] = sums[0, DECAY] * (-rate * step)
    for kind in range(2):
        for row in range(7):
            totals[kind, row : row + 1] = jnp.sum(sums[kind, row], axis=0, keepdims=True)
        totals[kind, 7:8] = jnp.zeros((1, channels), F32)

    for copy in outs_copies:
        copy.wait()

    @pl.when(stage < stages - 1)
    def _():
        for chunk in range(chunks):
            entry_remote(chunk).wait_send()

    reduce_phase(
        sections, count, channels, pool, early, kept, early_hbm, totals, mix_back, in_hbm, out_hbm, total_hbm, *reducing
    )

    for copy in fin_copies:
        copy.wait()
    for chunk in range(chunks):
        for copy in grad_copies(chunk, 0):
            copy.wait()
    for copy in small_remotes:
        copy.wait_send()
    for index in range(4):
        in_remote(index).wait_send()

    @pl.when(core == 1)
    def _():
        for index in range(hidden_blocks + 1):
            out_remote(index).wait_send()

    @pl.when(stage > 0)
    def _():
        for chunk in range(chunks):
            up_remote(chunk).wait_send()


C_BLOCKS = 9
T_BLOCKS = 4
BLOCKS = C_BLOCKS + T_BLOCKS
PLACES = (8, 9, 0, 1, 2, 10, 3, 11, 4, 5, 6, 12, 7)
PAIRED = 8
LENT = 3


def lookup(index, table):
    value = jnp.int32(table[0])
    for at, entry in enumerate(table[1:], 1):
        value = jnp.where(index == at, entry, value)
    return value


def reduce_plan(line, half):
    pieces = (max(16, half // (2 * line)), max(16, half // line))
    sizes = (2 * line * pieces[0], line * pieces[1])
    counts = (-(-PAIRED * half // sizes[0]), -(-(BLOCKS - PAIRED) * half // sizes[1]))
    return pieces, sizes, counts


def lends(sections, line, half):
    return sections == 4 and line == 4 and reduce_plan(line, half)[1:] == ((half, half), (8, 5))


def ready_times(first, size, count, half):
    made = {place: time for time, place in enumerate(PLACES)}
    times = []
    for group in range(count):
        begin, end = first + group * size, first + (group + 1) * size
        times.append(
            max(made[place] for place in range(BLOCKS) if place * half < end and begin < (place + 1) * half)
        )
    return tuple(times)


COMPUTE = 2
ORDERS_OF_FOUR = (
    (
        2000, 1000, 2010, 1010, 2020, 1001, 2030, 2040, 20, 1011, 1002, 2050, 1020, 2060, 2070, 1003,
        21, 1012, 2080, 40, 1021, 2090, 1004, 2100, 22, 1013, 2110, 1022, 41, 10, 1005, 2120,
        1014, 23, 1023, 42, 1006, 11, 1040, 1015, 24, 1024, 43, 1007, 50, 1041, 0, 12,
        1016, 1025, 25, 51, 1042, 1, 1017, 52, 1026, 13, 26, 1043, 2, 53, 1027, 27,
        3, 60, 14, 1044, 4, 70, 1030, 15, 61, 1045, 5, 54, 1031, 16, 62, 1046,
        71, 6, 55, 1047, 1032, 72, 17, 56, 7, 63, 57, 73, 1033, 44, 64, 74,
        45, 65, 75, 46, 1034, 76, 66, 47, 1035, 77, 67, 1036, 1037,
    ),
    (
        2000, 1000, 2010, 1010, 2020, 1001, 2030, 2040, 20, 1011, 1002, 2050, 1020, 2060, 2070, 1003,
        21, 1012, 2080, 40, 1021, 2090, 2100, 1004, 22, 1013, 2110, 1022, 41, 10, 2120, 1005,
        1014, 23, 1023, 42, 1006, 11, 1040, 1015, 24, 1024, 43, 1007, 50, 1041, 0, 12,
        1016, 1025, 25, 1050, 51, 1042, 1, 30, 1017, 52, 1026, 1051, 13, 26, 1043, 2,
        53, 1027, 31, 1052, 27, 3, 60, 14, 32, 1044, 4, 1053, 1030, 15, 61, 33,
        70, 1045, 5, 1054, 54, 1031, 16, 62, 1046, 71, 6, 1055, 55, 1047, 1032, 72,
        17, 56, 63, 1056, 7, 57, 73, 1033, 34, 44, 64, 1057, 35, 74, 45, 65,
        75, 36, 46, 1034, 76, 66, 37, 47, 1035, 77, 67, 1036, 1037,
    ),
    (
        2000, 1000, 2010, 1010, 2020, 1001, 2030, 2040, 20, 1011, 1002, 2050, 1020, 2060, 2070, 1003,
        21, 1012, 2080, 40, 1021, 2090, 2100, 1004, 22, 1013, 2110, 1022, 41, 10, 2120, 1005,
        1014, 23, 1023, 42, 1006, 11, 1040, 1015, 24, 1024, 43, 1007, 50, 1041, 0, 12,
        1016, 1025, 25, 51, 1042, 1, 30, 1017, 52, 1026, 13, 26, 1043, 2, 53, 1027,
        31, 27, 3, 60, 14, 32, 1044, 4, 1030, 15, 61, 33, 70, 1045, 5, 54,
        1031, 16, 62, 1046, 71, 6, 55, 1047, 1032, 72, 17, 56, 63, 7, 57, 73,
        1033, 34, 44, 64, 35, 74, 45, 65, 75, 36, 46, 1034, 76, 66, 37, 47,
        1035, 77, 67, 1036, 1037,
    ),
)


def event_order(line, half):
    _, sizes, counts = reduce_plan(line, half)
    firsts = (0, counts[0] * sizes[0])
    steps = [(block, 0, (COMPUTE, block, 0)) for block in range(BLOCKS)]
    for kind in range(2):
        times = ready_times(firsts[kind], sizes[kind], counts[kind], half)
        for group, time in enumerate(times):
            steps += [(time + turn, 1 + kind, (kind, group, turn)) for turn in range(2 * line)]
    return [step for _, _, step in sorted(steps)]


def stage_orders(sections, line, half):
    if lends(sections, line, half):
        return [[(code // 1000, code // 10 % 100, code % 10) for code in order] for order in ORDERS_OF_FOUR]
    return [event_order(line, half)]


def reduce_phase(
    sections,
    count,
    channels,
    pool,
    early,
    kept,
    early_hbm,
    totals,
    mix_back,
    in_hbm,
    out_hbm,
    total_hbm,
    small,
    ready_sem,
    back_sem,
    pair_sem,
    pair_send,
    y_sem,
    y_send,
    sum_sem0,
    sum_send0,
    sum_sem1,
    sum_send1,
    spread_sem0,
    spread_send0,
    spread_sem1,
    spread_send1,
    lend_sem,
    lend_send,
    give_sem,
    give_send,
    give_recv,
    small_sem,
    small_send,
):
    section = lax.axis_index("section")
    dp_index = lax.axis_index("dp")
    core = section % 2
    line = count // 2
    z, y = dp_index // 2, dp_index % 2
    half = channels // 2
    pieces, sizes, counts = reduce_plan(line, half)
    firsts = (0, counts[0] * sizes[0])
    lent = lends(sections, line, half)
    lender, borrower = section == 1, section == sections - 1
    partner = {"section": section + 1 - 2 * core}
    across = {"dp": dp_index + 1 - 2 * y}

    def peer(offset):
        return {"dp": lax.rem(dp_index + offset, count)}

    length, chunks = kept.shape[1], early.shape[1] - 2
    starts, _ = pool_plan(sections, count, channels, length, 0)
    mine = pool.at[pl.ds(starts[0], starts[1] - starts[0])]
    theirs = Stack(pool, starts[1], half)
    pair_landing = Stack(pool, starts[2], sizes[0] // 2)
    cross_landing = Stack(pool, starts[3], pieces[1])
    passed = [Stack(pool, starts[4 + kind], (line + 1) * pieces[kind], pieces[kind]) for kind in range(2)]

    def landing(kind, direction, group, step):
        return passed[kind].at[group, step if direction == 0 else line - step]

    right_peer, left_peer = {"dp": dp_index + 2}, {"dp": dp_index - 2}

    def ready(device):
        pl.semaphore_signal(ready_sem, inc=1, device_id=device, device_id_type=MESH)

    ready(partner)
    ready(across)
    pl.when(z < line - 1)(lambda: ready(right_peer))
    pl.when(z > 0)(lambda: ready(left_peer))
    neighbours = 2 + jnp.where(z < line - 1, 1, 0) + jnp.where(z > 0, 1, 0)
    if lent:
        pl.when(borrower)(lambda: ready({"section": section - 2}))
        neighbours = neighbours + jnp.where(lender, 1, 0)

    small_pair = pltpu.make_async_remote_copy(
        src_ref=totals.at[1 - core],
        dst_ref=small.at[1],
        send_sem=small_send.at[0],
        recv_sem=small_sem.at[1],
        device_id=partner,
        device_id_type=MESH,
    )

    def small_copy(offset):
        return pltpu.make_async_remote_copy(
            src_ref=small.at[0],
            dst_ref=small.at[1 + offset],
            send_sem=small_send.at[offset],
            recv_sem=small_sem.at[1 + offset],
            device_id=peer(offset),
            device_id_type=MESH,
        )

    def small_start(offset, _):
        small_copy(offset).start()
        return 0

    def small_add(offset, total):
        small_copy(offset).wait()
        return total + small[1 + offset]

    def product(block, which, use):
        columns = pl.ds(pl.multiple_of(which * half, 128), half)
        turn = block - C_BLOCKS
        mixed = (block < 4) | (block == 8)

        @pl.when(mixed)
        def _():
            side = jnp.where(block == 8, 1, 0)
            left = early[side, pl.ds(0, chunks), :, columns].reshape(length, half)
            use(tn(left, kept[jnp.where(block == 8, C_DQ, C_DPRE + block)]))

        @pl.when(~mixed)
        def _():
            left = jnp.where(block < 8, C_HID + block - 4, C_DPRE + turn)
            use(tn(kept[left, :, columns], kept[jnp.where(block < 8, C_DKV, T_DK + turn)]))

    def time_mix_back(turn):
        return pltpu.make_async_copy(
            early_hbm.at[T_MIX0 + turn], kept.at[C_DPRE + turn], back_sem.at[turn]
        )

    def block_rows(block):
        return pl.ds(pl.multiple_of(lookup(block, PLACES) * half, half), half)

    def pair_copy(block):
        return pltpu.make_async_remote_copy(
            src_ref=theirs.at[block % 2],
            dst_ref=mine.at[block_rows(block)],
            send_sem=pair_send.at[block],
            recv_sem=pair_sem.at[block],
            device_id=partner,
            device_id_type=MESH,
        )

    def for_partner(block):
        for side, first in ((0, 0), (1, 8)):

            @pl.when(block == first)
            def _():
                for chunk in range(chunks):
                    mix_back(side, chunk).wait()

        pl.when(block >= C_BLOCKS)(lambda: time_mix_back(block - C_BLOCKS).wait())
        pl.when(block >= 2)(lambda: pair_copy(block - 2).wait_send())

        def store(gradient):
            theirs.at[block % 2][...] = gradient.astype(BF16)

        product(block, 1 - core, store)

        @pl.when(block == 0)
        def _():
            pl.semaphore_wait(ready_sem, neighbours)
            small_pair.start()

        pair_copy(block).start()

    def lend_copy():
        return pltpu.make_async_remote_copy(
            src_ref=mine.at[pl.ds(LENT * half, half)],
            dst_ref=mine.at[pl.ds(BLOCKS * half, half)],
            send_sem=lend_send.at[0],
            recv_sem=lend_sem.at[0],
            device_id={"section": section + 2},
            device_id_type=MESH,
        )

    def for_me(block):
        rows = block_rows(block)

        def add(gradient):
            pair_copy(block).wait_recv()
            mine[rows, :] = (gradient + mine[rows, :].astype(F32)).astype(BF16)

        product(block, core, add)
        if lent:
            pl.when(lender & (block == PLACES.index(LENT)))(lambda: lend_copy().start())
        pl.when(block < 4)(lambda: time_mix_back(block).start())

    blocks_at = tuple(PLACES.index(place) for place in (*range(BLOCKS), LENT))

    def give(kind, group, start):
        size = pieces[kind]
        rows = pl.ds(pl.multiple_of(start, size), size)
        place = start // half if half % sizes[kind] else firsts[kind] // half + group * sizes[kind] // half
        block = lookup(place, blocks_at)
        row = core * half + start - place * half

        def copies(owner, target):
            foreign = kind == 1 and lent and group == counts[1]

            @pl.when((owner == core) & ~jnp.bool_(foreign))
            def _():
                pltpu.make_async_copy(mine.at[rows], target, give_sem.at[0]).start()

            def remote(device):
                return pltpu.make_async_remote_copy(
                    src_ref=mine.at[rows],
                    dst_ref=target,
                    send_sem=give_send.at[0],
                    recv_sem=give_recv.at[0],
                    device_id=device,
                    device_id_type=MESH,
                )

            @pl.when((owner != core) & ~jnp.bool_(foreign))
            def _():
                remote(partner).start()

            if kind == 1 and lent:
                pl.when(foreign)(lambda: remote({"section": section - core + owner - 2}).start())

            if kind == 0:
                remote({"section": section - core + owner, "dp": dp_index + 1 - 2 * y}).start()

        def to_in(owner, column):
            columns = pl.ds(pl.multiple_of(column * channels, channels), channels)
            copies(owner, in_hbm.at[pl.ds(pl.multiple_of(row, size), size), columns])

        def to_out():
            within = (block - 4) * channels + row
            copies(1, out_hbm.at[pl.ds(pl.multiple_of(within, size), size)])

        of_time = block >= C_BLOCKS
        pl.when((block < 4) | (of_time & (place < BLOCKS)))(
            lambda: to_in(jnp.where(of_time, 0, 1), jnp.where(of_time, block - C_BLOCKS, block))
        )
        pl.when((block >= 4) & ~of_time)(to_out)

    sum_sems = ((sum_sem0, sum_send0), (sum_sem1, sum_send1))
    spread_sems = ((spread_sem0, spread_send0), (spread_sem1, spread_send1))

    def piece_rows(kind, group, index):
        start = firsts[kind] + group * sizes[kind] + index * pieces[kind]
        if kind == 0:
            start = start + y * (sizes[0] // 2)
        return start, pl.ds(pl.multiple_of(start, pieces[kind]), pieces[kind])

    def sum_copy(kind, group, direction, step):
        place = landing(kind, direction, group, step)
        receive, send = sum_sems[kind]
        return pltpu.make_async_remote_copy(
            src_ref=place,
            dst_ref=place,
            send_sem=send.at[group, direction, step],
            recv_sem=receive.at[group, direction, step],
            device_id=(right_peer, left_peer)[direction],
            device_id_type=MESH,
        )

    def spread_copy(kind, group, direction, step, index):
        _, rows = piece_rows(kind, group, index)
        receive, send = spread_sems[kind]
        return pltpu.make_async_remote_copy(
            src_ref=mine.at[rows],
            dst_ref=mine.at[rows],
            send_sem=send.at[group, direction, step],
            recv_sem=receive.at[group, direction, step],
            device_id=(right_peer, left_peer)[direction],
            device_id_type=MESH,
        )

    def passing(kind, group, turn):
        for direction in range(2):
            behind = z if direction == 0 else line - 1 - z
            step = turn - behind
            index = line - 1 - step if direction == 0 else step
            place = landing(kind, direction, group, step)
            _, rows = piece_rows(kind, group, index)

            @pl.when((step >= 0) & (behind == 0) & (step < line - 1))
            def _():
                place[...] = mine[rows, :]
                sum_copy(kind, group, direction, step).start()

            @pl.when((step >= 0) & (behind > 0))
            def _():
                sum_copy(kind, group, direction, step).wait_recv()

                @pl.when(turn < line - 1)
                def _():
                    place[...] = (place[...].astype(F32) + mine[rows, :].astype(F32)).astype(BF16)
                    sum_copy(kind, group, direction, step).start()

    def arrived(kind, group):
        _, rows = piece_rows(kind, group, z)
        total = mine[rows, :].astype(F32)
        from_left = landing(kind, 0, group, jnp.minimum(line - 1 - z, line - 2))
        from_right = landing(kind, 1, group, jnp.minimum(z, line - 2))
        mine[rows, :] = total.astype(BF16)

        @pl.when(z == 0)
        def _():
            mine[rows, :] = (total + from_right[...].astype(F32)).astype(BF16)

        @pl.when(z == line - 1)
        def _():
            mine[rows, :] = (total + from_left[...].astype(F32)).astype(BF16)

        @pl.when((z > 0) & (z < line - 1))
        def _():
            mine[rows, :] = (
                total + from_left[...].astype(F32) + from_right[...].astype(F32)
            ).astype(BF16)

    def finished(kind, group, index):
        start, _ = piece_rows(kind, group, index)
        give(kind, group, start)

    def spread_own(kind, group):
        @pl.when(z < line - 1)
        def _():
            spread_copy(kind, group, 0, 0, z).start()

        @pl.when(z > 0)
        def _():
            spread_copy(kind, group, 1, 0, z).start()

        finished(kind, group, z)

    def spreading(kind, group, hop):
        for direction in range(2):
            index = z - hop if direction == 0 else z + hop
            onward = z < line - 1 if direction == 0 else z > 0
            exists = index >= 0 if direction == 0 else index < line

            @pl.when(exists)
            def _():
                spread_copy(kind, group, direction, hop - 1, index).wait_recv()

                @pl.when(onward)
                def _():
                    spread_copy(kind, group, direction, hop, index).start()

                finished(kind, group, index)

    def over(group):
        start = group * sizes[0] + (1 - y) * (sizes[0] // 2)
        return pltpu.make_async_remote_copy(
            src_ref=mine.at[pl.ds(pl.multiple_of(start, pieces[0]), sizes[0] // 2)],
            dst_ref=pair_landing.at[group],
            send_sem=y_send.at[group],
            recv_sem=y_sem.at[group],
            device_id=across,
            device_id_type=MESH,
        )

    def swap(group):
        _, rows = piece_rows(1, group, z)
        return pltpu.make_async_remote_copy(
            src_ref=mine.at[rows],
            dst_ref=cross_landing.at[group],
            send_sem=y_send.at[counts[0] + group],
            recv_sem=y_sem.at[counts[0] + group],
            device_id=across,
            device_id_type=MESH,
        )

    def event0(group, turn):
        @pl.when(turn == 0)
        def _():
            over(group).start()

        @pl.when(turn == 1)
        def _():
            over(group).wait_recv()

            def add(index, _):
                _, rows = piece_rows(0, group, index)
                local = pl.ds(pl.multiple_of(index * pieces[0], pieces[0]), pieces[0])
                arrived_rows = pair_landing.at[group][local, :]
                mine[rows, :] = (mine[rows, :].astype(F32) + arrived_rows.astype(F32)).astype(BF16)
                return 0

            lax.fori_loop(0, line, add, 0)

        @pl.when((turn >= 1) & (turn <= line))
        def _():
            passing(0, group, turn - 1)

        @pl.when(turn == line)
        def _():
            arrived(0, group)
            spread_own(0, group)

        @pl.when(turn > line)
        def _():
            spreading(0, group, turn - line)

    def event1(group, turn):
        if lent:
            pl.when((turn == 0) & (group == counts[1]))(lambda: lend_copy().wait_recv())

        @pl.when(turn < line)
        def _():
            passing(1, group, turn)

        @pl.when(turn == line - 1)
        def _():
            arrived(1, group)
            swap(group).start()

        @pl.when(turn == line)
        def _():
            swap(group).wait()
            _, rows = piece_rows(1, group, z)
            mine[rows, :] = (
                mine[rows, :].astype(F32) + cross_landing[group].astype(F32)
            ).astype(BF16)
            spread_own(1, group)

        @pl.when(turn > line)
        def _():
            spreading(1, group, turn - line)

    spare = firsts[1] + counts[1] * sizes[1] - BLOCKS * half
    if spare:
        mine[pl.ds(BLOCKS * half, spare), :] = jnp.zeros((spare, channels), BF16)
    tables = []
    for events in stage_orders(sections, line, half):
        order = [(COMPUTE, 0, 0)]
        for kind, group, turn in events:
            if kind == COMPUTE:
                order += [(COMPUTE, group + 1, 0)] * (group + 1 < BLOCKS) + [(COMPUTE, group, 1)]
            else:
                order.append((kind, group, turn))
        tables.append([kind * 1024 + group * 64 + turn for kind, group, turn in order])
    most = max(len(table) for table in tables)
    packed = []
    for table in tables:
        filled = table + [0] * (most + most % 2 - len(table))
        packed.append(tuple(a + 4096 * b for a, b in zip(filled[::2], filled[1::2], strict=True)))

    def mine_of(values):
        if len(values) == 1:
            return values[0]
        if len(set(values)) == 1:
            return jnp.int32(values[0])
        return jnp.where(lender, values[0], jnp.where(borrower, values[1], values[2]))

    steps = mine_of([len(table) for table in tables])

    def take(index, _):
        word = jnp.int32(0)
        for at, values in enumerate(zip(*packed, strict=True)):
            word = jnp.where(index // 2 == at, mine_of(values), word)
        code = jnp.where(index % 2 == 0, word % 4096, word // 4096)
        kind, group, turn = code // 1024, code // 64 % 16, code % 64

        @pl.when(kind == COMPUTE)
        def _():
            pl.when(turn == 0)(lambda: for_partner(group))
            pl.when(turn == 1)(lambda: for_me(group))

            @pl.when((turn == 1) & (group == BLOCKS // 2))
            def _():
                small_pair.wait()
                small[0] = totals[core] + small[1]
                lax.fori_loop(1, count, small_start, 0)

        pl.when(kind == 0)(lambda: event0(group, turn))
        pl.when(kind == 1)(lambda: event1(group, turn))
        return 0

    lax.fori_loop(0, steps, take, 0)
    small[0] = lax.fori_loop(1, count, small_add, small[0])
    total_copy = pltpu.make_async_copy(small.at[0], total_hbm, small_sem.at[0])
    total_copy.start()

    def summed_here(kind, group):
        if not lent:
            return group >= 0
        return (borrower | (group != counts[1])) if kind else (~lender | (group != LENT))

    def over_done(group, _):
        pl.when(summed_here(0, group))(lambda: over(group).wait_send())
        return 0

    for block in range(BLOCKS - 2, BLOCKS):
        pair_copy(jnp.int32(block)).wait_send()
    lax.fori_loop(0, counts[0], over_done, 0)
    for kind in range(2):

        def group_done(group, _):
            def step_done(step, _):
                for direction in range(2):
                    behind = z if direction == 0 else line - 1 - z

                    @pl.when((step < line - 1 - behind) & summed_here(kind, group))
                    def _():
                        sum_copy(kind, group, direction, step).wait_send()

                    @pl.when((step <= behind) & (behind < line - 1) & summed_here(kind, group))
                    def _():
                        spread_copy(kind, group, direction, step, 0).wait_send()

                return 0

            return lax.fori_loop(0, line - 1, step_done, 0)

        lax.fori_loop(0, counts[kind] + kind * lent, group_done, 0)

    if lent:
        pl.when(lender)(lambda: lend_copy().wait_send())

    def taken(rows, sem):
        if rows:
            ref = mine.at[pl.ds(0, rows)]
            pltpu.make_async_copy(ref, ref, sem.at[0]).wait()

    paired = [PLACES[block] < PAIRED for block in range(BLOCKS)]
    whole = [half // 2 if pair else half for pair in paired]
    by_kind = (range(C_BLOCKS, BLOCKS), range(C_BLOCKS))
    for own in range(2):
        for last in range(2):
            local = sum(whole[block] for block in by_kind[own])
            crossed = sum(half // 2 for block in range(BLOCKS) if paired[block])
            other = sum(whole[block] for block in by_kind[1 - own])
            if lent and own and last:
                other += half
            elif lent and own:
                crossed -= half // 2
                local -= whole[PLACES.index(LENT)]
            received = len(by_kind[own]) * channels - local

            @pl.when((core == own) & ((section >= 2) == bool(last)))
            def _(local=local, sent=other + crossed, received=received):
                taken(local, give_sem)
                taken(sent, give_send)
                taken(received, give_recv)

    total_copy.wait()


def pool_plan(sections, count, channels, length, slots):
    half, line = channels // 2, count // 2
    pieces, sizes, counts = reduce_plan(line, half)
    counts = (counts[0], counts[1] + lends(sections, line, half))
    heights = (
        counts[0] * sizes[0] + counts[1] * sizes[1],
        2 * half,
        counts[0] * sizes[0] // 2,
        counts[1] * pieces[1],
        *[counts[kind] * (line + 1) * pieces[kind] for kind in range(2)],
    )
    starts = [sum(heights[:at]) for at in range(len(heights))]
    return starts, max(sum(heights), slots * channels + 3 * length)


def chain(sections, count, x, cotangent, w_in, w_out, gain, bias, rates, wkv, state):
    length, channels = x.shape[2:]
    hidden_blocks = w_in.shape[2] // channels
    chunks = length // CHUNK
    anywhere = pl.BlockSpec(memory_space=pl.ANY)
    dma = pltpu.SemaphoreType.DMA
    slots = 9 + hidden_blocks
    line = count // 2
    _, _, counts = reduce_plan(line, channels // 2)
    counts = (counts[0], counts[1] + lends(sections, line, channels // 2))
    hops = [dma((counts[kind], 2, line - 1)) for kind in range(2)]
    _, pool_rows = pool_plan(sections, count, channels, length, slots)
    return pl.pallas_call(
        functools.partial(chain_kernel, sections, length, channels, hidden_blocks, count),
        out_shape=(
            jax.ShapeDtypeStruct((2, length, channels), BF16),
            jax.ShapeDtypeStruct((2, length, channels), BF16),
            jax.ShapeDtypeStruct((2, 8, channels), F32),
            jax.ShapeDtypeStruct((EARLY, length, channels), BF16),
            jax.ShapeDtypeStruct((channels, 4 * channels), BF16),
            jax.ShapeDtypeStruct(((C_BLOCKS - 4) * channels, channels), BF16),
            jax.ShapeDtypeStruct((8, channels), F32),
        ),
        in_specs=[anywhere] * 9,
        out_specs=(anywhere,) * 7,
        scratch_shapes=[
            pltpu.VMEM((pool_rows, channels), BF16),
            pltpu.VMEM((2, EARLY, CHUNK, channels), BF16),
            pltpu.VMEM((LATE, length, channels), BF16),
            pltpu.VMEM((2, length, channels), F32),
            pltpu.VMEM((length, channels), BF16),
            pltpu.VMEM((5, CHUNK, channels), F32),
            pltpu.VMEM((2 * CHUNK, 2 * channels), BF16),
            pltpu.VMEM((2, CHUNK, channels), F32),
            pltpu.VMEM((2, CHUNK, 2 * CHUNK), BF16),
            pltpu.VMEM((2, 1, channels), F32),
            pltpu.VMEM((2, 1, channels), F32),
            pltpu.VMEM((2, 3, 1, channels), F32),
            pltpu.VMEM((2, 2, channels), F32),
            pltpu.VMEM((2, 3, 2, 1, channels), F32),
            pltpu.VMEM((2, length // ROWS, channels), F32),
            pltpu.VMEM((8, channels), F32),
            pltpu.VMEM((8, channels), F32),
            pltpu.VMEM((2, 8, channels), F32),
            pltpu.VMEM((2, 8, 8, channels), F32),
            pltpu.VMEM((2, 8, channels), F32),
            dma((slots,)),
            dma((slots,)),
            dma((2, 5)),
            dma((5,)),
            dma((chunks,)),
            dma((chunks,)),
            dma((chunks,)),
            dma((chunks,)),
            dma((2 + chunks,)),
            dma((2 + chunks,)),
            dma((2 + chunks,)),
            dma((2,)),
            dma((2, chunks)),
            pltpu.VMEM((count + 1, 8, channels), F32),
            pltpu.SemaphoreType.REGULAR,
            dma((4,)),
            dma((BLOCKS,)),
            dma((BLOCKS,)),
            dma((sum(counts),)),
            dma((sum(counts),)),
            hops[0],
            hops[0],
            hops[1],
            hops[1],
            hops[0],
            hops[0],
            hops[1],
            hops[1],
            dma((1,)),
            dma((1,)),
            dma((1,)),
            dma((1,)),
            dma((1,)),
            dma((count + 1,)),
            dma((count + 1,)),
        ],
        compiler_params=pltpu.CompilerParams(
            collective_id=0, has_side_effects=True, vmem_limit_bytes=VMEM_BYTES
        ),
    )(x, cotangent, w_in, w_out, gain, bias, rates, wkv, state)


def finish_kernel(
    in_short,
    out_short,
    outs_in,
    grads_in,
    fin,
    total,
    in_wide,
    out_wide,
    outs,
    grads,
    states,
    normed,
    gain,
    bias,
    rates,
    wkv,
    in_held,
    out_held,
    in_made,
    out_made,
    tokens_held,
    load_sem,
    store_sem,
):
    holds_channel_mix = lax.axis_index("section") % 2 == 1
    sources, targets = (in_short, out_short), (in_wide, out_wide)
    held, made = (in_held, out_held), (in_made, out_made)
    parts = 8
    jobs = [(which, part) for part in range(parts) for which in range(2)]

    def rows_of(which, part):
        tall = sources[which].shape[0] // parts
        return pl.ds(part * tall, tall)

    def load(which, part):
        rows = rows_of(which, part)
        return pltpu.make_async_copy(
            sources[which].at[rows], held[which].at[rows], load_sem.at[which, part]
        )

    def store(which, part):
        rows = rows_of(which, part)
        return pltpu.make_async_copy(
            made[which].at[rows], targets[which].at[rows], store_sem.at[which, part]
        )

    def start(which, part):
        if which:
            pl.when(holds_channel_mix)(lambda: load(which, part).start())
        else:
            load(which, part).start()

    token_loads = [
        pltpu.make_async_copy(source, tokens_held.at[at], load_sem.at[2, at])
        for at, source in enumerate((outs_in, grads_in))
    ]
    token_stores = [
        pltpu.make_async_copy(tokens_held.at[at], target.at[0, :, 0], store_sem.at[2, at])
        for at, target in enumerate((outs, grads))
    ]
    ahead = 6
    for job in jobs[:2]:
        start(*job)
    for copy in token_loads:
        copy.start()
    for job in jobs[2:ahead]:
        start(*job)
    for micro in range(2):
        normed[0, micro] = fin[micro, 0:1]
        for row in range(2):
            states[0, row, micro] = fin[micro, 1 + row : 2 + row]
    gain[...] = total[GAIN : GAIN + 1]
    bias[...] = total[BIAS : BIAS + 1]
    for row in range(3):
        rates[row] = total[RATES + row : RATES + row + 1]
    wkv[0] = total[DECAY : DECAY + 2]
    for at, (which, part) in enumerate(jobs):
        tall = sources[which].shape[0] // parts
        step = 32 if which == 0 else 96

        def widen(index, _):
            rows = pl.ds(pl.multiple_of(part * tall + index * step, step), step)
            made[which][rows, :] = held[which][rows, :].astype(F32)
            return 0

        def clear(index, _):
            rows = pl.ds(pl.multiple_of(part * tall + index * step, step), step)
            made[which][rows, :] = jnp.zeros((step, made[which].shape[1]), F32)
            return 0

        def widened():
            load(which, part).wait()
            lax.fori_loop(0, tall // step, widen, 0)

        if which:
            pl.when(holds_channel_mix)(widened)

            @pl.when(~holds_channel_mix)
            def _():
                lax.fori_loop(0, tall // step, clear, 0)

        else:
            widened()
        if at + ahead < len(jobs):
            start(*jobs[at + ahead])
        store(which, part).start()
        if at < 2:
            token_loads[at].wait()
            token_stores[at].start()
    for job in jobs:
        store(*job).wait()
    for copy in token_stores:
        copy.wait()


def finished_outputs(in_short, out_short, outs, grads, fin, total):
    length, channels = outs.shape[1:]
    whole = pl.BlockSpec(memory_space=pltpu.VMEM)
    anywhere = pl.BlockSpec(memory_space=pl.ANY)

    def shape(*sizes, dtype=F32):
        return jax.ShapeDtypeStruct(sizes, dtype)

    in_wide, out_wide, *rest = pl.pallas_call(
        finish_kernel,
        out_shape=(
            shape(*in_short.shape),
            shape(*out_short.shape),
            shape(1, 2, 1, length, channels, dtype=BF16),
            shape(1, 2, 1, length, channels, dtype=BF16),
            shape(1, 2, 2, 1, channels),
            shape(1, 2, 1, channels),
            shape(1, channels),
            shape(1, channels),
            shape(3, 1, channels),
            shape(1, 2, channels),
        ),
        in_specs=[anywhere] * 4 + [whole] * 2,
        out_specs=(anywhere,) * 4 + (whole,) * 6,
        scratch_shapes=[
            pltpu.VMEM(in_short.shape, BF16),
            pltpu.VMEM(out_short.shape, BF16),
            pltpu.VMEM(in_short.shape, F32),
            pltpu.VMEM(out_short.shape, F32),
            pltpu.VMEM((2, 2, length, channels), BF16),
            pltpu.SemaphoreType.DMA((3, 8)),
            pltpu.SemaphoreType.DMA((3, 8)),
        ],
        compiler_params=pltpu.CompilerParams(vmem_limit_bytes=VMEM_BYTES),
    )(in_short, out_short, outs, grads, fin, total)
    *rest, rates, wkv = rest
    return in_wide, out_wide, *rest, jnp.swapaxes(rates, 0, 1), wkv


def shards(
    block_input,
    carried_state,
    output_cotangent,
    in_weight,
    out_weight,
    norm_gain,
    norm_bias,
    mix_rates,
    wkv_params,
):
    sections = lax.axis_size("section")
    outs, grads, fin, _, in_short, out_short, total = chain(
        sections,
        lax.axis_size("dp"),
        block_input,
        output_cotangent,
        in_weight,
        out_weight,
        norm_gain,
        norm_bias,
        jnp.swapaxes(mix_rates, 0, 1),
        wkv_params,
        carried_state,
    )
    in_grad, out_grad, outs, grads, states, normed, gain, bias, rates, wkv = finished_outputs(
        in_short, out_short, outs, grads, fin, total
    )
    return outs, states, normed, grads, in_grad[None], out_grad[None], gain, bias, rates, wkv


def solution(mesh):
    return jax.shard_map(
        shards,
        mesh=mesh,
        in_specs=(
            P(None, "dp", None, None),
            P("section", None, None, "dp", None),
            P(None, "dp", None, None),
            P("section", None, None),
            P("section", None, None),
            P("section", None),
            P("section", None),
            P("section", None, None),
            P("section", None, None),
        ),
        out_specs=(
            P("section", None, "dp", None, None),
            P("section", None, None, "dp", None),
            P("section", None, "dp", None),
            P("section", None, "dp", None, None),
            P("section", None, None),
            P("section", None, None),
            P("section", None),
            P("section", None),
            P("section", None, None),
            P("section", None, None),
        ),
        check_vma=False,
    )
```
